32 devices in a mesh: gx: 8 (over z, y), gy: 4 (over x, core).
Axes of the slice: x: 2, y: 2, z: 4, core: 2. Of those that a mesh axis runs over, the one named last changes fastest.
Arguments:
- populations: float32 [27, 32, 64, 256], P(None, 'gx', 'gy'), may hold values from 0.4 to 1.6
- omega: float32 [32, 64, 256], P('gx', 'gy'), may hold values from 1.2 to 1.9
- walls: int32 [32, 64, 256], P('gx', 'gy'), may hold values 0 or 1
- radiation: bfloat16 [4096, 512], replicated, may hold values from -0.25 to 0.25
- bins: int32 [128, 32], replicated, may hold values from 0 to 126
- counts: int32 [8, 4], P('gx', 'gy'), may hold values from 1 to 16, as said below
- sample_site: int32 [8, 4, 16], P('gx', 'gy'), may hold values from 0 to 127, as said below
- sample_patch: int32 [8, 4, 16], P('gx', 'gy'), may hold values from 0 to 127, as said below
Outputs:
- advanced: float32 [27, 32, 64, 256], P(None, 'gx', 'gy')
- signal: float32 [4096, 128], P(('gx', 'gy'))
The draws below stay inside these ranges and needn't reach their ends.
Inputs may be any that keep to these rules, and one draw needn't show every extreme that they name: `counts`: live samples fill a device's first slots; some device has all 16. `sample_site`: site numbers of one device are distinct. `sample_patch`: a device with gy index j names only patches j * 32 to (j + 1) * 32 - 1.
All inputs are finite; a program needn't handle non-finite values. No bound on the sum of `walls` on one device may be relied on, other than what follows from the above.
Results may differ from the reference program's by a relative error of at most 0.0037.
Values may be sent and summed in bfloat16 or wider, within the bound.
No kernel may reach another device: no remote copies, remote signals or barrier semaphores. Data moves between devices by JAX's collectives and lax.ppermute only.
A program may use at most 64 MiB of HBM per device.

```python
import jax
import jax.numpy as jnp
from jax import lax

CX = 4
CY = 16
NZ = 256
ZS = 128
SAMP = 16
OBS = 4096
OBS_BLK = 128
LEVELS = 128
STEPS = 2
NX = 32
NY = 64
SITES = 128
PCOL = 32
PATCHES = 128
OBLK = 32
N_GX = 8
N_GY = 4


def draw_counts(key, part):
    drawn = jax.random.randint(key, (N_GX * N_GY,), 1, SAMP + 1)
    chosen_device = jax.random.randint(jax.random.fold_in(key, 7), (), 0, N_GX * N_GY)
    filled = jnp.where(jnp.arange(N_GX * N_GY) == chosen_device, SAMP, drawn)
    return filled.reshape(N_GX, N_GY).astype(jnp.int32)


def draw_sample_site(key, part):
    device_keys = jax.random.split(key, N_GX * N_GY)
    picked = jax.vmap(lambda device_key: jax.random.permutation(device_key, SITES)[:SAMP])(device_keys)
    return picked.reshape(N_GX, N_GY, SAMP).astype(jnp.int32)


def draw_sample_patch(key, part):
    drawn = jax.random.randint(key, (N_GX, N_GY, SAMP), 0, PCOL)
    offset = jnp.arange(N_GY)[None, :, None] * PCOL
    patches = (drawn + offset).astype(jnp.int32)
    patches = patches.at[0, 0, 0].set(0)
    patches = patches.at[0, N_GY - 1, 0].set(PATCHES - 1)
    return patches.astype(jnp.int32)


def place_ends(values, stream_key, smallest, largest):
    shape = values.shape
    index_at = [jax.random.randint(jax.random.fold_in(stream_key, axis), (), 0, shape[axis]) for axis in range(len(shape))]
    values = values.at[tuple(index_at)].set(smallest)
    longest = shape.index(max(shape))
    index_at[longest] = (index_at[longest] + 1) % shape[longest]
    return values.at[tuple(index_at)].set(largest)


def block_levels(stream_key, dims, shards, least, largest):
    gain = 1.0
    for dim, parts in shards:
        steps = jax.random.uniform(jax.random.fold_in(jax.random.fold_in(stream_key, 6), dim), (parts,), jnp.float32, least / len(shards), largest / len(shards))
        gain = gain * jnp.repeat(jnp.exp(steps), dims[dim] // parts).reshape((-1,) + (1,) * (len(dims) - 1 - dim))
    return gain


def gaussian(stream_key, shape, spread, most, kind=jnp.bfloat16):
    values = jax.random.normal(stream_key, shape, jnp.float32) * spread
    return jnp.minimum(jnp.maximum(values, -most), most).astype(kind)


def setup_inputs(seed: int = 0) -> dict:
    arg_keys = jax.random.split(jax.random.key(seed), 9)
    return {
        "populations": jnp.clip(0.4 + 1.2 * jax.random.uniform(arg_keys[0], (27, NX, NY, NZ), jnp.float32) ** block_levels(arg_keys[0], (27, NX, NY, NZ), ((1, 8), (2, 4)), -0.2, 0.2), 0.4, 1.6),
        "omega": jnp.clip(1.2 + 0.6999999 * jax.random.uniform(arg_keys[1], (NX, NY, NZ), jnp.float32) ** block_levels(arg_keys[1], (NX, NY, NZ), ((0, 8), (1, 4)), -0.2, 0.2), 1.2, 1.9),
        "walls": place_ends((jax.random.randint(arg_keys[2], (NX, NY, NZ), 0, 8) < 1).astype(jnp.int32), jax.random.fold_in(arg_keys[2], 1), 0, 1),
        "radiation": gaussian(arg_keys[3], (OBS, 4 * ZS), (4 * ZS) ** -0.5, 0.25),
        "bins": place_ends(jax.random.randint(arg_keys[4], (PATCHES, OBLK), 0, LEVELS - STEPS + 1), jax.random.fold_in(arg_keys[4], 1), 0, LEVELS - STEPS).astype(jnp.int32),
        "counts": draw_counts(jax.random.fold_in(arg_keys[8], 71), 0),
        "sample_site": draw_sample_site(jax.random.fold_in(arg_keys[8], 71), 0),
        "sample_patch": draw_sample_patch(jax.random.fold_in(arg_keys[8], 71), 0),
    }


def lattice_weight():
    values = []
    for direction in range(27):
        moving = int(direction // 9 != 1) + int((direction // 3) % 3 != 1) + int(direction % 3 != 1)
        values.append([8.0 / 27.0, 2.0 / 27.0, 1.0 / 54.0, 1.0 / 216.0][moving])
    return jnp.array(values, dtype=jnp.float32)


def forward(lattice, axis_index, velocity):
    rotated = jnp.moveaxis(lattice, axis_index, 0)
    minus_side, centre, plus_side = rotated[0], rotated[1], rotated[2]
    summed = minus_side + centre + plus_side
    difference = plus_side - minus_side
    first_order = difference - velocity * summed
    second_order = plus_side + minus_side - 2.0 * velocity * difference + velocity * velocity * summed
    return jnp.moveaxis(jnp.stack([summed, first_order, second_order]), 0, axis_index)


def backward(lattice, axis_index, velocity):
    rotated = jnp.moveaxis(lattice, axis_index, 0)
    order_zero, order_one, order_two = rotated[0], rotated[1], rotated[2]
    difference = order_one + velocity * order_zero
    summed_ends = order_two + 2.0 * velocity * order_one + velocity * velocity * order_zero
    minus_side = 0.5 * (summed_ends - difference)
    plus_side = 0.5 * (summed_ends + difference)
    centre = order_zero - summed_ends
    return jnp.moveaxis(jnp.stack([minus_side, centre, plus_side]), 0, axis_index)


def collide(distribution, omega):
    trailing = distribution.shape[1:]
    lattice = distribution.reshape((3, 3, 3) + trailing)
    density = jnp.sum(lattice, axis=(0, 1, 2))
    vel_x = jnp.sum(lattice[2] - lattice[0], axis=(0, 1)) / density
    vel_y = jnp.sum(lattice[:, 2] - lattice[:, 0], axis=(0, 1)) / density
    vel_z = jnp.sum(lattice[:, :, 2] - lattice[:, :, 0], axis=(0, 1)) / density
    moments = forward(lattice, 2, vel_z)
    moments = forward(moments, 1, vel_y)
    moments = forward(moments, 0, vel_x)
    retain = 1.0 - omega
    normal_xy = retain * (moments[2, 0, 0] - moments[0, 2, 0])
    normal_xz = retain * (moments[2, 0, 0] - moments[0, 0, 2])
    post_xx = (density + normal_xy + normal_xz) / 3.0
    post_yy = (density - 2.0 * normal_xy + normal_xz) / 3.0
    post_zz = (density + normal_xy - 2.0 * normal_xz) / 3.0
    post_xy = retain * moments[1, 1, 0]
    post_xz = retain * moments[1, 0, 1]
    post_yz = retain * moments[0, 1, 1]
    inverse = 1.0 / density
    entries = {
        (0, 0, 0): density,
        (2, 0, 0): post_xx,
        (0, 2, 0): post_yy,
        (0, 0, 2): post_zz,
        (1, 1, 0): post_xy,
        (1, 0, 1): post_xz,
        (0, 1, 1): post_yz,
        (2, 2, 0): (post_xx * post_yy + 2.0 * post_xy * post_xy) * inverse,
        (2, 0, 2): (post_xx * post_zz + 2.0 * post_xz * post_xz) * inverse,
        (0, 2, 2): (post_yy * post_zz + 2.0 * post_yz * post_yz) * inverse,
        (2, 1, 1): (post_xx * post_yz + 2.0 * post_xy * post_xz) * inverse,
        (1, 2, 1): (post_yy * post_xz + 2.0 * post_xy * post_yz) * inverse,
        (1, 1, 2): (post_zz * post_xy + 2.0 * post_xz * post_yz) * inverse,
        (2, 2, 2): (post_xx * post_yy * post_zz + 2.0 * post_xx * post_yz * post_yz
                    + 2.0 * post_yy * post_xz * post_xz + 2.0 * post_zz * post_xy * post_xy
                    + 8.0 * post_xy * post_xz * post_yz) * inverse * inverse,
    }
    nothing = jnp.zeros_like(density)
    listed = [entries.get((order_x, order_y, order_z), nothing)
              for order_x in range(3) for order_y in range(3) for order_z in range(3)]
    relaxed = jnp.stack(listed).reshape((3, 3, 3) + trailing)
    relaxed = backward(relaxed, 0, vel_x)
    relaxed = backward(relaxed, 1, vel_y)
    relaxed = backward(relaxed, 2, vel_z)
    return relaxed.reshape((27,) + trailing)


def macro_rows(read):
    lattice = read.reshape((3, 3, 3) + read.shape[1:])
    density = jnp.sum(lattice, axis=(0, 1, 2))
    mom_x = jnp.sum(lattice[2] - lattice[0], axis=(0, 1))
    mom_y = jnp.sum(lattice[:, 2] - lattice[:, 0], axis=(0, 1))
    mom_z = jnp.sum(lattice[:, :, 2] - lattice[:, :, 0], axis=(0, 1))
    return jnp.stack([density - 1.0, mom_x, mom_y, mom_z])


def radiate(read, radiation, bins, counts, sample_site, sample_patch, step_index):
    fields = macro_rows(read).reshape(4, NX, NY, NZ // ZS, ZS)
    local_x = sample_site // (CY * (NZ // ZS))
    local_y = (sample_site // (NZ // ZS)) % CY
    segment = sample_site % (NZ // ZS)
    global_x = jnp.arange(N_GX, dtype=jnp.int32)[:, None, None] * CX + local_x
    global_y = jnp.arange(N_GY, dtype=jnp.int32)[None, :, None] * CY + local_y
    picked = fields[:, global_x, global_y, segment, :]
    picked = jnp.moveaxis(picked, 0, 3).reshape(N_GX * N_GY * SAMP, 4 * ZS)
    live_slot = (jnp.arange(SAMP, dtype=jnp.int32)[None, None, :] < counts[:, :, None]).reshape(-1)
    surface = jnp.where(live_slot[:, None], picked, 0.0).astype(jnp.bfloat16)
    patch_sum = jax.ops.segment_sum(surface.astype(jnp.float32), sample_patch.reshape(-1), num_segments=PATCHES)
    response = lax.dot_general(radiation, patch_sum.astype(jnp.bfloat16), (((1,), (1,)), ((), ())),
                               preferred_element_type=jnp.float32)
    levels_hit = bins + step_index
    one_hot = (levels_hit[:, :, None] == jnp.arange(LEVELS, dtype=jnp.int32)).astype(jnp.float32)
    binned = jnp.einsum("bop,pbl->bol", response.reshape(OBS // OBS_BLK, OBS_BLK, PATCHES), one_hot,
                        precision=lax.Precision.HIGHEST)
    return binned.reshape(OBS, LEVELS)


def reference(populations, omega, walls, radiation, bins, counts, sample_site, sample_patch):
    weight = lattice_weight()[:, None, None, None]
    solid_cell = walls == 1
    current = populations
    signal = jnp.zeros((OBS, LEVELS), jnp.float32)
    for step_index in range(STEPS):
        before = current * weight
        planes = lax.map(lambda plane_pair: collide(plane_pair[0], plane_pair[1]),
                         (jnp.moveaxis(before, 1, 0), omega))
        relaxed = jnp.moveaxis(planes, 0, 1)
        gathered = []
        for direction in range(27):
            step_x = direction // 9 - 1
            step_y = (direction // 3) % 3 - 1
            step_z = direction % 3 - 1
            pulled = jnp.roll(relaxed[direction], (step_x, step_y, step_z), axis=(0, 1, 2))
            blocked = jnp.roll(solid_cell, (step_x, step_y, step_z), axis=(0, 1, 2))
            bounced = jnp.where(blocked, relaxed[26 - direction], pulled)
            gathered.append(jnp.where(solid_cell, before[direction], bounced))
        read = jnp.stack(gathered)
        current = read / weight
        signal = signal + radiate(read, radiation, bins, counts, sample_site, sample_patch, step_index)
    return current, signal
```

```python
import functools

import jax
import jax.numpy as jnp
from jax import lax
from jax.experimental import pallas as pl
from jax.experimental.pallas import tpu as pltpu
from jax.sharding import PartitionSpec as P

F32 = jnp.float32
BF16 = jnp.bfloat16
LEVELS = 128
OBS_BLK = 128
SOLID = 1e30
LIMIT = 1e29
LANES = 128
SUB = 8

WEIGHT = [
    (8.0 / 27.0, 2.0 / 27.0, 1.0 / 54.0, 1.0 / 216.0)[
        int(i // 9 != 1) + int(i // 3 % 3 != 1) + int(i % 3 != 1)
    ]
    for i in range(27)
]
STEP = [(i // 9 - 1, i // 3 % 3 - 1, i % 3 - 1) for i in range(27)]
VMEM = pl.BlockSpec(memory_space=pltpu.VMEM)
SMEM = pl.BlockSpec(memory_space=pltpu.SMEM)


def call(kernel, out_shape, scratch=(), in_specs=None, n_in=0, flops=0, nbytes=0, aliases=None):
    outs = out_shape if isinstance(out_shape, (list, tuple)) else [out_shape]
    return pl.pallas_call(
        kernel,
        out_shape=out_shape,
        in_specs=in_specs or [VMEM] * n_in,
        out_specs=[VMEM] * len(outs) if isinstance(out_shape, (list, tuple)) else VMEM,
        scratch_shapes=list(scratch),
        compiler_params=pltpu.CompilerParams(vmem_limit_bytes=56 * 1024 * 1024),
        cost_estimate=pl.CostEstimate(flops=flops, bytes_accessed=nbytes, transcendentals=0),
    )


def raw_moments(f):
    s, d, e = [], [], []
    for k in range(9):
        low, mid, high = f[3 * k : 3 * k + 3]
        ends = high + low
        s.append(ends + mid)
        d.append(high - low)
        e.append(ends)
    s_y, dy, ey, dz, dyz, ez = [], [], [], [], [], []
    for a in range(3):
        ends = s[3 * a + 2] + s[3 * a]
        s_y.append(ends + s[3 * a + 1])
        dy.append(s[3 * a + 2] - s[3 * a])
        ey.append(ends)
        dz.append(d[3 * a] + d[3 * a + 1] + d[3 * a + 2])
        dyz.append(d[3 * a + 2] - d[3 * a])
        ez.append(e[3 * a] + e[3 * a + 1] + e[3 * a + 2])
    m200 = s_y[2] + s_y[0]
    rho = m200 + s_y[1]
    jx = s_y[2] - s_y[0]
    jy = dy[0] + dy[1] + dy[2]
    jz = dz[0] + dz[1] + dz[2]
    m020 = ey[0] + ey[1] + ey[2]
    m002 = ez[0] + ez[1] + ez[2]
    m110 = dy[2] - dy[0]
    m101 = dz[2] - dz[0]
    m011 = dyz[0] + dyz[1] + dyz[2]
    return rho, jx, jy, jz, m200, m020, m002, m110, m101, m011


def unshift(k0, k1, k2, v, v2, vv, vp, vm):
    if k0 is None and k2 is None:
        return vm * k1, -(v2 * k1), vp * k1
    diff = v * k0
    ends = vv * k0
    if k1 is not None:
        diff = diff + k1
        ends = ends + v2 * k1
    if k2 is not None:
        ends = ends + k2
    high = 0.5 * (ends + diff)
    return high - diff, k0 - ends, high


def collide(f, retain):
    rho, jx, jy, jz, m200, m020, m002, m110, m101, m011 = raw_moments(f)
    inv = 1.0 / rho
    ux, uy, uz = jx * inv, jy * inv, jz * inv
    k200, k020, k002 = m200 - jx * ux, m020 - jy * uy, m002 - jz * uz
    third = 1.0 / 3.0
    d1 = retain * (k200 - k020)
    d2 = retain * (k200 - k002)
    xx = (rho + d1 + d2) * third
    yy = xx - d1
    zz = xx - d2
    xy = retain * (m110 - jx * uy)
    xz = retain * (m101 - jx * uz)
    yz = retain * (m011 - jy * uz)
    xy2, xz2, yz2 = 2.0 * xy, 2.0 * xz, 2.0 * yz
    xyi, xzi, yzi = xy2 * inv, xz2 * inv, yz2 * inv
    xxi = xx * inv
    yyi = yy * inv
    q_xy, q_xz, q_yz = xy * xyi, xz * xzi, yz * yzi
    xxyy = xxi * yy + q_xy
    xxzz = xxi * zz + q_xz
    yyzz = yyi * zz + q_yz
    xxyz = xxi * yz + xy * xzi
    xyyz = yyi * xz + xy * yzi
    xyzz = (zz * inv) * xy + xz * yzi
    full = xxi * (yyi * zz + q_yz) + (yyi * q_xz + (zz * inv) * q_xy) + (2.0 * xyi) * (xz * yzi)
    table = {
        (0, 0): (rho, None, xx),
        (1, 0): (None, xy, None),
        (2, 0): (yy, None, xxyy),
        (0, 1): (None, xz, None),
        (1, 1): (yz, None, xxyz),
        (2, 1): (None, xyyz, None),
        (0, 2): (zz, None, xxzz),
        (1, 2): (None, xyzz, None),
        (2, 2): (yyzz, None, full),
    }

    def speeds(v):
        return v, 2.0 * v, v * v, v + 0.5, v - 0.5

    sx, sy, sz = speeds(ux), speeds(uy), speeds(uz)
    after_x = {}
    for (b, c), ks in table.items():
        for a, value in enumerate(unshift(*ks, *sx)):
            after_x[a, b, c] = value
    out = [None] * 27
    for a in range(3):
        after_y = {}
        for c in range(3):
            triple = unshift(*(after_x[a, b, c] for b in range(3)), *sy)
            for b, value in enumerate(triple):
                after_y[b, c] = value
        for b in range(3):
            triple = unshift(*(after_y[b, c] for c in range(3)), *sz)
            for c, value in enumerate(triple):
                out[9 * a + 3 * b + c] = value
    return out, (rho, jx, jy, jz)


def rows_kernel(pops, omega, walls, up, down):
    planes, ny, nz = omega.shape
    row = lax.broadcasted_iota(jnp.int32, (SUB, nz), 0)

    def read(group, plane, first):
        part = pl.ds(first, SUB)
        if group < 27:
            return pops[group, plane, part, :] - 1.0
        if group == 27:
            return 1.0 - omega[plane, part, :]
        return walls[plane, part, :].astype(F32)

    def pack(group, first, at):
        if group > 28:
            return jnp.zeros((SUB, nz), F32)
        tile = None
        for plane in range(planes):
            turn = (2 * plane - at) % SUB
            piece = read(group, plane, first)
            piece = pltpu.roll(piece, turn, 0) if turn else piece
            tile = piece if tile is None else jnp.where(row // 2 == plane, piece, tile)
        return tile

    for pair in range(15):
        for out, first, at in ((up, ny - SUB, SUB - 2), (down, 0, 0)):
            both = [pack(2 * pair + k, first, at) for k in range(2)]
            out[pl.ds(16 * pair, 16), :] = jnp.concatenate(both, axis=0).astype(BF16)


def pack_x(post, plane, first, out):
    rows = post.shape[2]
    parts = [
        post[first + k, plane, :, :] * (1.0 / WEIGHT[first + k]) - 1.0 for k in range(9)
    ]
    spare = out.shape[0] - 9 * rows
    parts.append(jnp.zeros((spare, out.shape[1]), F32))
    out[...] = jnp.concatenate(parts, axis=0).astype(BF16)


def first_kernel(pops, omega, walls, before, after, post, retain, solid, send_up, send_down, wide_before, wide_after):
    planes, ny, nz = omega.shape
    rows = ny + SUB
    row = lax.broadcasted_iota(jnp.int32, (SUB, nz), 0)
    wide_before[...] = before[...].astype(F32)
    wide_after[...] = after[...].astype(F32)

    def beside(group, plane):
        low = wide_after[pl.ds(SUB * group, SUB), :]
        high = wide_before[pl.ds(SUB * group, SUB), :]
        turn_low, turn_high = (-2 * plane) % SUB, (SUB - 2 - 2 * plane) % SUB
        low = pltpu.roll(low, turn_low, 0) if turn_low else low
        high = pltpu.roll(high, turn_high, 0) if turn_high else high
        return jnp.where(row < 4, low, high)

    for plane in range(planes):
        retain[plane, pl.ds(0, ny), :] = 1.0 - omega[plane, :, :]
        retain[plane, pl.ds(ny, SUB), :] = beside(27, plane)
        solid[plane, pl.ds(0, ny), :] = walls[plane, :, :].astype(F32)
        solid[plane, pl.ds(ny, SUB), :] = beside(28, plane)
        for i in range(27):
            post[i, plane, pl.ds(0, ny), :] = pops[i, plane, :, :] * WEIGHT[i]
            post[i, plane, pl.ds(ny, SUB), :] = (beside(i, plane) + 1.0) * WEIGHT[i]

    def body(plane, carry):
        for t in range(rows // SUB):
            for part in range(nz // LANES):
                at = (plane, pl.ds(SUB * t, SUB), pl.ds(LANES * part, LANES))
                f = [post[(i, *at)] for i in range(27)]
                closed = solid[at] > 0.5
                out, _ = collide(f, retain[at])
                for i in range(27):
                    post[(i, *at)] = jnp.where(closed, SOLID, out[i])
        return carry

    lax.fori_loop(0, planes, body, 0)
    pack_x(post, planes - 1, 18, send_up)
    pack_x(post, 0, 0, send_down)


def pull(post, wide_before, wide_after, i, plane):
    planes, rows = post.shape[1], post.shape[2]
    sx, sy, sz = STEP[i]
    source = plane - sx
    if source < 0:
        value = (wide_before[pl.ds((i - 18) * rows, rows), :] + 1.0) * WEIGHT[i]
    elif source >= planes:
        value = (wide_after[pl.ds(i * rows, rows), :] + 1.0) * WEIGHT[i]
    else:
        value = post[i, source, :, :]
    if sy:
        value = pltpu.roll(value, sy % rows, 0)
    if sz:
        value = pltpu.roll(value, sz % value.shape[1], 1)
    return jnp.where(value > LIMIT, post[26 - i, plane, :, :], value)


def middle_kernel(post, retain, solid, pops, before, after, post2, macro, send_up, send_down, wide_before, wide_after, read):
    planes, rows, nz = retain.shape
    ny = rows - SUB
    wide_before[...] = before[...].astype(F32)
    wide_after[...] = after[...].astype(F32)
    for plane in range(planes):
        own = solid[plane, pl.ds(0, ny), :] > 0.5
        for i in range(27):
            value = pull(post, wide_before, wide_after, i, plane)
            read[i, pl.ds(0, ny), :] = jnp.where(own, pops[i, plane, :, :] * WEIGHT[i], value[:ny])
            read[i, pl.ds(ny, SUB), :] = value[ny:]

        def body(t, carry, plane=plane):
            for part in range(nz // LANES):
                at = (pl.ds(pl.multiple_of(SUB * t, SUB), SUB), pl.ds(LANES * part, LANES))
                f = [read[(i, *at)] for i in range(27)]
                closed = solid[(plane, *at)] > 0.5
                out, sums = collide(f, retain[(plane, *at)])
                for i in range(27):
                    post2[(i, plane, *at)] = jnp.where(closed, SOLID, out[i])
                macro[(0, plane, *at)] = sums[0] - 1.0
                for m in range(1, 4):
                    macro[(m, plane, *at)] = sums[m]
            return carry

        lax.fori_loop(0, rows // SUB, body, 0)
    pack_x(post2, planes - 1, 18, send_up)
    pack_x(post2, 0, 0, send_down)


def last_kernel(
    post, solid, pops, before, after, macro, radiation, bins, counts, sites, patches,
    out, send, wide_before, wide_after, fields,
):
    planes, rows, nz = solid.shape
    ny = rows - SUB
    slots = sites.shape[-1]
    halves = nz // LANES
    wide_before[...] = before[...].astype(F32)
    wide_after[...] = after[...].astype(F32)
    for plane in range(planes):
        own = solid[plane, pl.ds(0, ny), :] > 0.5
        sums = [None] * 4
        for i in range(27):
            value = pull(post, wide_before, wide_after, i, plane)[:ny]
            g = jnp.where(own, pops[i, plane, :, :], value * (1.0 / WEIGHT[i]))
            out[i, plane, :, :] = g
            f = g * WEIGHT[i]
            for m, sign in enumerate((1,) + STEP[i]):
                if sign:
                    term = f if sign > 0 else -f
                    sums[m] = term if sums[m] is None else sums[m] + term
        fields[1, 0, pl.ds(plane * ny, ny), :] = (sums[0] - 1.0).astype(BF16)
        for m in range(1, 4):
            fields[1, m, pl.ds(plane * ny, ny), :] = sums[m].astype(BF16)
        for m in range(4):
            fields[0, m, pl.ds(plane * ny, ny), :] = macro[m, plane, pl.ds(0, ny), :].astype(BF16)
    lines = planes * ny
    slot = lax.broadcasted_iota(jnp.int32, (slots, lines), 0)
    line = lax.broadcasted_iota(jnp.int32, (slots, lines), 1)
    wanted = jnp.full((slots, lines), -1, jnp.int32)
    for k in range(slots):
        site = jnp.where(k < counts[0, 0], sites[0, 0, k], -halves)
        wanted = jnp.where(slot == k, site, wanted)
    pick = [(wanted == line * halves + h).astype(BF16) for h in range(halves)]
    taken = []
    for step in range(2):
        parts = []
        for m in range(4):
            total = None
            for h in range(halves):
                term = jnp.dot(pick[h], fields[step, m, :, pl.ds(LANES * h, LANES)], preferred_element_type=F32)
                total = term if total is None else total + term
            parts.append(total)
        taken.append(jnp.concatenate(parts, axis=1))
    surface = jnp.concatenate(taken, axis=0).astype(BF16)
    response = lax.dot_general(
        surface, radiation[...], (((1,), (1,)), ((), ())), preferred_element_type=F32
    ).astype(BF16)

    n_patch, n_blk = bins.shape
    slot = lax.broadcasted_iota(jnp.int32, (LANES, n_patch), 0)
    named = lax.broadcasted_iota(jnp.int32, (LANES, n_patch), 1)
    wanted = jnp.full((LANES, n_patch), -1, jnp.int32)
    for k in range(slots):
        wanted = jnp.where(slot == k, patches[0, 0, k], wanted)
    chosen = (wanted == named).astype(BF16)
    level = lax.dot_general(
        bins[...].astype(F32).astype(BF16), chosen, (((0,), (1,)), ((), ())), preferred_element_type=F32
    )
    devices, _, width = send.shape
    first = lax.broadcasted_iota(jnp.int32, (SUB, width), 0) == 0
    for d in range(devices):
        send[d, pl.ds(0, 2 * slots), :] = response[:, d * width : (d + 1) * width]
        blk = d * width // OBS_BLK
        line = jnp.broadcast_to(level[blk : blk + 1, :width], (SUB, width))
        send[d, pl.ds(2 * slots, SUB), :] = jnp.where(first, line, 0.0).astype(BF16)


def bin_kernel(slots, received, signal, hits):
    devices, _, width = received.shape
    lev = received[:, pl.ds(2 * slots, SUB), :].astype(F32)[:, 0, :].astype(BF16)
    total = devices * slots
    src = lax.broadcasted_iota(jnp.int32, (total, devices), 0) // slots
    col = lax.broadcasted_iota(jnp.int32, (total, devices), 1)
    spread = jnp.dot((src == col).astype(BF16), lev, preferred_element_type=F32)
    slot = lax.broadcasted_iota(jnp.int32, (total, width), 0) % slots
    lane = lax.broadcasted_iota(jnp.int32, (total, width), 1)
    mine = jnp.where(slot == lane, spread, 0.0).astype(BF16)
    level = jnp.dot(mine, jnp.ones((width, LEVELS), BF16), preferred_element_type=F32)
    lane = lax.broadcasted_iota(jnp.int32, (total, LEVELS), 1).astype(F32)
    for step in range(2):
        hit = (level + float(step) == lane).astype(F32).astype(BF16)
        hits[:, pl.ds(step * slots, slots), :] = hit.reshape(devices, slots, LEVELS)
    left = received[:, pl.ds(0, 2 * slots), :].reshape(2 * total, width)
    right = hits[...].reshape(2 * total, LEVELS)
    signal[...] = lax.dot_general(left, right, (((0,), (0,)), ((), ())), preferred_element_type=F32)


def per_device(populations, omega, walls, radiation, bins, counts, sample_site, sample_patch):
    _, planes, ny, nz = populations.shape
    rows = ny + SUB
    slots = sample_site.shape[-1]
    size_x, size_y = lax.axis_size("gx"), lax.axis_size("gy")
    devices = size_x * size_y
    width = radiation.shape[0] // devices

    def exchange(up, down, axis, size):
        right = [(i, (i + 1) % size) for i in range(size)]
        left = [(j, i) for i, j in right]
        return lax.ppermute(up, axis, right), lax.ppermute(down, axis, left)

    beside = jax.ShapeDtypeStruct((30 * SUB, nz), BF16)
    up, down = call(rows_kernel, [beside, beside], n_in=3)(populations, omega, walls)
    before, after = exchange(up, down, "gy", size_y)

    lattice = jax.ShapeDtypeStruct((27, planes, rows, nz), F32)
    cells = jax.ShapeDtypeStruct((planes, rows, nz), F32)
    face = jax.ShapeDtypeStruct((9 * rows + SUB, nz), BF16)
    wide = pltpu.VMEM((30 * SUB, nz), F32)
    post, retain, solid, up, down = call(
        first_kernel, [lattice, cells, cells, face, face], [wide, wide], n_in=5
    )(populations, omega, walls, before, after)
    before, after = exchange(up, down, "gx", size_x)

    wide = pltpu.VMEM(face.shape, F32)
    post, macro, up, down = call(
        middle_kernel,
        [lattice, jax.ShapeDtypeStruct((4, planes, rows, nz), F32), face, face],
        [wide, wide, pltpu.VMEM((27, rows, nz), F32)],
        n_in=6,
    )(post, retain, solid, populations, before, after)
    before, after = exchange(up, down, "gx", size_x)

    advanced, send = call(
        last_kernel,
        [
            jax.ShapeDtypeStruct(populations.shape, F32),
            jax.ShapeDtypeStruct((devices, 2 * slots + SUB, width), BF16),
        ],
        [wide, wide, pltpu.VMEM((2, 4, planes * ny, nz), BF16)],
        in_specs=[VMEM] * 8 + [SMEM] * 3,
    )(post, solid, populations, before, after, macro, radiation, bins, counts, sample_site, sample_patch)
    received = lax.all_to_all(send, ("gx", "gy"), 0, 0, tiled=True)
    signal = call(
        functools.partial(bin_kernel, slots),
        jax.ShapeDtypeStruct((width, LEVELS), F32),
        [pltpu.VMEM((devices, 2 * slots, LEVELS), BF16)],
        n_in=1,
    )(received)
    return advanced, signal


def solution(mesh):
    return jax.shard_map(
        per_device,
        mesh=mesh,
        in_specs=(
            P(None, "gx", "gy", None),
            P("gx", "gy", None),
            P("gx", "gy", None),
            P(),
            P(),
            P("gx", "gy"),
            P("gx", "gy", None),
            P("gx", "gy", None),
        ),
        out_specs=(P(None, "gx", "gy", None), P(("gx", "gy"), None)),
        check_vma=False,
    )
```

```python
import jax
import jax.numpy as jnp
from jax import lax
from jax.experimental import pallas as pl
from jax.experimental.pallas import tpu as pltpu
from jax.sharding import PartitionSpec as P

F32 = jnp.float32
BF16 = jnp.bfloat16
LEVELS = 128
OBS_BLK = 128
SOLID = 1e30
LIMIT = 1e29
LANES = 128
SUB = 8

WEIGHT = [
    (8.0 / 27.0, 2.0 / 27.0, 1.0 / 54.0, 1.0 / 216.0)[
        int(i // 9 != 1) + int(i // 3 % 3 != 1) + int(i % 3 != 1)
    ]
    for i in range(27)
]
STEP = [(i // 9 - 1, i // 3 % 3 - 1, i % 3 - 1) for i in range(27)]
VMEM = pl.BlockSpec(memory_space=pltpu.VMEM)
SMEM = pl.BlockSpec(memory_space=pltpu.SMEM)
HBM = pl.BlockSpec(memory_space=pltpu.HBM)


def call(kernel, in_specs, out, scratch=(), aliases=None, cost=0, limit=14 * 1024 * 1024):
    return pl.pallas_call(
        kernel,
        out_shape=[jax.ShapeDtypeStruct(shape, dtype) for _, shape, dtype in out],
        in_specs=in_specs,
        out_specs=[spec for spec, _, _ in out],
        scratch_shapes=list(scratch),
        input_output_aliases=aliases or {},
        compiler_params=pltpu.CompilerParams(vmem_limit_bytes=limit),
        cost_estimate=pl.CostEstimate(flops=cost, bytes_accessed=cost, transcendentals=0),
    )


def raw_moments(f):
    s, d, e = [], [], []
    for k in range(9):
        low, mid, high = f[3 * k : 3 * k + 3]
        ends = high + low
        s.append(ends + mid)
        d.append(high - low)
        e.append(ends)
    s_y, dy, ey, dz, dyz, ez = [], [], [], [], [], []
    for a in range(3):
        ends = s[3 * a + 2] + s[3 * a]
        s_y.append(ends + s[3 * a + 1])
        dy.append(s[3 * a + 2] - s[3 * a])
        ey.append(ends)
        dz.append(d[3 * a] + d[3 * a + 1] + d[3 * a + 2])
        dyz.append(d[3 * a + 2] - d[3 * a])
        ez.append(e[3 * a] + e[3 * a + 1] + e[3 * a + 2])
    m200 = s_y[2] + s_y[0]
    rho = m200 + s_y[1]
    jx = s_y[2] - s_y[0]
    jy = dy[0] + dy[1] + dy[2]
    jz = dz[0] + dz[1] + dz[2]
    m020 = ey[0] + ey[1] + ey[2]
    m002 = ez[0] + ez[1] + ez[2]
    m110 = dy[2] - dy[0]
    m101 = dz[2] - dz[0]
    m011 = dyz[0] + dyz[1] + dyz[2]
    return rho, jx, jy, jz, m200, m020, m002, m110, m101, m011


def unshift(k0, k1, k2, v, v2, vv, vp, vm):
    if k0 is None and k2 is None:
        return vm * k1, -(v2 * k1), vp * k1
    diff = v * k0
    ends = vv * k0
    if k1 is not None:
        diff = diff + k1
        ends = ends + v2 * k1
    if k2 is not None:
        ends = ends + k2
    high = 0.5 * (ends + diff)
    return high - diff, k0 - ends, high


def collide(f, retain):
    rho, jx, jy, jz, m200, m020, m002, m110, m101, m011 = raw_moments(f)
    inv = 1.0 / rho
    ux, uy, uz = jx * inv, jy * inv, jz * inv
    k200, k020, k002 = m200 - jx * ux, m020 - jy * uy, m002 - jz * uz
    third = 1.0 / 3.0
    d1 = retain * (k200 - k020)
    d2 = retain * (k200 - k002)
    xx = (rho + d1 + d2) * third
    yy = xx - d1
    zz = xx - d2
    xy = retain * (m110 - jx * uy)
    xz = retain * (m101 - jx * uz)
    yz = retain * (m011 - jy * uz)
    xy2, xz2, yz2 = 2.0 * xy, 2.0 * xz, 2.0 * yz
    xyi, xzi, yzi = xy2 * inv, xz2 * inv, yz2 * inv
    xxi = xx * inv
    yyi = yy * inv
    q_xy, q_xz, q_yz = xy * xyi, xz * xzi, yz * yzi
    xxyy = xxi * yy + q_xy
    xxzz = xxi * zz + q_xz
    yyzz = yyi * zz + q_yz
    xxyz = xxi * yz + xy * xzi
    xyyz = yyi * xz + xy * yzi
    xyzz = (zz * inv) * xy + xz * yzi
    full = xxi * (yyi * zz + q_yz) + (yyi * q_xz + (zz * inv) * q_xy) + (2.0 * xyi) * (xz * yzi)
    table = {
        (0, 0): (rho, None, xx),
        (1, 0): (None, xy, None),
        (2, 0): (yy, None, xxyy),
        (0, 1): (None, xz, None),
        (1, 1): (yz, None, xxyz),
        (2, 1): (None, xyyz, None),
        (0, 2): (zz, None, xxzz),
        (1, 2): (None, xyzz, None),
        (2, 2): (yyzz, None, full),
    }

    def speeds(v):
        return v, 2.0 * v, v * v, v + 0.5, v - 0.5

    sx, sy, sz = speeds(ux), speeds(uy), speeds(uz)
    after_x = {}
    for (b, c), ks in table.items():
        for a, value in enumerate(unshift(*ks, *sx)):
            after_x[a, b, c] = value
    out = [None] * 27
    for a in range(3):
        after_y = {}
        for c in range(3):
            triple = unshift(*(after_x[a, b, c] for b in range(3)), *sy)
            for b, value in enumerate(triple):
                after_y[b, c] = value
        for b in range(3):
            triple = unshift(*(after_y[b, c] for c in range(3)), *sz)
            for c, value in enumerate(triple):
                out[9 * a + 3 * b + c] = value
    return out, (rho, jx, jy, jz)


def start_all(copies):
    for copy in copies:
        copy.start()
    return copies


def rows_kernel(pops_in, omega_in, walls_in, up, down, pops, omega, walls, sems):
    planes, ny, nz = omega.shape
    row = lax.broadcasted_iota(jnp.int32, (SUB, nz), 0)
    chunk = 4
    spans = [pl.ds(i, min(chunk, 27 - i)) for i in range(0, 27, chunk)]
    cells = [
        pltpu.make_async_copy(omega_in, omega, sems.at[len(spans)]),
        pltpu.make_async_copy(walls_in, walls, sems.at[len(spans) + 1]),
    ]
    copies = [pltpu.make_async_copy(pops_in.at[span], pops.at[span], sems.at[k]) for k, span in enumerate(spans)]
    start_all(cells + copies)

    def read(group, plane, first):
        part = pl.ds(first, SUB)
        if group < 27:
            return pops[group, plane, part, :] - 1.0
        if group == 27:
            return 1.0 - omega[plane, part, :]
        return walls[plane, part, :].astype(F32)

    def pack(group, first, at):
        if group > 28:
            return jnp.zeros((SUB, nz), F32)
        tile = None
        for plane in range(planes):
            turn = (2 * plane - at) % SUB
            piece = read(group, plane, first)
            piece = pltpu.roll(piece, turn, 0) if turn else piece
            tile = piece if tile is None else jnp.where(row // 2 == plane, piece, tile)
        return tile

    for pair in range(15):
        if pair % 2 == 0 and pair < 14:
            copies[pair // 2].wait()
        if pair == 13:
            for copy in cells:
                copy.wait()
        for out, first, at in ((up, ny - SUB, SUB - 2), (down, 0, 0)):
            both = [pack(2 * pair + k, first, at) for k in range(2)]
            out[pl.ds(16 * pair, 16), :] = jnp.concatenate(both, axis=0).astype(BF16)


def first_main_kernel(pops, omega, walls, post):
    planes, ny, nz = omega.shape

    def body(plane, carry):
        for t in range(ny // SUB):
            for part in range(nz // LANES):
                at = (plane, pl.ds(SUB * t, SUB), pl.ds(LANES * part, LANES))
                f = [pops[(i, *at)] * WEIGHT[i] for i in range(27)]
                closed = walls[at] == 1
                out, _ = collide(f, 1.0 - omega[at])
                for i in range(27):
                    post[(i, *at)] = jnp.where(closed, SOLID, out[i])
        return carry

    lax.fori_loop(0, planes, body, 0)


def fold(tiles):
    if len(tiles) == 1:
        return tiles[0]
    row = lax.broadcasted_iota(jnp.int32, tiles[0].shape, 0)
    return jnp.where((row < 2) | (row > 5), tiles[0], pltpu.roll(tiles[1], 4, 0))


def pack_x(main, halo, plane, first, out):
    ny, nz = main.shape[2:]
    scaled = lambda ref, i: ref[i, plane, :, :] * (1.0 / WEIGHT[i]) - 1.0
    for k in range(9):
        out[pl.ds(ny * k, ny), :] = scaled(main, first + k).astype(BF16)
    tiles = [fold([scaled(halo, first + k + j) for j in range(2) if k + j < 9]) for k in range(0, 9, 2)]
    tiles.append(jnp.zeros((SUB, nz), F32))
    out[pl.ds(9 * ny, SUB * len(tiles)), :] = jnp.concatenate(tiles, axis=0).astype(BF16)


def first_halo_kernel(before, after, main, halo, retain, solid, send_up, send_down, wide_before, wide_after):
    _, planes, _, nz = halo.shape
    row = lax.broadcasted_iota(jnp.int32, (SUB, nz), 0)
    wide_before[...] = before[...].astype(F32)
    wide_after[...] = after[...].astype(F32)

    def beside(group, plane):
        low = wide_after[pl.ds(SUB * group, SUB), :]
        high = wide_before[pl.ds(SUB * group, SUB), :]
        turn_low, turn_high = (-2 * plane) % SUB, (SUB - 2 - 2 * plane) % SUB
        low = pltpu.roll(low, turn_low, 0) if turn_low else low
        high = pltpu.roll(high, turn_high, 0) if turn_high else high
        return jnp.where(row < 4, low, high)

    for plane in range(planes):
        retain[plane, :, :] = beside(27, plane)
        solid[plane, :, :] = beside(28, plane)
        for i in range(27):
            halo[i, plane, :, :] = (beside(i, plane) + 1.0) * WEIGHT[i]

    def body(plane, carry):
        for part in range(nz // LANES):
            at = (plane, slice(None), pl.ds(LANES * part, LANES))
            closed = solid[at] > 0.5
            out, _ = collide([halo[(i, *at)] for i in range(27)], retain[at])
            for i in range(27):
                halo[(i, *at)] = jnp.where(closed, SOLID, out[i])
        return carry

    lax.fori_loop(0, planes, body, 0)
    pack_x(main, halo, planes - 1, 18, send_up)
    pack_x(main, halo, 0, 0, send_down)


def turned(value, i):
    _, sy, sz = STEP[i]
    if sy:
        value = pltpu.roll(value, sy % value.shape[0], 0)
    if sz:
        value = pltpu.roll(value, sz % value.shape[1], 1)
    return value


def pull(load, i, plane):
    value = turned(load(i, plane - STEP[i][0]), i)
    return jnp.where(value > LIMIT, load(26 - i, plane), value)


def widen(face, wide):
    wide[...] = face[...].astype(F32)


def loader(planes, ny, places, before=None, after=None):
    def load(i, plane):
        if 0 <= plane < planes:
            main, halo, at = places[plane]
            return jnp.concatenate([main[i, at, :, :], halo[i, at, :, :]], axis=0)
        wide, k = (before, i - 18) if plane < 0 else (after, i)
        halo = wide[pl.ds(9 * ny + SUB * (k // 2), SUB), :]
        if k % 2:
            halo = pltpu.roll(halo, 4, 0)
        both = jnp.concatenate([wide[pl.ds(ny * k, ny), :], halo], axis=0)
        return (both + 1.0) * WEIGHT[i]

    return load


def middle(mine, load, pops, omega, walls, retain, solid, main2, halo2, macro, read):
    planes, ny, nz = omega.shape
    for at, plane in enumerate(mine):
        own = walls[plane, :, :] == 1
        for i in range(27):
            value = pull(load, i, plane)
            read[i, pl.ds(0, ny), :] = jnp.where(own, pops[i, plane, :, :] * WEIGHT[i], value[:ny])
            read[i, pl.ds(ny, SUB), :] = value[ny:]
        for t in range(ny // SUB + 1):
            for part in range(nz // LANES):
                rows, cols = pl.ds(SUB * t, SUB), pl.ds(LANES * part, LANES)
                inner = SUB * t < ny
                if inner:
                    closed = walls[plane, rows, cols] == 1
                    keep = 1.0 - omega[plane, rows, cols]
                else:
                    closed = solid[plane, :, cols] > 0.5
                    keep = retain[plane, :, cols]
                out, sums = collide([read[i, rows, cols] for i in range(27)], keep)
                for i in range(27):
                    value = jnp.where(closed, SOLID, out[i])
                    if inner:
                        main2[i, at, rows, cols] = value
                    else:
                        halo2[i, at, :, cols] = value
                if inner:
                    macro[0, at, rows, cols] = sums[0] - 1.0
                    for m in range(1, 4):
                        macro[m, at, rows, cols] = sums[m]


def middle_inner_kernel(main, halo, pops, omega, walls, retain, solid, main2, halo2, macro, read):
    planes, ny, _ = omega.shape
    load = loader(planes, ny, [(main, halo, p) for p in range(planes)])
    middle(range(1, planes - 1), load, pops, omega, walls, retain, solid, main2, halo2, macro, read)


def middle_outer_kernel(
    main, halo, pops, omega, walls, retain, solid, before, after, _,
    main2, halo2, macro, send_up, send_down, read, wide_before, wide_after,
):
    planes, ny, _ = omega.shape
    widen(before, wide_before)
    widen(after, wide_after)
    load = loader(planes, ny, [(main, halo, p) for p in range(planes)], wide_before, wide_after)
    middle((0, planes - 1), load, pops, omega, walls, retain, solid, main2, halo2, macro, read)
    pack_x(main2, halo2, 1, 18, send_up)
    pack_x(main2, halo2, 0, 0, send_down)


def add_moments(sums, i, f):
    for m, sign in enumerate((1,) + STEP[i]):
        if sign:
            term = f if sign > 0 else -f
            sums[m] = term if sums[m] is None else sums[m] + term


def respond(planes, radiation, pick, fields):
    for p, rows in enumerate(planes):
        ny = rows[0].shape[0]
        for m in range(4):
            fields[m, pl.ds(p * ny, ny), :] = rows[m].astype(BF16)
    parts = []
    for m in range(4):
        total = None
        for h in range(pick.shape[0]):
            term = jnp.dot(pick[h, :, :], fields[m, :, pl.ds(LANES * h, LANES)], preferred_element_type=F32)
            total = term if total is None else total + term
        parts.append(total)
    surface = jnp.concatenate(parts, axis=1).astype(BF16)
    response = lax.dot_general(
        surface, radiation[...], (((1,), (1,)), ((), ())), preferred_element_type=F32
    )
    return response.astype(BF16)


def slots_kernel(bins, counts, sites, patches, pick, level):
    halves, slots, lines = pick.shape
    slot = lax.broadcasted_iota(jnp.int32, (slots, lines), 0)
    line = lax.broadcasted_iota(jnp.int32, (slots, lines), 1)
    wanted = jnp.full((slots, lines), -1, jnp.int32)
    for k in range(slots):
        site = jnp.where(k < counts[0, 0], sites[0, 0, k], -halves)
        wanted = jnp.where(slot == k, site, wanted)
    for h in range(halves):
        pick[h, :, :] = (wanted == line * halves + h).astype(BF16)

    n_patch = bins.shape[1]
    slot = lax.broadcasted_iota(jnp.int32, (LANES, n_patch), 0)
    named = lax.broadcasted_iota(jnp.int32, (LANES, n_patch), 1)
    wanted = jnp.full((LANES, n_patch), -1, jnp.int32)
    for k in range(slots):
        wanted = jnp.where(slot == k, patches[0, 0, k], wanted)
    chosen = (wanted == named).astype(BF16)
    per_block = lax.dot_general(
        bins[...].astype(F32).astype(BF16), chosen, (((1,), (1,)), ((), ())), preferred_element_type=F32
    )
    devices, _, width = level.shape
    first = lax.broadcasted_iota(jnp.int32, (SUB, width), 0) == 0
    for d in range(devices):
        blk = d * width // OBS_BLK
        line = jnp.broadcast_to(per_block[blk : blk + 1, :width], (SUB, width))
        level[d, :, :] = jnp.where(first, line, 0.0).astype(BF16)


def last_early_kernel(
    main_in, halo_in, main_out, halo_out, pops, walls, macro_in, macro_out, radiation, pick,
    out, spare, part, inner, send, g_out, fields, sems,
):
    planes, ny, _ = walls.shape
    last = planes - 1
    places = [(main_out, halo_out, 0)]
    places += [(main_in, halo_in, p) for p in range(planes - 2)]
    places += [(main_out, halo_out, 1)]
    load = loader(planes, ny, places)
    copies = []
    for plane in (0, last, *range(1, last)):
        own = walls[plane, :, :] == 1
        edge = {0: 0, last: 1}.get(plane)
        sums = [None] * 4
        for i in range(27):
            if 0 <= plane - STEP[i][0] <= last:
                value = pull(load, i, plane)[:ny]
                g = jnp.where(own, pops[i, plane, :, :], value * (1.0 / WEIGHT[i]))
                g_out[i, plane, :, :] = g
                add_moments(sums, i, g * WEIGHT[i])
            else:
                bounced = load(26 - i, plane)[:ny]
                spare[edge, i % 9, :, :] = jnp.where(own, pops[i, plane, :, :] * WEIGHT[i], bounced)
        for m in range(4):
            if edge is None:
                inner[m, plane - 1, :, :] = sums[m] - 1.0 if m == 0 else sums[m]
            else:
                part[m, edge, :, :] = sums[m]
        span = pl.ds((0, 9)[edge], 18) if edge is not None else pl.ds(0, 27)
        copies += start_all(
            [pltpu.make_async_copy(g_out.at[span, plane], out.at[span, plane], sems.at[len(copies)])]
        )
    rows = [[macro_out[m, 0, :, :] for m in range(4)]]
    rows += [[macro_in[m, p, :, :] for m in range(4)] for p in range(planes - 2)]
    rows += [[macro_out[m, 1, :, :] for m in range(4)]]
    response = respond(rows, radiation, pick, fields)
    devices, _, width = send.shape
    for d in range(devices):
        send[d, :, :] = response[:, d * width : (d + 1) * width]
    for copy in copies:
        copy.wait()


def last_kernel(
    before, after, walls, spare, part, inner, radiation, pick, early, level, started,
    out, send, g_out, fields, wide_before, wide_after, sems,
):
    planes, ny, _ = walls.shape
    last = planes - 1
    widen(before, wide_before)
    widen(after, wide_after)
    load = loader(planes, ny, None, wide_before, wide_after)
    rows, copies = {}, []
    for edge, (plane, first) in enumerate(((0, 18), (last, 0))):
        own = walls[plane, :, :] == 1
        sums = [part[m, edge, :, :] for m in range(4)]
        for k in range(9):
            i = first + k
            value = turned(load(i, plane - STEP[i][0]), i)[:ny]
            f = jnp.where(own | (value > LIMIT), spare[edge, k, :, :], value)
            g_out[k, edge, :, :] = f * (1.0 / WEIGHT[i])
            add_moments(sums, i, f)
        rows[plane] = [sums[0] - 1.0, *sums[1:]]
        copies += start_all(
            [pltpu.make_async_copy(g_out.at[:, edge], out.at[pl.ds(first, 9), plane], sems.at[edge])]
        )
    for p in range(planes - 2):
        rows[p + 1] = [inner[m, p, :, :] for m in range(4)]
    response = respond([rows[p] for p in range(planes)], radiation, pick, fields)
    devices, _, width = send.shape
    slots = early.shape[1]
    for d in range(devices):
        send[d, pl.ds(0, slots), :] = early[d, :, :]
        send[d, pl.ds(slots, slots), :] = response[:, d * width : (d + 1) * width]
        send[d, pl.ds(2 * slots, SUB), :] = level[d, :, :]
    for copy in copies:
        copy.wait()


def bin_kernel(received, signal, hits):
    devices, rows, width = received.shape
    slots = (rows - SUB) // 2
    lev = received[:, pl.ds(2 * slots, SUB), :].astype(F32)[:, 0, :].astype(BF16)
    total = devices * slots
    src = lax.broadcasted_iota(jnp.int32, (total, devices), 0) // slots
    col = lax.broadcasted_iota(jnp.int32, (total, devices), 1)
    spread = jnp.dot((src == col).astype(BF16), lev, preferred_element_type=F32)
    slot = lax.broadcasted_iota(jnp.int32, (total, width), 0) % slots
    lane = lax.broadcasted_iota(jnp.int32, (total, width), 1)
    mine = jnp.where(slot == lane, spread, 0.0).astype(BF16)
    level = jnp.dot(mine, jnp.ones((width, LEVELS), BF16), preferred_element_type=F32)
    lane = lax.broadcasted_iota(jnp.int32, (total, LEVELS), 1).astype(F32)
    for step in range(2):
        hit = (level + float(step) == lane).astype(F32).astype(BF16)
        hits[:, pl.ds(step * slots, slots), :] = hit.reshape(devices, slots, LEVELS)
    left = received[:, pl.ds(0, 2 * slots), :].reshape(2 * total, width)
    right = hits[...].reshape(2 * total, LEVELS)
    signal[...] = lax.dot_general(left, right, (((0,), (0,)), ((), ())), preferred_element_type=F32)


def per_device(populations, omega, walls, radiation, bins, counts, sample_site, sample_patch):
    _, planes, ny, nz = populations.shape
    slots = sample_site.shape[-1]
    size_x, size_y = lax.axis_size("gx"), lax.axis_size("gy")
    devices = size_x * size_y
    width = radiation.shape[0] // devices

    def exchange(up, down, axis, size):
        right = [(i, (i + 1) % size) for i in range(size)]
        left = [(j, i) for i, j in right]
        return lax.ppermute(up, axis, right), lax.ppermute(down, axis, left)

    dma = pltpu.SemaphoreType.DMA
    block, cells = populations.shape, (planes, ny, nz)
    beside = (30 * SUB, nz)
    up, down = call(
        rows_kernel,
        [HBM] * 3,
        [(VMEM, beside, BF16)] * 2,
        [pltpu.VMEM(block, F32), pltpu.VMEM(cells, F32), pltpu.VMEM(cells, walls.dtype), dma((9,))],
        cost=1 << 20,
        limit=64800000,
    )(populations, omega, walls)
    before, after = exchange(up, down, "gy", size_y)
    pick, level = call(
        slots_kernel,
        [VMEM] + [SMEM] * 3,
        [(VMEM, (nz // LANES, slots, planes * ny), BF16), (VMEM, (devices, SUB, width), BF16)],
        cost=1 << 18,
    )(bins.T, counts, sample_site, sample_patch)
    (main,) = call(first_main_kernel, [VMEM] * 3, [(VMEM, block, F32)], cost=1 << 22)(populations, omega, walls)

    edge = (planes, SUB, nz)
    face = (9 * ny + 6 * SUB, nz)
    faces = [(VMEM, face, BF16)] * 2
    halo, retain, solid, up, down = call(
        first_halo_kernel,
        [VMEM] * 3,
        [(VMEM, (27, *edge), F32), (VMEM, edge, F32), (VMEM, edge, F32), *faces],
        [pltpu.VMEM(beside, F32)] * 2,
        cost=1 << 20,
    )(before, after, main)
    before, after = exchange(up, down, "gx", size_x)

    def relaxed(n):
        return [(VMEM, (27, n, ny, nz), F32), (VMEM, (27, n, SUB, nz), F32), (VMEM, (4, n, ny, nz), F32)]

    read = pltpu.VMEM((27, ny + SUB, nz), F32)
    wide = [pltpu.VMEM(face, F32)] * 2
    args = (main, halo, populations, omega, walls, retain, solid)
    main_in, halo_in, macro_in = call(
        middle_inner_kernel, [VMEM] * 7, relaxed(planes - 2), [read], cost=1 << 22
    )(*args)
    main_out, halo_out, macro_out, up, down = call(
        middle_outer_kernel, [VMEM] * 10, relaxed(2) + faces, [read, *wide], cost=1 << 22
    )(*args, before, after, macro_in)
    before, after = exchange(up, down, "gx", size_x)

    fields = pltpu.VMEM((4, planes * ny, nz), BF16)
    inner = (4, planes - 2, ny, nz)
    started, spare, part, inner, early = call(
        last_early_kernel,
        [VMEM] * 10,
        [
            (HBM, block, F32),
            (VMEM, (2, 9, ny, nz), F32),
            (VMEM, (4, 2, ny, nz), F32),
            (VMEM, inner, F32),
            (VMEM, (devices, slots, width), BF16),
        ],
        [pltpu.VMEM(block, F32), fields, dma((planes,))],
        cost=1 << 22,
    )(main_in, halo_in, main_out, halo_out, populations, walls, macro_in, macro_out, radiation, pick)
    advanced, send = call(
        last_kernel,
        [VMEM] * 10 + [HBM],
        [(HBM, block, F32), (VMEM, (devices, 2 * slots + SUB, width), BF16)],
        [pltpu.VMEM((9, 2, ny, nz), F32), fields, *wide, dma((2,))],
        aliases={10: 0},
        cost=1 << 22,
    )(before, after, walls, spare, part, inner, radiation, pick, early, level, started)
    received = lax.all_to_all(send, ("gx", "gy"), 0, 0, tiled=True)
    (signal,) = call(
        bin_kernel, [VMEM], [(VMEM, (width, LEVELS), F32)], [pltpu.VMEM((devices, 2 * slots, LEVELS), BF16)], cost=1 << 20
    )(received)
    return advanced, signal


def solution(mesh):
    return jax.shard_map(
        per_device,
        mesh=mesh,
        in_specs=(
            P(None, "gx", "gy", None),
            P("gx", "gy", None),
            P("gx", "gy", None),
            P(),
            P(),
            P("gx", "gy"),
            P("gx", "gy", None),
            P("gx", "gy", None),
        ),
        out_specs=(P(None, "gx", "gy", None), P(("gx", "gy"), None)),
        check_vma=False,
    )
```

```python
import jax
import jax.numpy as jnp
from jax import lax
from jax.experimental import pallas as pl
from jax.experimental.pallas import tpu as pltpu
from jax.sharding import PartitionSpec as P

F32 = jnp.float32
BF16 = jnp.bfloat16
LEVELS = 128
OBS_BLK = 128
SOLID = 1e30
LIMIT = 1e29
LANES = 128
SUB = 8

WEIGHT = [
    (8.0 / 27.0, 2.0 / 27.0, 1.0 / 54.0, 1.0 / 216.0)[
        int(i // 9 != 1) + int(i // 3 % 3 != 1) + int(i % 3 != 1)
    ]
    for i in range(27)
]
STEP = [(i // 9 - 1, i // 3 % 3 - 1, i % 3 - 1) for i in range(27)]
VMEM = pl.BlockSpec(memory_space=pltpu.VMEM)
SMEM = pl.BlockSpec(memory_space=pltpu.SMEM)
HBM = pl.BlockSpec(memory_space=pltpu.HBM)


def call(kernel, in_specs, out, scratch=(), aliases=None, cost=0, limit=14 * 1024 * 1024):
    return pl.pallas_call(
        kernel,
        out_shape=[jax.ShapeDtypeStruct(shape, dtype) for _, shape, dtype in out],
        in_specs=in_specs,
        out_specs=[spec for spec, _, _ in out],
        scratch_shapes=list(scratch),
        input_output_aliases=aliases or {},
        compiler_params=pltpu.CompilerParams(vmem_limit_bytes=limit),
        cost_estimate=pl.CostEstimate(flops=cost, bytes_accessed=cost, transcendentals=0),
    )


def raw_moments(f):
    s, d, e = [], [], []
    for k in range(9):
        low, mid, high = f[3 * k : 3 * k + 3]
        ends = high + low
        s.append(ends + mid)
        d.append(high - low)
        e.append(ends)
    s_y, dy, ey, dz, dyz, ez = [], [], [], [], [], []
    for a in range(3):
        ends = s[3 * a + 2] + s[3 * a]
        s_y.append(ends + s[3 * a + 1])
        dy.append(s[3 * a + 2] - s[3 * a])
        ey.append(ends)
        dz.append(d[3 * a] + d[3 * a + 1] + d[3 * a + 2])
        dyz.append(d[3 * a + 2] - d[3 * a])
        ez.append(e[3 * a] + e[3 * a + 1] + e[3 * a + 2])
    m200 = s_y[2] + s_y[0]
    rho = m200 + s_y[1]
    jx = s_y[2] - s_y[0]
    jy = dy[0] + dy[1] + dy[2]
    jz = dz[0] + dz[1] + dz[2]
    m020 = ey[0] + ey[1] + ey[2]
    m002 = ez[0] + ez[1] + ez[2]
    m110 = dy[2] - dy[0]
    m101 = dz[2] - dz[0]
    m011 = dyz[0] + dyz[1] + dyz[2]
    return rho, jx, jy, jz, m200, m020, m002, m110, m101, m011


def unshift(k0, k1, k2, v, v2, vv, vp, vm):
    if k0 is None and k2 is None:
        return vm * k1, -(v2 * k1), vp * k1
    diff = v * k0
    ends = vv * k0
    if k1 is not None:
        diff = diff + k1
        ends = ends + v2 * k1
    if k2 is not None:
        ends = ends + k2
    high = 0.5 * (ends + diff)
    return high - diff, k0 - ends, high


def collide(f, retain):
    rho, jx, jy, jz, m200, m020, m002, m110, m101, m011 = raw_moments(f)
    inv = 1.0 / rho
    ux, uy, uz = jx * inv, jy * inv, jz * inv
    k200, k020, k002 = m200 - jx * ux, m020 - jy * uy, m002 - jz * uz
    third = 1.0 / 3.0
    d1 = retain * (k200 - k020)
    d2 = retain * (k200 - k002)
    xx = (rho + d1 + d2) * third
    yy = xx - d1
    zz = xx - d2
    xy = retain * (m110 - jx * uy)
    xz = retain * (m101 - jx * uz)
    yz = retain * (m011 - jy * uz)
    xy2, xz2, yz2 = 2.0 * xy, 2.0 * xz, 2.0 * yz
    xyi, xzi, yzi = xy2 * inv, xz2 * inv, yz2 * inv
    xxi = xx * inv
    yyi = yy * inv
    q_xy, q_xz, q_yz = xy * xyi, xz * xzi, yz * yzi
    xxyy = xxi * yy + q_xy
    xxzz = xxi * zz + q_xz
    yyzz = yyi * zz + q_yz
    xxyz = xxi * yz + xy * xzi
    xyyz = yyi * xz + xy * yzi
    xyzz = (zz * inv) * xy + xz * yzi
    full = xxi * (yyi * zz + q_yz) + (yyi * q_xz + (zz * inv) * q_xy) + (2.0 * xyi) * (xz * yzi)
    table = {
        (0, 0): (rho, None, xx),
        (1, 0): (None, xy, None),
        (2, 0): (yy, None, xxyy),
        (0, 1): (None, xz, None),
        (1, 1): (yz, None, xxyz),
        (2, 1): (None, xyyz, None),
        (0, 2): (zz, None, xxzz),
        (1, 2): (None, xyzz, None),
        (2, 2): (yyzz, None, full),
    }

    def speeds(v):
        return v, 2.0 * v, v * v, v + 0.5, v - 0.5

    sx, sy, sz = speeds(ux), speeds(uy), speeds(uz)
    after_x = {}
    for (b, c), ks in table.items():
        for a, value in enumerate(unshift(*ks, *sx)):
            after_x[a, b, c] = value
    out = [None] * 27
    for a in range(3):
        after_y = {}
        for c in range(3):
            triple = unshift(*(after_x[a, b, c] for b in range(3)), *sy)
            for b, value in enumerate(triple):
                after_y[b, c] = value
        for b in range(3):
            triple = unshift(*(after_y[b, c] for c in range(3)), *sz)
            for c, value in enumerate(triple):
                out[9 * a + 3 * b + c] = value
    return out, (rho, jx, jy, jz)


def start_all(copies):
    for copy in copies:
        copy.start()
    return copies


def rows_order(side):
    outward = 1 - 2 * side
    both = [i for i in range(27) if STEP[i][1] == outward]
    return both, [i for i in range(27) if STEP[i][1] != outward]


def rows_kernel(pops_in, omega_in, walls_in, up, down, pops, omega, walls, packed, sems):
    planes, ny, nz = omega.shape
    row = lax.broadcasted_iota(jnp.int32, (SUB, nz), 0)
    chunk = 4
    spans = [pl.ds(i, min(chunk, 27 - i)) for i in range(0, 27, chunk)]
    cells = [
        pltpu.make_async_copy(omega_in, omega, sems.at[len(spans)]),
        pltpu.make_async_copy(walls_in, walls, sems.at[len(spans) + 1]),
    ]
    copies = [pltpu.make_async_copy(pops_in.at[span], pops.at[span], sems.at[k]) for k, span in enumerate(spans)]
    start_all(cells + copies)

    def read(group, plane, first):
        part = pl.ds(first, SUB)
        if group < 27:
            return pops[group, plane, part, :]
        if group == 27:
            return 1.0 - omega[plane, part, :]
        return walls[plane, part, :].astype(F32)

    def pack(group):
        for side, first, at in ((0, ny - SUB, SUB - 2), (1, 0, 0)):
            tile = None
            for plane in range(planes):
                turn = (2 * plane - at) % SUB
                piece = read(group, plane, first)
                piece = pltpu.roll(piece, turn, 0) if turn else piece
                tile = piece if tile is None else jnp.where(row // 2 == plane, piece, tile)
            packed[side, group, :, :] = tile

    for copy in cells:
        copy.wait()
    pack(27)
    pack(28)
    for i in range(27):
        if i % chunk == 0:
            copies[i // chunk].wait()
        pack(i)
    for side, out in ((0, up), (1, down)):
        for part in range(nz // LANES):
            cols = pl.ds(LANES * part, LANES)
            closed = packed[side, 28, :, cols] > 0.5
            f = [packed[side, i, :, cols] * WEIGHT[i] for i in range(27)]
            relaxed, _ = collide(f, packed[side, 27, :, cols])
            for i in range(27):
                packed[side, i, :, cols] = jnp.where(closed, SOLID, relaxed[i]) * (1.0 / WEIGHT[i]) - 1.0
        both, edge = rows_order(side)
        edge = edge + [27, 28]
        tiles = [packed[side, i, :, :] for i in both]
        for k in range(0, len(edge), 2):
            one, two = (packed[side, i, :, :] for i in edge[k : k + 2])
            at_edge = row % 2 == 1 - side
            tiles.append(jnp.where(at_edge, one, pltpu.roll(two, SUB - 1 if side == 0 else 1, 0)))
        tiles.append(jnp.zeros((SUB, nz), F32))
        for k in range(0, len(tiles), 2):
            out[pl.ds(SUB * k, 2 * SUB), :] = jnp.concatenate(tiles[k : k + 2], axis=0).astype(BF16)


def first_main_kernel(pops, omega, walls, post):
    planes, ny, nz = omega.shape

    def body(plane, carry):
        for t in range(ny // SUB):
            for part in range(nz // LANES):
                at = (plane, pl.ds(SUB * t, SUB), pl.ds(LANES * part, LANES))
                f = [pops[(i, *at)] * WEIGHT[i] for i in range(27)]
                closed = walls[at] == 1
                out, _ = collide(f, 1.0 - omega[at])
                for i in range(27):
                    post[(i, *at)] = jnp.where(closed, SOLID, out[i])
        return carry

    lax.fori_loop(0, planes, body, 0)


def corner_rows(reach):
    places = {}
    for k in range(9):
        sy, j = STEP[k][1], k % 3
        if reach == 2:
            rows = {1: ((6, 6), (7, 7)), 0: ((7, 3), (0, 4)), -1: ((0, 0), (1, 1))}[sy]
            places[k] = [(ring, j, at) for ring, at in rows]
        else:
            places[k] = {1: [(7, 0, j)], 0: [], -1: [(0, 0, 3 + j)]}[sy]
    return places


def face_rows(ny, reach):
    return 9 * ny + (4 if reach == 2 else 2) * SUB


def pack_x(main, halo, plane, first, reach, out):
    ny, nz = main.shape[2:]
    row = lax.broadcasted_iota(jnp.int32, (SUB, nz), 0)
    scaled = lambda ref, k: ref[first + k, plane, :, :] * (1.0 / WEIGHT[k]) - 1.0
    for k in range(9):
        out[pl.ds(ny * k, ny), :] = scaled(main, k).astype(BF16)
    tiles = [jnp.zeros((SUB, nz), F32) for _ in range((out.shape[0] - 9 * ny) // SUB)]
    for k, places in corner_rows(reach).items():
        for ring, tile, at in places:
            turn = (at - ring) % SUB
            value = scaled(halo, k)
            value = pltpu.roll(value, turn, 0) if turn else value
            tiles[tile] = jnp.where(row == at, value, tiles[tile])
    out[pl.ds(9 * ny, SUB * len(tiles)), :] = jnp.concatenate(tiles, axis=0).astype(BF16)


def odd_block():
    return lax.rem(lax.axis_index("gx"), 2)


def pack_faces(main, halo, last, reach, far, near):
    odd = odd_block()
    pack_x(main, halo, odd * last, odd * 18, reach, far)
    pack_x(main, halo, (1 - odd) * last, (1 - odd) * 18, reach, near)


def first_halo_kernel(before, after, main, halo, retain, solid, send_far, send_near, wide_before, wide_after):
    _, planes, _, nz = halo.shape
    row = lax.broadcasted_iota(jnp.int32, (SUB, nz), 0)
    wide_before[...] = before[...].astype(F32)
    wide_after[...] = after[...].astype(F32)

    def received(side, group, plane):
        both, edge = rows_order(side)
        edge = edge + [27, 28]
        turn = (SUB - 2, 0)[side] - 2 * plane
        if group in both:
            tile = both.index(group)
        else:
            k = edge.index(group)
            tile = len(both) + k // 2
            turn += (k % 2) * (1 - 2 * side)
        value = (wide_before, wide_after)[side][pl.ds(SUB * tile, SUB), :]
        return pltpu.roll(value, turn % SUB, 0) if turn % SUB else value

    def beside(group, plane):
        return jnp.where(row < 4, received(1, group, plane), received(0, group, plane))

    for plane in range(planes):
        retain[plane, :, :] = beside(27, plane)
        solid[plane, :, :] = beside(28, plane)
        for i in range(27):
            halo[i, plane, :, :] = (beside(i, plane) + 1.0) * WEIGHT[i]
    pack_faces(main, halo, planes - 1, 2, send_far, send_near)


def turned(value, i):
    _, sy, sz = STEP[i]
    if sy:
        value = pltpu.roll(value, sy % value.shape[0], 0)
    if sz:
        value = pltpu.roll(value, sz % value.shape[1], 1)
    return value


def pull(load, i, plane):
    value = turned(load(i, plane - STEP[i][0]), i)
    return jnp.where(value > LIMIT, load(26 - i, plane), value)


def widen(far, near, wide):
    odd = odd_block()
    wide[odd, :, :] = far[...].astype(F32)
    wide[1 - odd, :, :] = near[...].astype(F32)


def loader(planes, ny, places, wide=None):
    def load(i, plane):
        if 0 <= plane < planes:
            main, halo, at = places[plane]
            return jnp.concatenate([main[i, at, :, :], halo[i, at, :, :]], axis=0)
        side, k = (0, i - 18) if plane < 0 else (1, i)
        reach = 2 if wide.shape[1] == face_rows(ny, 2) else 1
        used = corner_rows(reach)[k]
        if used:
            ring, tile, at = used[0]
            halo = wide[side, pl.ds(9 * ny + SUB * tile, SUB), :]
            halo = pltpu.roll(halo, (ring - at) % SUB, 0) if ring != at else halo
        else:
            halo = jnp.zeros((SUB, wide.shape[2]), F32)
        both = jnp.concatenate([wide[side, pl.ds(ny * k, ny), :], halo], axis=0)
        return (both + 1.0) * WEIGHT[i]

    return load


def middle(mine, load, pops, omega, walls, retain, solid, main2, halo2, macro, read):
    planes, ny, nz = omega.shape
    for at, plane in enumerate(mine):
        own = walls[plane, :, :] == 1
        for i in range(27):
            value = pull(load, i, plane)
            read[i, pl.ds(0, ny), :] = jnp.where(own, pops[i, plane, :, :] * WEIGHT[i], value[:ny])
            read[i, pl.ds(ny, SUB), :] = value[ny:]
        for t in range(ny // SUB + 1):
            for part in range(nz // LANES):
                rows, cols = pl.ds(SUB * t, SUB), pl.ds(LANES * part, LANES)
                inner = SUB * t < ny
                if inner:
                    closed = walls[plane, rows, cols] == 1
                    keep = 1.0 - omega[plane, rows, cols]
                else:
                    closed = solid[plane, :, cols] > 0.5
                    keep = retain[plane, :, cols]
                out, sums = collide([read[i, rows, cols] for i in range(27)], keep)
                for i in range(27):
                    value = jnp.where(closed, SOLID, out[i])
                    if inner:
                        main2[i, at, rows, cols] = value
                    else:
                        halo2[i, at, :, cols] = value
                if inner:
                    macro[0, at, rows, cols] = sums[0] - 1.0
                    for m in range(1, 4):
                        macro[m, at, rows, cols] = sums[m]


def middle_inner_kernel(main, halo, pops, omega, walls, retain, solid, main2, halo2, macro, read):
    planes, ny, _ = omega.shape
    load = loader(planes, ny, [(main, halo, p) for p in range(planes)])
    middle(range(1, planes - 1), load, pops, omega, walls, retain, solid, main2, halo2, macro, read)


def middle_outer_kernel(
    main, halo, pops, omega, walls, retain, solid, far, near, _, __,
    main2, halo2, macro, send_far, send_near, read, wide,
):
    planes, ny, _ = omega.shape
    widen(far, near, wide)
    load = loader(planes, ny, [(main, halo, p) for p in range(planes)], wide)
    middle((0, planes - 1), load, pops, omega, walls, retain, solid, main2, halo2, macro, read)
    pack_faces(main2, halo2, 1, 1, send_far, send_near)


def add_moments(sums, i, f):
    for m, sign in enumerate((1,) + STEP[i]):
        if sign:
            term = f if sign > 0 else -f
            sums[m] = term if sums[m] is None else sums[m] + term


def respond(planes, radiation, pick, fields):
    for p, rows in enumerate(planes):
        ny = rows[0].shape[0]
        for m in range(4):
            fields[m, pl.ds(p * ny, ny), :] = rows[m].astype(BF16)
    parts = []
    for m in range(4):
        total = None
        for h in range(pick.shape[0]):
            term = jnp.dot(pick[h, :, :], fields[m, :, pl.ds(LANES * h, LANES)], preferred_element_type=F32)
            total = term if total is None else total + term
        parts.append(total)
    surface = jnp.concatenate(parts, axis=1).astype(BF16)
    response = jnp.dot(surface, radiation[...], preferred_element_type=F32)
    return response.astype(BF16)


def slots_kernel(bins, radiation, counts, sites, patches, pick, level, turned_radiation):
    halves, slots, lines = pick.shape
    slot = lax.broadcasted_iota(jnp.int32, (slots, lines), 0)
    line = lax.broadcasted_iota(jnp.int32, (slots, lines), 1)
    wanted = jnp.full((slots, lines), -1, jnp.int32)
    for k in range(slots):
        site = jnp.where(k < counts[0, 0], sites[0, 0, k], -halves)
        wanted = jnp.where(slot == k, site, wanted)
    for h in range(halves):
        pick[h, :, :] = (wanted == line * halves + h).astype(BF16)

    n_patch = bins.shape[1]
    slot = lax.broadcasted_iota(jnp.int32, (slots, n_patch), 0)
    named = lax.broadcasted_iota(jnp.int32, (slots, n_patch), 1)
    wanted = jnp.full((slots, n_patch), -1, jnp.int32)
    for k in range(slots):
        wanted = jnp.where(slot == k, patches[0, 0, k], wanted)
    chosen = (wanted == named).astype(BF16)
    per_block = lax.dot_general(
        chosen, bins[...].astype(F32).astype(BF16), (((1,), (1,)), ((), ())), preferred_element_type=F32
    )
    devices, _, width = level.shape
    groups = slots // SUB
    group = lax.broadcasted_iota(jnp.int32, (SUB, width), 1) // (width // groups)
    tiles = {}
    for d in range(devices):
        blk = d * width // OBS_BLK
        if blk not in tiles:
            tile = None
            for g in range(groups):
                column = per_block[SUB * g : SUB * (g + 1), blk : blk + 1]
                column = jnp.broadcast_to(column, (SUB, width))
                tile = column if tile is None else jnp.where(group == g, column, tile)
            tiles[blk] = tile.astype(BF16)
        level[d, :, :] = tiles[blk]

    observers, terms = radiation.shape

    def body(k, carry):
        rows = pl.ds(pl.multiple_of(k * terms, terms), terms)
        turned_radiation[:, rows] = radiation[rows, :].T
        return carry

    lax.fori_loop(0, observers // terms, body, 0)


def last_early_kernel(
    main_in, halo_in, main_out, halo_out, pops, walls, macro_in, macro_out, radiation, pick,
    out, spare, part, inner, send, g_out, fields, sems,
):
    planes, ny, _ = walls.shape
    last = planes - 1
    places = [(main_out, halo_out, 0)]
    places += [(main_in, halo_in, p) for p in range(planes - 2)]
    places += [(main_out, halo_out, 1)]
    load = loader(planes, ny, places)
    copies = []
    for plane in (0, last, *range(1, last)):
        own = walls[plane, :, :] == 1
        edge = {0: 0, last: 1}.get(plane)
        sums = [None] * 4
        for i in range(27):
            if 0 <= plane - STEP[i][0] <= last:
                value = pull(load, i, plane)[:ny]
                g = jnp.where(own, pops[i, plane, :, :], value * (1.0 / WEIGHT[i]))
                g_out[i, plane, :, :] = g
                add_moments(sums, i, g * WEIGHT[i])
            else:
                bounced = load(26 - i, plane)[:ny]
                spare[edge, i % 9, :, :] = jnp.where(own, pops[i, plane, :, :] * WEIGHT[i], bounced)
        for m in range(4):
            if edge is None:
                inner[m, plane - 1, :, :] = sums[m] - 1.0 if m == 0 else sums[m]
            else:
                part[m, edge, :, :] = sums[m]
        span = pl.ds((0, 9)[edge], 18) if edge is not None else pl.ds(0, 27)
        copies += start_all(
            [pltpu.make_async_copy(g_out.at[span, plane], out.at[span, plane], sems.at[len(copies)])]
        )
    rows = [[macro_out[m, 0, :, :] for m in range(4)]]
    rows += [[macro_in[m, p, :, :] for m in range(4)] for p in range(planes - 2)]
    rows += [[macro_out[m, 1, :, :] for m in range(4)]]
    response = respond(rows, radiation, pick, fields)
    devices, _, width = send.shape
    for d in range(devices):
        send[d, :, :] = response[:, d * width : (d + 1) * width]
    for copy in copies:
        copy.wait()


def last_kernel(
    far, near, walls, spare, part, inner, radiation, pick, early, level, started,
    out, send, g_out, fields, wide, sems,
):
    planes, ny, _ = walls.shape
    last = planes - 1
    widen(far, near, wide)
    load = loader(planes, ny, None, wide)
    rows, copies = {}, []
    for edge, (plane, first) in enumerate(((0, 18), (last, 0))):
        own = walls[plane, :, :] == 1
        sums = [part[m, edge, :, :] for m in range(4)]
        for k in range(9):
            i = first + k
            value = turned(load(i, plane - STEP[i][0]), i)[:ny]
            f = jnp.where(own | (value > LIMIT), spare[edge, k, :, :], value)
            g_out[k, edge, :, :] = f * (1.0 / WEIGHT[i])
            add_moments(sums, i, f)
        rows[plane] = [sums[0] - 1.0, *sums[1:]]
        copies += start_all(
            [pltpu.make_async_copy(g_out.at[:, edge], out.at[pl.ds(first, 9), plane], sems.at[edge])]
        )
    for p in range(planes - 2):
        rows[p + 1] = [inner[m, p, :, :] for m in range(4)]
    response = respond([rows[p] for p in range(planes)], radiation, pick, fields)
    devices, _, width = send.shape
    slots = early.shape[1]
    for d in range(devices):
        send[d, pl.ds(0, slots), :] = early[d, :, :]
        send[d, pl.ds(slots, slots), :] = response[:, d * width : (d + 1) * width]
        send[d, pl.ds(2 * slots, SUB), :] = level[d, :, :]
    for copy in copies:
        copy.wait()


def bin_kernel(received, signal, hits):
    devices, rows, width = received.shape
    slots = (rows - SUB) // 2
    groups = slots // SUB
    lane = lax.broadcasted_iota(jnp.int32, (slots, LEVELS), 1).astype(F32)
    for d in range(devices):
        tile = received[d, pl.ds(2 * slots, SUB), :].astype(F32)
        starts = [g * (width // groups) for g in range(groups)]
        level = jnp.concatenate([jnp.broadcast_to(tile[:, k : k + 1], (SUB, LEVELS)) for k in starts], axis=0)
        for step in range(2):
            hit = (level == lane - float(step)).astype(F32).astype(BF16)
            hits[d, pl.ds(step * slots, slots), :] = hit
    left = received[:, pl.ds(0, 2 * slots), :].reshape(devices * 2 * slots, width)
    right = hits[...].reshape(devices * 2 * slots, LEVELS)
    signal[...] = lax.dot_general(left, right, (((0,), (0,)), ((), ())), preferred_element_type=F32)


def per_device(populations, omega, walls, radiation, bins, counts, sample_site, sample_patch):
    _, planes, ny, nz = populations.shape
    slots = sample_site.shape[-1]
    size_x, size_y = lax.axis_size("gx"), lax.axis_size("gy")
    devices = size_x * size_y
    width = radiation.shape[0] // devices

    def exchange(up, down):
        right = [(i, (i + 1) % size_y) for i in range(size_y)]
        left = [(j, i) for i, j in right]
        return lax.ppermute(up, "gy", right), lax.ppermute(down, "gy", left)

    def swap(far, near):
        far_pairs = [(i, (i - 1 + 2 * (i % 2)) % size_x) for i in range(size_x)]
        near_pairs = [(i, i + 1 - 2 * (i % 2)) for i in range(size_x)]
        return lax.ppermute(far, "gx", far_pairs), lax.ppermute(near, "gx", near_pairs)

    dma = pltpu.SemaphoreType.DMA
    block, cells = populations.shape, (planes, ny, nz)
    beside = (20 * SUB, nz)
    up, down = call(
        rows_kernel,
        [HBM] * 3,
        [(VMEM, beside, BF16)] * 2,
        [
            pltpu.VMEM(block, F32), pltpu.VMEM(cells, F32), pltpu.VMEM(cells, walls.dtype),
            pltpu.VMEM((2, 29, SUB, nz), F32), dma((9,)),
        ],
        cost=1 << 20,
        limit=64800000,
    )(populations, omega, walls)
    before, after = exchange(up, down)
    pick, level, radiation = call(
        slots_kernel,
        [VMEM] * 2 + [SMEM] * 3,
        [
            (VMEM, (nz // LANES, slots, planes * ny), BF16),
            (VMEM, (devices, SUB, width), BF16),
            (VMEM, radiation.shape[::-1], BF16),
        ],
        cost=1 << 22,
    )(bins.T, radiation, counts, sample_site, sample_patch)
    (main,) = call(first_main_kernel, [VMEM] * 3, [(VMEM, block, F32)], cost=1 << 22)(populations, omega, walls)

    edge = (planes, SUB, nz)
    face, last_face = ((face_rows(ny, reach), nz) for reach in (2, 1))
    faces, last_faces = ([(VMEM, shape, BF16)] * 2 for shape in (face, last_face))
    halo, retain, solid, far, near = call(
        first_halo_kernel,
        [VMEM] * 3,
        [(VMEM, (27, *edge), F32), (VMEM, edge, F32), (VMEM, edge, F32), *faces],
        [pltpu.VMEM(beside, F32)] * 2,
        cost=1 << 20,
    )(before, after, main)
    far, near = swap(far, near)

    def relaxed(n):
        return [(VMEM, (27, n, ny, nz), F32), (VMEM, (27, n, SUB, nz), F32), (VMEM, (4, n, ny, nz), F32)]

    read = pltpu.VMEM((27, ny + SUB, nz), F32)
    wide, last_wide = (pltpu.VMEM((2, *shape), F32) for shape in (face, last_face))
    args = (main, halo, populations, omega, walls, retain, solid)
    main_in, halo_in, macro_in = call(
        middle_inner_kernel, [VMEM] * 7, relaxed(planes - 2), [read], cost=1 << 22
    )(*args)
    main_out, halo_out, macro_out, far, near = call(
        middle_outer_kernel, [VMEM] * 11, relaxed(2) + last_faces, [read, wide], cost=1 << 22
    )(*args, far, near, macro_in, pick)
    far, near = swap(far, near)

    fields = pltpu.VMEM((4, planes * ny, nz), BF16)
    inner = (4, planes - 2, ny, nz)
    started, spare, part, inner, early = call(
        last_early_kernel,
        [VMEM] * 10,
        [
            (HBM, block, F32),
            (VMEM, (2, 9, ny, nz), F32),
            (VMEM, (4, 2, ny, nz), F32),
            (VMEM, inner, F32),
            (VMEM, (devices, slots, width), BF16),
        ],
        [pltpu.VMEM(block, F32), fields, dma((planes,))],
        cost=1 << 22,
    )(main_in, halo_in, main_out, halo_out, populations, walls, macro_in, macro_out, radiation, pick)
    advanced, send = call(
        last_kernel,
        [VMEM] * 10 + [HBM],
        [(HBM, block, F32), (VMEM, (devices, 2 * slots + SUB, width), BF16)],
        [pltpu.VMEM((9, 2, ny, nz), F32), fields, last_wide, dma((2,))],
        aliases={10: 0},
        cost=1 << 22,
    )(far, near, walls, spare, part, inner, radiation, pick, early, level, started)
    received = lax.all_to_all(send, ("gx", "gy"), 0, 0, tiled=True)
    (signal,) = call(
        bin_kernel, [VMEM], [(VMEM, (width, LEVELS), F32)], [pltpu.VMEM((devices, 2 * slots, LEVELS), BF16)], cost=1 << 20
    )(received)
    return advanced, signal


def solution(mesh):
    return jax.shard_map(
        per_device,
        mesh=mesh,
        in_specs=(
            P(None, "gx", "gy", None),
            P("gx", "gy", None),
            P("gx", "gy", None),
            P(),
            P(),
            P("gx", "gy"),
            P("gx", "gy", None),
            P("gx", "gy", None),
        ),
        out_specs=(P(None, "gx", "gy", None), P(("gx", "gy"), None)),
        check_vma=False,
    )
```

```python
import jax
import jax.numpy as jnp
from jax import lax
from jax.experimental import pallas as pl
from jax.experimental.pallas import tpu as pltpu
from jax.sharding import PartitionSpec as P

F32 = jnp.float32
BF16 = jnp.bfloat16
LEVELS = 128
OBS_BLK = 128
SOLID = 1e30
LIMIT = 1e29
LANES = 128
SUB = 8

WEIGHT = [
    (8.0 / 27.0, 2.0 / 27.0, 1.0 / 54.0, 1.0 / 216.0)[
        int(i // 9 != 1) + int(i // 3 % 3 != 1) + int(i % 3 != 1)
    ]
    for i in range(27)
]
STEP = [(i // 9 - 1, i // 3 % 3 - 1, i % 3 - 1) for i in range(27)]
VMEM = pl.BlockSpec(memory_space=pltpu.VMEM)
SMEM = pl.BlockSpec(memory_space=pltpu.SMEM)
HBM = pl.BlockSpec(memory_space=pltpu.HBM)


def call(kernel, in_specs, out, scratch=(), aliases=None, cost=0, limit=14 * 1024 * 1024):
    return pl.pallas_call(
        kernel,
        out_shape=[jax.ShapeDtypeStruct(shape, dtype) for _, shape, dtype in out],
        in_specs=in_specs,
        out_specs=[spec for spec, _, _ in out],
        scratch_shapes=list(scratch),
        input_output_aliases=aliases or {},
        compiler_params=pltpu.CompilerParams(vmem_limit_bytes=limit),
        cost_estimate=pl.CostEstimate(flops=cost, bytes_accessed=cost, transcendentals=0),
    )


def raw_moments(f):
    s, d, e = [], [], []
    for k in range(9):
        low, mid, high = f[3 * k : 3 * k + 3]
        ends = high + low
        s.append(ends + mid)
        d.append(high - low)
        e.append(ends)
    s_y, dy, ey, dz, dyz, ez = [], [], [], [], [], []
    for a in range(3):
        ends = s[3 * a + 2] + s[3 * a]
        s_y.append(ends + s[3 * a + 1])
        dy.append(s[3 * a + 2] - s[3 * a])
        ey.append(ends)
        dz.append(d[3 * a] + d[3 * a + 1] + d[3 * a + 2])
        dyz.append(d[3 * a + 2] - d[3 * a])
        ez.append(e[3 * a] + e[3 * a + 1] + e[3 * a + 2])
    m200 = s_y[2] + s_y[0]
    rho = m200 + s_y[1]
    jx = s_y[2] - s_y[0]
    jy = dy[0] + dy[1] + dy[2]
    jz = dz[0] + dz[1] + dz[2]
    m020 = ey[0] + ey[1] + ey[2]
    m002 = ez[0] + ez[1] + ez[2]
    m110 = dy[2] - dy[0]
    m101 = dz[2] - dz[0]
    m011 = dyz[0] + dyz[1] + dyz[2]
    return rho, jx, jy, jz, m200, m020, m002, m110, m101, m011


def unshift(k0, k1, k2, v, v2, vv, vp, vm):
    if k0 is None and k2 is None:
        return vm * k1, -(v2 * k1), vp * k1
    diff = v * k0
    ends = vv * k0
    if k1 is not None:
        diff = diff + k1
        ends = ends + v2 * k1
    if k2 is not None:
        ends = ends + k2
    high = 0.5 * (ends + diff)
    return high - diff, k0 - ends, high


def collide(f, retain):
    rho, jx, jy, jz, m200, m020, m002, m110, m101, m011 = raw_moments(f)
    inv = 1.0 / rho
    ux, uy, uz = jx * inv, jy * inv, jz * inv
    k200, k020, k002 = m200 - jx * ux, m020 - jy * uy, m002 - jz * uz
    third = 1.0 / 3.0
    d1 = retain * (k200 - k020)
    d2 = retain * (k200 - k002)
    xx = (rho + d1 + d2) * third
    yy = xx - d1
    zz = xx - d2
    xy = retain * (m110 - jx * uy)
    xz = retain * (m101 - jx * uz)
    yz = retain * (m011 - jy * uz)
    xy2, xz2, yz2 = 2.0 * xy, 2.0 * xz, 2.0 * yz
    xyi, xzi, yzi = xy2 * inv, xz2 * inv, yz2 * inv
    xxi = xx * inv
    yyi = yy * inv
    q_xy, q_xz, q_yz = xy * xyi, xz * xzi, yz * yzi
    xxyy = xxi * yy + q_xy
    xxzz = xxi * zz + q_xz
    yyzz = yyi * zz + q_yz
    xxyz = xxi * yz + xy * xzi
    xyyz = yyi * xz + xy * yzi
    xyzz = (zz * inv) * xy + xz * yzi
    full = xxi * (yyi * zz + q_yz) + (yyi * q_xz + (zz * inv) * q_xy) + (2.0 * xyi) * (xz * yzi)
    table = {
        (0, 0): (rho, None, xx),
        (1, 0): (None, xy, None),
        (2, 0): (yy, None, xxyy),
        (0, 1): (None, xz, None),
        (1, 1): (yz, None, xxyz),
        (2, 1): (None, xyyz, None),
        (0, 2): (zz, None, xxzz),
        (1, 2): (None, xyzz, None),
        (2, 2): (yyzz, None, full),
    }

    def speeds(v):
        return v, 2.0 * v, v * v, v + 0.5, v - 0.5

    sx, sy, sz = speeds(ux), speeds(uy), speeds(uz)
    after_x = {}
    for (b, c), ks in table.items():
        for a, value in enumerate(unshift(*ks, *sx)):
            after_x[a, b, c] = value
    out = [None] * 27
    for a in range(3):
        after_y = {}
        for c in range(3):
            triple = unshift(*(after_x[a, b, c] for b in range(3)), *sy)
            for b, value in enumerate(triple):
                after_y[b, c] = value
        for b in range(3):
            triple = unshift(*(after_y[b, c] for c in range(3)), *sz)
            for c, value in enumerate(triple):
                out[9 * a + 3 * b + c] = value
    return out, (rho, jx, jy, jz)


def odd_block(axis):
    return lax.rem(lax.axis_index(axis), 2)


def widen(far, near, wide, axis):
    odd = odd_block(axis)
    wide[odd, :, :] = far[...].astype(F32)
    wide[1 - odd, :, :] = near[...].astype(F32)


def start_all(copies):
    for copy in copies:
        copy.start()
    return copies


def rows_order(side):
    outward = 1 - 2 * side
    both = [i for i in range(27) if STEP[i][1] == outward]
    return both, [i for i in range(27) if STEP[i][1] != outward]


def rows_kernel(pops_in, omega_in, walls_in, far, near, pops, omega, walls, packed, faces, sems):
    planes, ny, nz = omega.shape
    row = lax.broadcasted_iota(jnp.int32, (SUB, nz), 0)
    chunk = 4
    spans = [pl.ds(i, min(chunk, 27 - i)) for i in range(0, 27, chunk)]
    cells = [
        pltpu.make_async_copy(omega_in, omega, sems.at[len(spans)]),
        pltpu.make_async_copy(walls_in, walls, sems.at[len(spans) + 1]),
    ]
    copies = [pltpu.make_async_copy(pops_in.at[span], pops.at[span], sems.at[k]) for k, span in enumerate(spans)]
    start_all(cells + copies)

    def read(group, plane, first):
        part = pl.ds(first, SUB)
        if group < 27:
            return pops[group, plane, part, :]
        if group == 27:
            return 1.0 - omega[plane, part, :]
        return walls[plane, part, :].astype(F32)

    def pack(group):
        for side, first, at in ((0, ny - SUB, SUB - 2), (1, 0, 0)):
            tile = None
            for plane in range(planes):
                turn = (2 * plane - at) % SUB
                piece = read(group, plane, first)
                piece = pltpu.roll(piece, turn, 0) if turn else piece
                tile = piece if tile is None else jnp.where(row // 2 == plane, piece, tile)
            packed[side, group, :, :] = tile

    for copy in cells:
        copy.wait()
    pack(27)
    pack(28)
    for i in range(27):
        if i % chunk == 0:
            copies[i // chunk].wait()
        pack(i)
    for side in range(2):
        for part in range(nz // LANES):
            cols = pl.ds(LANES * part, LANES)
            closed = packed[side, 28, :, cols] > 0.5
            f = [packed[side, i, :, cols] * WEIGHT[i] for i in range(27)]
            relaxed, _ = collide(f, packed[side, 27, :, cols])
            for i in range(27):
                packed[side, i, :, cols] = jnp.where(closed, SOLID, relaxed[i]) * (1.0 / WEIGHT[i]) - 1.0
        both, edge = rows_order(side)
        edge = edge + [27, 28]
        tiles = [packed[side, i, :, :] for i in both]
        for k in range(0, len(edge), 2):
            one, two = (packed[side, i, :, :] for i in edge[k : k + 2])
            at_edge = row % 2 == 1 - side
            tiles.append(jnp.where(at_edge, one, pltpu.roll(two, SUB - 1 if side == 0 else 1, 0)))
        tiles.append(jnp.zeros((SUB, nz), F32))
        for k, tile in enumerate(tiles):
            faces[side, pl.ds(SUB * k, SUB), :] = tile
    odd = odd_block("gy")
    far[...] = faces[1 - odd, :, :].astype(BF16)
    near[...] = faces[odd, :, :].astype(BF16)


def first_main_kernel(pops, omega, walls, post):
    planes, ny, nz = omega.shape

    def body(plane, carry):
        for t in range(ny // SUB):
            for part in range(nz // LANES):
                at = (plane, pl.ds(SUB * t, SUB), pl.ds(LANES * part, LANES))
                f = [pops[(i, *at)] * WEIGHT[i] for i in range(27)]
                closed = walls[at] == 1
                out, _ = collide(f, 1.0 - omega[at])
                for i in range(27):
                    post[(i, *at)] = jnp.where(closed, SOLID, out[i])
        return carry

    lax.fori_loop(0, planes, body, 0)


def corner_rows(reach):
    places = {}
    for k in range(9):
        sy, j = STEP[k][1], k % 3
        if reach == 2:
            rows = {1: ((6, 6), (7, 7)), 0: ((7, 3), (0, 4)), -1: ((0, 0), (1, 1))}[sy]
            places[k] = [(ring, j, at) for ring, at in rows]
        else:
            places[k] = {1: [(7, 0, j)], 0: [], -1: [(0, 0, 3 + j)]}[sy]
    return places


def face_rows(ny, reach):
    return 9 * ny + (4 if reach == 2 else 2) * SUB


def pack_x(main, halo, plane, first, reach, out):
    ny, nz = main.shape[2:]
    row = lax.broadcasted_iota(jnp.int32, (SUB, nz), 0)
    scaled = lambda ref, k: ref[first + k, plane, :, :] * (1.0 / WEIGHT[k]) - 1.0
    for k in range(9):
        out[pl.ds(ny * k, ny), :] = scaled(main, k).astype(BF16)
    tiles = [jnp.zeros((SUB, nz), F32) for _ in range((out.shape[0] - 9 * ny) // SUB)]
    for k, places in corner_rows(reach).items():
        for ring, tile, at in places:
            turn = (at - ring) % SUB
            value = scaled(halo, k)
            value = pltpu.roll(value, turn, 0) if turn else value
            tiles[tile] = jnp.where(row == at, value, tiles[tile])
    out[pl.ds(9 * ny, SUB * len(tiles)), :] = jnp.concatenate(tiles, axis=0).astype(BF16)


def pack_faces(main, halo, last, reach, far, near):
    odd = odd_block("gx")
    pack_x(main, halo, odd * last, odd * 18, reach, far)
    pack_x(main, halo, (1 - odd) * last, (1 - odd) * 18, reach, near)


def first_halo_kernel(far, near, main, halo, retain, solid, send_far, send_near, wide):
    _, planes, _, nz = halo.shape
    row = lax.broadcasted_iota(jnp.int32, (SUB, nz), 0)
    widen(far, near, wide, "gy")

    def received(side, group, plane):
        both, edge = rows_order(side)
        edge = edge + [27, 28]
        turn = (SUB - 2, 0)[side] - 2 * plane
        if group in both:
            tile = both.index(group)
        else:
            k = edge.index(group)
            tile = len(both) + k // 2
            turn += (k % 2) * (1 - 2 * side)
        value = wide[side, pl.ds(SUB * tile, SUB), :]
        return pltpu.roll(value, turn % SUB, 0) if turn % SUB else value

    def beside(group, plane):
        return jnp.where(row < 4, received(1, group, plane), received(0, group, plane))

    for plane in range(planes):
        retain[plane, :, :] = beside(27, plane)
        solid[plane, :, :] = beside(28, plane)
        for i in range(27):
            halo[i, plane, :, :] = (beside(i, plane) + 1.0) * WEIGHT[i]
    pack_faces(main, halo, planes - 1, 2, send_far, send_near)


def turned(value, i):
    _, sy, sz = STEP[i]
    if sy:
        value = pltpu.roll(value, sy % value.shape[0], 0)
    if sz:
        value = pltpu.roll(value, sz % value.shape[1], 1)
    return value


def pull(load, i, plane):
    value = turned(load(i, plane - STEP[i][0]), i)
    return jnp.where(value > LIMIT, load(26 - i, plane), value)


def loader(planes, ny, places, wide=None):
    def load(i, plane):
        if 0 <= plane < planes:
            main, halo, at = places[plane]
            return jnp.concatenate([main[i, at, :, :], halo[i, at, :, :]], axis=0)
        side, k = (0, i - 18) if plane < 0 else (1, i)
        reach = 2 if wide.shape[1] == face_rows(ny, 2) else 1
        used = corner_rows(reach)[k]
        if used:
            ring, tile, at = used[0]
            halo = wide[side, pl.ds(9 * ny + SUB * tile, SUB), :]
            halo = pltpu.roll(halo, (ring - at) % SUB, 0) if ring != at else halo
        else:
            halo = jnp.zeros((SUB, wide.shape[2]), F32)
        both = jnp.concatenate([wide[side, pl.ds(ny * k, ny), :], halo], axis=0)
        return (both + 1.0) * WEIGHT[i]

    return load


def middle(mine, load, pops, omega, walls, retain, solid, main2, halo2, macro, read):
    planes, ny, nz = omega.shape
    for at, plane in enumerate(mine):
        own = walls[plane, :, :] == 1
        for i in range(27):
            value = pull(load, i, plane)
            read[i, pl.ds(0, ny), :] = jnp.where(own, pops[i, plane, :, :] * WEIGHT[i], value[:ny])
            read[i, pl.ds(ny, SUB), :] = value[ny:]
        for t in range(ny // SUB + 1):
            for part in range(nz // LANES):
                rows, cols = pl.ds(SUB * t, SUB), pl.ds(LANES * part, LANES)
                inner = SUB * t < ny
                if inner:
                    closed = walls[plane, rows, cols] == 1
                    keep = 1.0 - omega[plane, rows, cols]
                else:
                    closed = solid[plane, :, cols] > 0.5
                    keep = retain[plane, :, cols]
                out, sums = collide([read[i, rows, cols] for i in range(27)], keep)
                for i in range(27):
                    value = jnp.where(closed, SOLID, out[i])
                    if inner:
                        main2[i, at, rows, cols] = value
                    else:
                        halo2[i, at, :, cols] = value
                if inner:
                    macro[0, at, rows, cols] = sums[0] - 1.0
                    for m in range(1, 4):
                        macro[m, at, rows, cols] = sums[m]


def middle_inner_kernel(main, halo, pops, omega, walls, retain, solid, main2, halo2, macro, read):
    planes, ny, _ = omega.shape
    load = loader(planes, ny, [(main, halo, p) for p in range(planes)])
    middle(range(1, planes - 1), load, pops, omega, walls, retain, solid, main2, halo2, macro, read)


def middle_outer_kernel(
    main, halo, pops, omega, walls, retain, solid, far, near, _, __,
    main2, halo2, macro, send_far, send_near, read, wide,
):
    planes, ny, _ = omega.shape
    widen(far, near, wide, "gx")
    load = loader(planes, ny, [(main, halo, p) for p in range(planes)], wide)
    middle((0, planes - 1), load, pops, omega, walls, retain, solid, main2, halo2, macro, read)
    pack_faces(main2, halo2, 1, 1, send_far, send_near)


def add_moments(sums, i, f):
    for m, sign in enumerate((1,) + STEP[i]):
        if sign:
            term = f if sign > 0 else -f
            sums[m] = term if sums[m] is None else sums[m] + term


def respond(planes, radiation, pick, fields):
    for p, rows in enumerate(planes):
        ny = rows[0].shape[0]
        for m in range(4):
            fields[m, pl.ds(p * ny, ny), :] = rows[m].astype(BF16)
    parts = []
    for m in range(4):
        total = None
        for h in range(pick.shape[0]):
            term = jnp.dot(pick[h, :, :], fields[m, :, pl.ds(LANES * h, LANES)], preferred_element_type=F32)
            total = term if total is None else total + term
        parts.append(total)
    surface = jnp.concatenate(parts, axis=1).astype(BF16)
    response = jnp.dot(surface, radiation[...], preferred_element_type=F32)
    return response.astype(BF16)


def slots_kernel(bins, radiation, counts, sites, patches, pick, level, turned_radiation):
    halves, slots, lines = pick.shape
    slot = lax.broadcasted_iota(jnp.int32, (slots, lines), 0)
    line = lax.broadcasted_iota(jnp.int32, (slots, lines), 1)
    wanted = jnp.full((slots, lines), -1, jnp.int32)
    for k in range(slots):
        site = jnp.where(k < counts[0, 0], sites[0, 0, k], -halves)
        wanted = jnp.where(slot == k, site, wanted)
    for h in range(halves):
        pick[h, :, :] = (wanted == line * halves + h).astype(BF16)

    n_patch = bins.shape[1]
    slot = lax.broadcasted_iota(jnp.int32, (slots, n_patch), 0)
    named = lax.broadcasted_iota(jnp.int32, (slots, n_patch), 1)
    wanted = jnp.full((slots, n_patch), -1, jnp.int32)
    for k in range(slots):
        wanted = jnp.where(slot == k, patches[0, 0, k], wanted)
    chosen = (wanted == named).astype(BF16)
    per_block = lax.dot_general(
        chosen, bins[...].astype(F32).astype(BF16), (((1,), (1,)), ((), ())), preferred_element_type=F32
    )
    devices, _, width = level.shape
    groups = slots // SUB
    group = lax.broadcasted_iota(jnp.int32, (SUB, width), 1) // (width // groups)
    tiles = {}
    for d in range(devices):
        blk = d * width // OBS_BLK
        if blk not in tiles:
            tile = None
            for g in range(groups):
                column = per_block[SUB * g : SUB * (g + 1), blk : blk + 1]
                column = jnp.broadcast_to(column, (SUB, width))
                tile = column if tile is None else jnp.where(group == g, column, tile)
            tiles[blk] = tile.astype(BF16)
        level[d, :, :] = tiles[blk]

    observers, terms = radiation.shape

    def body(k, carry):
        rows = pl.ds(pl.multiple_of(k * terms, terms), terms)
        turned_radiation[:, rows] = radiation[rows, :].T
        return carry

    lax.fori_loop(0, observers // terms, body, 0)


def last_early_kernel(
    main_in, halo_in, main_out, halo_out, pops, walls, macro_in, macro_out, radiation, pick,
    out, spare, part, inner, send, g_out, fields, sems,
):
    planes, ny, _ = walls.shape
    last = planes - 1
    places = [(main_out, halo_out, 0)]
    places += [(main_in, halo_in, p) for p in range(planes - 2)]
    places += [(main_out, halo_out, 1)]
    load = loader(planes, ny, places)
    copies = []
    for plane in (0, last, *range(1, last)):
        own = walls[plane, :, :] == 1
        edge = {0: 0, last: 1}.get(plane)
        sums = [None] * 4
        for i in range(27):
            if 0 <= plane - STEP[i][0] <= last:
                value = pull(load, i, plane)[:ny]
                g = jnp.where(own, pops[i, plane, :, :], value * (1.0 / WEIGHT[i]))
                g_out[i, plane, :, :] = g
                add_moments(sums, i, g * WEIGHT[i])
            else:
                bounced = load(26 - i, plane)[:ny]
                spare[edge, i % 9, :, :] = jnp.where(own, pops[i, plane, :, :] * WEIGHT[i], bounced)
        for m in range(4):
            if edge is None:
                inner[m, plane - 1, :, :] = sums[m] - 1.0 if m == 0 else sums[m]
            else:
                part[m, edge, :, :] = sums[m]
        span = pl.ds((0, 9)[edge], 18) if edge is not None else pl.ds(0, 27)
        copies += start_all(
            [pltpu.make_async_copy(g_out.at[span, plane], out.at[span, plane], sems.at[len(copies)])]
        )
    rows = [[macro_out[m, 0, :, :] for m in range(4)]]
    rows += [[macro_in[m, p, :, :] for m in range(4)] for p in range(planes - 2)]
    rows += [[macro_out[m, 1, :, :] for m in range(4)]]
    response = respond(rows, radiation, pick, fields)
    devices, _, width = send.shape
    for d in range(devices):
        send[d, :, :] = response[:, d * width : (d + 1) * width]
    for copy in copies:
        copy.wait()


def last_kernel(
    far, near, walls, spare, part, inner, radiation, pick, early, level, started,
    out, send, g_out, fields, wide, sems,
):
    planes, ny, _ = walls.shape
    last = planes - 1
    widen(far, near, wide, "gx")
    load = loader(planes, ny, None, wide)
    rows, copies = {}, []
    for edge, (plane, first) in enumerate(((0, 18), (last, 0))):
        own = walls[plane, :, :] == 1
        sums = [part[m, edge, :, :] for m in range(4)]
        for k in range(9):
            i = first + k
            value = turned(load(i, plane - STEP[i][0]), i)[:ny]
            f = jnp.where(own | (value > LIMIT), spare[edge, k, :, :], value)
            g_out[k, edge, :, :] = f * (1.0 / WEIGHT[i])
            add_moments(sums, i, f)
        rows[plane] = [sums[0] - 1.0, *sums[1:]]
        copies += start_all(
            [pltpu.make_async_copy(g_out.at[:, edge], out.at[pl.ds(first, 9), plane], sems.at[edge])]
        )
    for p in range(planes - 2):
        rows[p + 1] = [inner[m, p, :, :] for m in range(4)]
    response = respond([rows[p] for p in range(planes)], radiation, pick, fields)
    devices, _, width = send.shape
    slots = early.shape[1]
    for d in range(devices):
        send[d, pl.ds(0, slots), :] = early[d, :, :]
        send[d, pl.ds(slots, slots), :] = response[:, d * width : (d + 1) * width]
        send[d, pl.ds(2 * slots, SUB), :] = level[d, :, :]
    for copy in copies:
        copy.wait()


def bin_kernel(received, signal, hits):
    devices, rows, width = received.shape
    slots = (rows - SUB) // 2
    groups = slots // SUB
    lane = lax.broadcasted_iota(jnp.int32, (slots, LEVELS), 1).astype(F32)
    for d in range(devices):
        tile = received[d, pl.ds(2 * slots, SUB), :].astype(F32)
        starts = [g * (width // groups) for g in range(groups)]
        level = jnp.concatenate([jnp.broadcast_to(tile[:, k : k + 1], (SUB, LEVELS)) for k in starts], axis=0)
        for step in range(2):
            hit = (level == lane - float(step)).astype(F32).astype(BF16)
            hits[d, pl.ds(step * slots, slots), :] = hit
    left = received[:, pl.ds(0, 2 * slots), :].reshape(devices * 2 * slots, width)
    right = hits[...].reshape(devices * 2 * slots, LEVELS)
    signal[...] = lax.dot_general(left, right, (((0,), (0,)), ((), ())), preferred_element_type=F32)


def per_device(populations, omega, walls, radiation, bins, counts, sample_site, sample_patch):
    _, planes, ny, nz = populations.shape
    slots = sample_site.shape[-1]
    size_x, size_y = lax.axis_size("gx"), lax.axis_size("gy")
    devices = size_x * size_y
    width = radiation.shape[0] // devices

    def swap(far, near, axis, size):
        far_pairs = [(i, (i - 1 + 2 * (i % 2)) % size) for i in range(size)]
        near_pairs = [(i, i + 1 - 2 * (i % 2)) for i in range(size)]
        return lax.ppermute(far, axis, far_pairs), lax.ppermute(near, axis, near_pairs)

    dma = pltpu.SemaphoreType.DMA
    block, cells = populations.shape, (planes, ny, nz)
    beside = (20 * SUB, nz)
    far, near = call(
        rows_kernel,
        [HBM] * 3,
        [(VMEM, beside, BF16)] * 2,
        [
            pltpu.VMEM(block, F32), pltpu.VMEM(cells, F32), pltpu.VMEM(cells, walls.dtype),
            pltpu.VMEM((2, 29, SUB, nz), F32), pltpu.VMEM((2, *beside), F32), dma((9,)),
        ],
        cost=1 << 20,
        limit=64800000,
    )(populations, omega, walls)
    far, near = swap(far, near, "gy", size_y)
    pick, level, radiation = call(
        slots_kernel,
        [VMEM] * 2 + [SMEM] * 3,
        [
            (VMEM, (nz // LANES, slots, planes * ny), BF16),
            (VMEM, (devices, SUB, width), BF16),
            (VMEM, radiation.shape[::-1], BF16),
        ],
        cost=1 << 22,
    )(bins.T, radiation, counts, sample_site, sample_patch)
    (main,) = call(first_main_kernel, [VMEM] * 3, [(VMEM, block, F32)], cost=1 << 22)(populations, omega, walls)

    edge = (planes, SUB, nz)
    face, last_face = ((face_rows(ny, reach), nz) for reach in (2, 1))
    faces, last_faces = ([(VMEM, shape, BF16)] * 2 for shape in (face, last_face))
    halo, retain, solid, far, near = call(
        first_halo_kernel,
        [VMEM] * 3,
        [(VMEM, (27, *edge), F32), (VMEM, edge, F32), (VMEM, edge, F32), *faces],
        [pltpu.VMEM((2, *beside), F32)],
        cost=1 << 20,
    )(far, near, main)
    far, near = swap(far, near, "gx", size_x)

    def relaxed(n):
        return [(VMEM, (27, n, ny, nz), F32), (VMEM, (27, n, SUB, nz), F32), (VMEM, (4, n, ny, nz), F32)]

    read = pltpu.VMEM((27, ny + SUB, nz), F32)
    wide, last_wide = (pltpu.VMEM((2, *shape), F32) for shape in (face, last_face))
    args = (main, halo, populations, omega, walls, retain, solid)
    main_in, halo_in, macro_in = call(
        middle_inner_kernel, [VMEM] * 7, relaxed(planes - 2), [read], cost=1 << 22
    )(*args)
    main_out, halo_out, macro_out, far, near = call(
        middle_outer_kernel, [VMEM] * 11, relaxed(2) + last_faces, [read, wide], cost=1 << 22
    )(*args, far, near, macro_in, pick)
    far, near = swap(far, near, "gx", size_x)

    fields = pltpu.VMEM((4, planes * ny, nz), BF16)
    inner = (4, planes - 2, ny, nz)
    started, spare, part, inner, early = call(
        last_early_kernel,
        [VMEM] * 10,
        [
            (HBM, block, F32),
            (VMEM, (2, 9, ny, nz), F32),
            (VMEM, (4, 2, ny, nz), F32),
            (VMEM, inner, F32),
            (VMEM, (devices, slots, width), BF16),
        ],
        [pltpu.VMEM(block, F32), fields, dma((planes,))],
        cost=1 << 22,
    )(main_in, halo_in, main_out, halo_out, populations, walls, macro_in, macro_out, radiation, pick)
    advanced, send = call(
        last_kernel,
        [VMEM] * 10 + [HBM],
        [(HBM, block, F32), (VMEM, (devices, 2 * slots + SUB, width), BF16)],
        [pltpu.VMEM((9, 2, ny, nz), F32), fields, last_wide, dma((2,))],
        aliases={10: 0},
        cost=1 << 22,
    )(far, near, walls, spare, part, inner, radiation, pick, early, level, started)
    received = lax.all_to_all(send, ("gx", "gy"), 0, 0, tiled=True)
    (signal,) = call(
        bin_kernel, [VMEM], [(VMEM, (width, LEVELS), F32)], [pltpu.VMEM((devices, 2 * slots, LEVELS), BF16)], cost=1 << 20
    )(received)
    return advanced, signal


def solution(mesh):
    return jax.shard_map(
        per_device,
        mesh=mesh,
        in_specs=(
            P(None, "gx", "gy", None),
            P("gx", "gy", None),
            P("gx", "gy", None),
            P(),
            P(),
            P("gx", "gy"),
            P("gx", "gy", None),
            P("gx", "gy", None),
        ),
        out_specs=(P(None, "gx", "gy", None), P(("gx", "gy"), None)),
        check_vma=False,
    )
```

```python
import functools

import jax
import jax.numpy as jnp
from jax import lax
from jax.experimental import pallas as pl
from jax.experimental.pallas import tpu as pltpu
from jax.sharding import PartitionSpec as P

F32 = jnp.float32
BF16 = jnp.bfloat16
LEVELS = 128
OBS_BLK = 128
SOLID = 1e30
LIMIT = 1e29
LANES = 128
SUB = 8

WEIGHT = [
    (8.0 / 27.0, 2.0 / 27.0, 1.0 / 54.0, 1.0 / 216.0)[
        int(i // 9 != 1) + int(i // 3 % 3 != 1) + int(i % 3 != 1)
    ]
    for i in range(27)
]
STEP = [(i // 9 - 1, i // 3 % 3 - 1, i % 3 - 1) for i in range(27)]
VMEM = pl.BlockSpec(memory_space=pltpu.VMEM)
SMEM = pl.BlockSpec(memory_space=pltpu.SMEM)
HBM = pl.BlockSpec(memory_space=pltpu.HBM)


def call(kernel, in_specs, out, scratch=(), aliases=None, cost=0, limit=14 * 1024 * 1024):
    return pl.pallas_call(
        kernel,
        out_shape=[jax.ShapeDtypeStruct(shape, dtype) for _, shape, dtype in out],
        in_specs=in_specs,
        out_specs=[spec for spec, _, _ in out],
        scratch_shapes=list(scratch),
        input_output_aliases=aliases or {},
        compiler_params=pltpu.CompilerParams(vmem_limit_bytes=limit),
        cost_estimate=pl.CostEstimate(flops=cost, bytes_accessed=cost, transcendentals=0),
    )


def raw_moments(f):
    s, d, e = [], [], []
    for k in range(9):
        low, mid, high = f[3 * k : 3 * k + 3]
        ends = high + low
        s.append(ends + mid)
        d.append(high - low)
        e.append(ends)
    s_y, dy, ey, dz, dyz, ez = [], [], [], [], [], []
    for a in range(3):
        ends = s[3 * a + 2] + s[3 * a]
        s_y.append(ends + s[3 * a + 1])
        dy.append(s[3 * a + 2] - s[3 * a])
        ey.append(ends)
        dz.append(d[3 * a] + d[3 * a + 1] + d[3 * a + 2])
        dyz.append(d[3 * a + 2] - d[3 * a])
        ez.append(e[3 * a] + e[3 * a + 1] + e[3 * a + 2])
    m200 = s_y[2] + s_y[0]
    rho = m200 + s_y[1]
    jx = s_y[2] - s_y[0]
    jy = dy[0] + dy[1] + dy[2]
    jz = dz[0] + dz[1] + dz[2]
    m020 = ey[0] + ey[1] + ey[2]
    m002 = ez[0] + ez[1] + ez[2]
    m110 = dy[2] - dy[0]
    m101 = dz[2] - dz[0]
    m011 = dyz[0] + dyz[1] + dyz[2]
    return rho, jx, jy, jz, m200, m020, m002, m110, m101, m011


def unshift(k0, k1, k2, v, v2, vv, vp, vm):
    if k0 is None and k2 is None:
        return vm * k1, -(v2 * k1), vp * k1
    diff = v * k0
    ends = vv * k0
    if k1 is not None:
        diff = diff + k1
        ends = ends + v2 * k1
    if k2 is not None:
        ends = ends + k2
    high = 0.5 * (ends + diff)
    return high - diff, k0 - ends, high


def collide(f, retain):
    rho, jx, jy, jz, m200, m020, m002, m110, m101, m011 = raw_moments(f)
    inv = 1.0 / rho
    ux, uy, uz = jx * inv, jy * inv, jz * inv
    k200, k020, k002 = m200 - jx * ux, m020 - jy * uy, m002 - jz * uz
    third = 1.0 / 3.0
    d1 = retain * (k200 - k020)
    d2 = retain * (k200 - k002)
    xx = (rho + d1 + d2) * third
    yy = xx - d1
    zz = xx - d2
    xy = retain * (m110 - jx * uy)
    xz = retain * (m101 - jx * uz)
    yz = retain * (m011 - jy * uz)
    xy2, xz2, yz2 = 2.0 * xy, 2.0 * xz, 2.0 * yz
    xyi, xzi, yzi = xy2 * inv, xz2 * inv, yz2 * inv
    xxi = xx * inv
    yyi = yy * inv
    q_xy, q_xz, q_yz = xy * xyi, xz * xzi, yz * yzi
    xxyy = xxi * yy + q_xy
    xxzz = xxi * zz + q_xz
    yyzz = yyi * zz + q_yz
    xxyz = xxi * yz + xy * xzi
    xyyz = yyi * xz + xy * yzi
    xyzz = (zz * inv) * xy + xz * yzi
    full = xxi * (yyi * zz + q_yz) + (yyi * q_xz + (zz * inv) * q_xy) + (2.0 * xyi) * (xz * yzi)
    table = {
        (0, 0): (rho, None, xx),
        (1, 0): (None, xy, None),
        (2, 0): (yy, None, xxyy),
        (0, 1): (None, xz, None),
        (1, 1): (yz, None, xxyz),
        (2, 1): (None, xyyz, None),
        (0, 2): (zz, None, xxzz),
        (1, 2): (None, xyzz, None),
        (2, 2): (yyzz, None, full),
    }

    def speeds(v):
        return v, 2.0 * v, v * v, v + 0.5, v - 0.5

    sx, sy, sz = speeds(ux), speeds(uy), speeds(uz)
    after_x = {}
    for (b, c), ks in table.items():
        for a, value in enumerate(unshift(*ks, *sx)):
            after_x[a, b, c] = value
    out = [None] * 27
    for a in range(3):
        after_y = {}
        for c in range(3):
            triple = unshift(*(after_x[a, b, c] for b in range(3)), *sy)
            for b, value in enumerate(triple):
                after_y[b, c] = value
        for b in range(3):
            triple = unshift(*(after_y[b, c] for c in range(3)), *sz)
            for c, value in enumerate(triple):
                out[9 * a + 3 * b + c] = value
    return out, (rho, jx, jy, jz)


def odd_block(axis):
    return lax.rem(lax.axis_index(axis), 2)


def widen(far, near, wide, axis):
    odd = odd_block(axis)
    wide[odd, :, :] = far[...].astype(F32)
    wide[1 - odd, :, :] = near[...].astype(F32)


def merge_named(own, wide, *others):
    named = own
    for more in (wide[0, pl.ds(wide.shape[1] - SUB, SUB), :], wide[1, pl.ds(wide.shape[1] - SUB, SUB), :], *others):
        named = jnp.maximum(named, more)
    return named


def start_all(copies):
    for copy in copies:
        copy.start()
    return copies


def rows_order(side):
    outward = 1 - 2 * side
    both = [i for i in range(27) if STEP[i][1] == outward]
    return both, [i for i in range(27) if STEP[i][1] != outward]


def named_tile(patches, place, nz):
    slots = patches.shape[-1]
    groups = slots // SUB
    ids = jnp.broadcast_to(patches[0, :, :].astype(F32) + 1.0, (SUB, slots))
    row = lax.broadcasted_iota(jnp.int32, (SUB, slots), 0)
    slot = lax.broadcasted_iota(jnp.int32, (SUB, slots), 1)
    lane = lax.broadcasted_iota(jnp.int32, (SUB, nz), 1)
    tile = jnp.zeros((SUB, nz), F32)
    for g in range(groups):
        column = jnp.sum(jnp.where(slot == SUB * g + row, ids, 0.0), axis=1, keepdims=True)
        tile = jnp.where(lane == place * groups + g, column, tile)
    return tile


def rows_kernel(
    size_y, pops_in, omega_in, walls_in, patches_in, far, near, own,
    pops, omega, walls, patches, packed, faces, sems,
):
    planes, ny, nz = omega.shape
    row = lax.broadcasted_iota(jnp.int32, (SUB, nz), 0)
    chunk = 4
    spans = [pl.ds(i, min(chunk, 27 - i)) for i in range(0, 27, chunk)]
    cells = [
        pltpu.make_async_copy(omega_in, omega, sems.at[len(spans)]),
        pltpu.make_async_copy(walls_in, walls, sems.at[len(spans) + 1]),
        pltpu.make_async_copy(patches_in, patches, sems.at[len(spans) + 2]),
    ]
    copies = [pltpu.make_async_copy(pops_in.at[span], pops.at[span], sems.at[k]) for k, span in enumerate(spans)]
    start_all(cells + copies)

    def read(group, plane, first):
        part = pl.ds(first, SUB)
        if group < 27:
            return pops[group, plane, part, :]
        if group == 27:
            return 1.0 - omega[plane, part, :]
        return walls[plane, part, :].astype(F32)

    def pack(group):
        for side, first, at in ((0, ny - SUB, SUB - 2), (1, 0, 0)):
            tile = None
            for plane in range(planes):
                turn = (2 * plane - at) % SUB
                piece = read(group, plane, first)
                piece = pltpu.roll(piece, turn, 0) if turn else piece
                tile = piece if tile is None else jnp.where(row // 2 == plane, piece, tile)
            packed[side, group, :, :] = tile

    for copy in cells:
        copy.wait()
    pack(27)
    pack(28)
    named = named_tile(patches, lax.axis_index("gx") * size_y + lax.axis_index("gy"), nz)
    own[...] = jnp.concatenate([named, jnp.zeros((SUB, nz), F32)], axis=0).astype(BF16)
    for i in range(27):
        if i % chunk == 0:
            copies[i // chunk].wait()
        pack(i)
    for side in range(2):
        for part in range(nz // LANES):
            cols = pl.ds(LANES * part, LANES)
            closed = packed[side, 28, :, cols] > 0.5
            f = [packed[side, i, :, cols] * WEIGHT[i] for i in range(27)]
            relaxed, _ = collide(f, packed[side, 27, :, cols])
            for i in range(27):
                packed[side, i, :, cols] = jnp.where(closed, SOLID, relaxed[i]) * (1.0 / WEIGHT[i]) - 1.0
        both, edge = rows_order(side)
        edge = edge + [27, 28]
        tiles = [packed[side, i, :, :] for i in both]
        for k in range(0, len(edge), 2):
            one, two = (packed[side, i, :, :] for i in edge[k : k + 2])
            at_edge = row % 2 == 1 - side
            tiles.append(jnp.where(at_edge, one, pltpu.roll(two, SUB - 1 if side == 0 else 1, 0)))
        tiles.append(named)
        for k, tile in enumerate(tiles):
            faces[side, pl.ds(SUB * k, SUB), :] = tile
    odd = odd_block("gy")
    far[...] = faces[1 - odd, :, :].astype(BF16)
    near[...] = faces[odd, :, :].astype(BF16)


def first_main_kernel(pops, omega, walls, post):
    planes, ny, nz = omega.shape

    def body(plane, carry):
        for t in range(ny // SUB):
            for part in range(nz // LANES):
                at = (plane, pl.ds(SUB * t, SUB), pl.ds(LANES * part, LANES))
                f = [pops[(i, *at)] * WEIGHT[i] for i in range(27)]
                closed = walls[at] == 1
                out, _ = collide(f, 1.0 - omega[at])
                for i in range(27):
                    post[(i, *at)] = jnp.where(closed, SOLID, out[i])
        return carry

    lax.fori_loop(0, planes, body, 0)


def corner_rows(reach):
    places = {}
    for k in range(9):
        sy, j = STEP[k][1], k % 3
        if reach == 2:
            rows = {1: ((6, 6), (7, 7)), 0: ((7, 3), (0, 4)), -1: ((0, 0), (1, 1))}[sy]
            places[k] = [(ring, j, at) for ring, at in rows]
        else:
            places[k] = {1: [(7, 0, j)], 0: [], -1: [(0, 0, 3 + j)]}[sy]
    return places


def face_rows(ny, reach):
    return 9 * ny + (4 if reach == 2 else 2) * SUB


def pack_x(main, halo, plane, first, reach, named, out):
    ny, nz = main.shape[2:]
    row = lax.broadcasted_iota(jnp.int32, (SUB, nz), 0)
    scaled = lambda ref, k: ref[first + k, plane, :, :] * (1.0 / WEIGHT[k]) - 1.0
    for k in range(9):
        out[pl.ds(ny * k, ny), :] = scaled(main, k).astype(BF16)
    tiles = [jnp.zeros((SUB, nz), F32) for _ in range((out.shape[0] - 9 * ny) // SUB)]
    for k, places in corner_rows(reach).items():
        for ring, tile, at in places:
            turn = (at - ring) % SUB
            value = scaled(halo, k)
            value = pltpu.roll(value, turn, 0) if turn else value
            tiles[tile] = jnp.where(row == at, value, tiles[tile])
    tiles[-1] = named
    out[pl.ds(9 * ny, SUB * len(tiles)), :] = jnp.concatenate(tiles, axis=0).astype(BF16)


def pack_faces(main, halo, last, reach, named, far, near):
    odd = odd_block("gx")
    pack_x(main, halo, odd * last, odd * 18, reach, named, far)
    pack_x(main, halo, (1 - odd) * last, (1 - odd) * 18, reach, named, near)


def first_halo_kernel(far, near, main, own, across, halo, retain, solid, named, send_far, send_near, wide):
    _, planes, _, nz = halo.shape
    row = lax.broadcasted_iota(jnp.int32, (SUB, nz), 0)
    widen(far, near, wide, "gy")

    def received(side, group, plane):
        both, edge = rows_order(side)
        edge = edge + [27, 28]
        turn = (SUB - 2, 0)[side] - 2 * plane
        if group in both:
            tile = both.index(group)
        else:
            k = edge.index(group)
            tile = len(both) + k // 2
            turn += (k % 2) * (1 - 2 * side)
        value = wide[side, pl.ds(SUB * tile, SUB), :]
        return pltpu.roll(value, turn % SUB, 0) if turn % SUB else value

    def beside(group, plane):
        return jnp.where(row < 4, received(1, group, plane), received(0, group, plane))

    for plane in range(planes):
        retain[plane, :, :] = beside(27, plane)
        solid[plane, :, :] = beside(28, plane)
        for i in range(27):
            halo[i, plane, :, :] = (beside(i, plane) + 1.0) * WEIGHT[i]
    named[...] = merge_named(own[...].astype(F32)[:SUB], wide, across[...].astype(F32)[:SUB])
    pack_faces(main, halo, planes - 1, 2, named[...], send_far, send_near)


def turned(value, i):
    _, sy, sz = STEP[i]
    if sy:
        value = pltpu.roll(value, sy % value.shape[0], 0)
    if sz:
        value = pltpu.roll(value, sz % value.shape[1], 1)
    return value


def pull(load, i, plane):
    value = turned(load(i, plane - STEP[i][0]), i)
    return jnp.where(value > LIMIT, load(26 - i, plane), value)


def loader(planes, ny, places, wide=None):
    def load(i, plane):
        if 0 <= plane < planes:
            main, halo, at = places[plane]
            return jnp.concatenate([main[i, at, :, :], halo[i, at, :, :]], axis=0)
        side, k = (0, i - 18) if plane < 0 else (1, i)
        reach = 2 if wide.shape[1] == face_rows(ny, 2) else 1
        used = corner_rows(reach)[k]
        if used:
            ring, tile, at = used[0]
            halo = wide[side, pl.ds(9 * ny + SUB * tile, SUB), :]
            halo = pltpu.roll(halo, (ring - at) % SUB, 0) if ring != at else halo
        else:
            halo = jnp.zeros((SUB, wide.shape[2]), F32)
        both = jnp.concatenate([wide[side, pl.ds(ny * k, ny), :], halo], axis=0)
        return (both + 1.0) * WEIGHT[i]

    return load


def middle(mine, load, pops, omega, walls, retain, solid, main2, halo2, macro, read):
    planes, ny, nz = omega.shape
    for at, plane in enumerate(mine):
        own = walls[plane, :, :] == 1
        for i in range(27):
            value = pull(load, i, plane)
            read[i, pl.ds(0, ny), :] = jnp.where(own, pops[i, plane, :, :] * WEIGHT[i], value[:ny])
            read[i, pl.ds(ny, SUB), :] = value[ny:]
        for t in range(ny // SUB + 1):
            for part in range(nz // LANES):
                rows, cols = pl.ds(SUB * t, SUB), pl.ds(LANES * part, LANES)
                inner = SUB * t < ny
                if inner:
                    closed = walls[plane, rows, cols] == 1
                    keep = 1.0 - omega[plane, rows, cols]
                else:
                    closed = solid[plane, :, cols] > 0.5
                    keep = retain[plane, :, cols]
                out, sums = collide([read[i, rows, cols] for i in range(27)], keep)
                for i in range(27):
                    value = jnp.where(closed, SOLID, out[i])
                    if inner:
                        main2[i, at, rows, cols] = value
                    else:
                        halo2[i, at, :, cols] = value
                if inner:
                    macro[0, at, rows, cols] = sums[0] - 1.0
                    for m in range(1, 4):
                        macro[m, at, rows, cols] = sums[m]


def middle_inner_kernel(main, halo, pops, omega, walls, retain, solid, main2, halo2, macro, read):
    planes, ny, _ = omega.shape
    load = loader(planes, ny, [(main, halo, p) for p in range(planes)])
    middle(range(1, planes - 1), load, pops, omega, walls, retain, solid, main2, halo2, macro, read)


def middle_outer_kernel(
    main, halo, pops, omega, walls, retain, solid, far, near, own, _, __,
    main2, halo2, macro, named, send_far, send_near, read, wide,
):
    planes, ny, _ = omega.shape
    widen(far, near, wide, "gx")
    load = loader(planes, ny, [(main, halo, p) for p in range(planes)], wide)
    middle((0, planes - 1), load, pops, omega, walls, retain, solid, main2, halo2, macro, read)
    more = merge_named(own[...], wide)
    named[...] = jnp.concatenate([more, jnp.zeros(more.shape, F32)], axis=0).astype(BF16)
    pack_faces(main2, halo2, 1, 1, more, send_far, send_near)


def add_moments(sums, i, f):
    for m, sign in enumerate((1,) + STEP[i]):
        if sign:
            term = f if sign > 0 else -f
            sums[m] = term if sums[m] is None else sums[m] + term


def respond(planes, radiation, pick, fields):
    for p, rows in enumerate(planes):
        ny = rows[0].shape[0]
        for m in range(4):
            fields[m, pl.ds(p * ny, ny), :] = rows[m].astype(BF16)
    parts = []
    for m in range(4):
        total = None
        for h in range(pick.shape[0]):
            term = jnp.dot(pick[h, :, :], fields[m, :, pl.ds(LANES * h, LANES)], preferred_element_type=F32)
            total = term if total is None else total + term
        parts.append(total)
    surface = jnp.concatenate(parts, axis=1).astype(BF16)
    response = jnp.dot(surface, radiation[...], preferred_element_type=F32)
    return response.astype(BF16)


def slots_kernel(size_y, bins, radiation, counts, sites, patches, pick, level, own_bins, turned_radiation):
    halves, slots, lines = pick.shape
    slot = lax.broadcasted_iota(jnp.int32, (slots, lines), 0)
    line = lax.broadcasted_iota(jnp.int32, (slots, lines), 1)
    wanted = jnp.full((slots, lines), -1, jnp.int32)
    for k in range(slots):
        site = jnp.where(k < counts[0, 0], sites[0, 0, k], -halves)
        wanted = jnp.where(slot == k, site, wanted)
    for h in range(halves):
        pick[h, :, :] = (wanted == line * halves + h).astype(BF16)

    n_patch = bins.shape[1]
    slot = lax.broadcasted_iota(jnp.int32, (slots, n_patch), 0)
    named = lax.broadcasted_iota(jnp.int32, (slots, n_patch), 1)
    wanted = jnp.full((slots, n_patch), -1, jnp.int32)
    for k in range(slots):
        wanted = jnp.where(slot == k, patches[0, 0, k], wanted)
    chosen = (wanted == named).astype(BF16)
    per_block = lax.dot_general(
        chosen, bins[...].astype(F32).astype(BF16), (((1,), (1,)), ((), ())), preferred_element_type=F32
    )
    devices, _, width = level.shape
    groups = slots // SUB
    group = lax.broadcasted_iota(jnp.int32, (SUB, width), 1) // (width // groups)
    tiles = {}
    for d in range(devices):
        blk = d * width // OBS_BLK
        if blk not in tiles:
            tile = None
            for g in range(groups):
                column = per_block[SUB * g : SUB * (g + 1), blk : blk + 1]
                column = jnp.broadcast_to(column, (SUB, width))
                tile = column if tile is None else jnp.where(group == g, column, tile)
            tiles[blk] = tile.astype(BF16)
        level[d, :, :] = tiles[blk]

    place = lax.axis_index("gx") * size_y + lax.axis_index("gy")
    mine = bins[pl.ds(lax.div(place * width, OBS_BLK), 1), :].astype(F32)
    own_bins[...] = jnp.broadcast_to(mine, own_bins.shape).astype(BF16)

    observers, terms = radiation.shape

    def body(k, carry):
        rows = pl.ds(pl.multiple_of(k * terms, terms), terms)
        turned_radiation[:, rows] = radiation[rows, :].T
        return carry

    lax.fori_loop(0, observers // terms, body, 0)


def last_early_kernel(
    main_in, halo_in, main_out, halo_out, pops, walls, macro_in, macro_out, radiation, pick,
    out, spare, part, inner, send, g_out, fields, sems,
):
    planes, ny, _ = walls.shape
    last = planes - 1
    places = [(main_out, halo_out, 0)]
    places += [(main_in, halo_in, p) for p in range(planes - 2)]
    places += [(main_out, halo_out, 1)]
    load = loader(planes, ny, places)
    copies = []
    for plane in (0, last, *range(1, last)):
        own = walls[plane, :, :] == 1
        edge = {0: 0, last: 1}.get(plane)
        sums = [None] * 4
        for i in range(27):
            if 0 <= plane - STEP[i][0] <= last:
                value = pull(load, i, plane)[:ny]
                g = jnp.where(own, pops[i, plane, :, :], value * (1.0 / WEIGHT[i]))
                g_out[i, plane, :, :] = g
                add_moments(sums, i, g * WEIGHT[i])
            else:
                bounced = load(26 - i, plane)[:ny]
                spare[edge, i % 9, :, :] = jnp.where(own, pops[i, plane, :, :] * WEIGHT[i], bounced)
        for m in range(4):
            if edge is None:
                inner[m, plane - 1, :, :] = sums[m] - 1.0 if m == 0 else sums[m]
            else:
                part[m, edge, :, :] = sums[m]
        span = pl.ds((0, 9)[edge], 18) if edge is not None else pl.ds(0, 27)
        copies += start_all(
            [pltpu.make_async_copy(g_out.at[span, plane], out.at[span, plane], sems.at[len(copies)])]
        )
    rows = [[macro_out[m, 0, :, :] for m in range(4)]]
    rows += [[macro_in[m, p, :, :] for m in range(4)] for p in range(planes - 2)]
    rows += [[macro_out[m, 1, :, :] for m in range(4)]]
    response = respond(rows, radiation, pick, fields)
    devices, _, width = send.shape
    for d in range(devices):
        send[d, :, :] = response[:, d * width : (d + 1) * width]
    for copy in copies:
        copy.wait()


def last_kernel(
    far, near, walls, spare, part, inner, radiation, pick, early, level, own, across, started,
    out, send, named, g_out, fields, wide, sems,
):
    planes, ny, _ = walls.shape
    last = planes - 1
    widen(far, near, wide, "gx")
    load = loader(planes, ny, None, wide)
    rows, copies = {}, []
    for edge, (plane, first) in enumerate(((0, 18), (last, 0))):
        own = walls[plane, :, :] == 1
        sums = [part[m, edge, :, :] for m in range(4)]
        for k in range(9):
            i = first + k
            value = turned(load(i, plane - STEP[i][0]), i)[:ny]
            f = jnp.where(own | (value > LIMIT), spare[edge, k, :, :], value)
            g_out[k, edge, :, :] = f * (1.0 / WEIGHT[i])
            add_moments(sums, i, f)
        rows[plane] = [sums[0] - 1.0, *sums[1:]]
        copies += start_all(
            [pltpu.make_async_copy(g_out.at[:, edge], out.at[pl.ds(first, 9), plane], sems.at[edge])]
        )
    for p in range(planes - 2):
        rows[p + 1] = [inner[m, p, :, :] for m in range(4)]
    response = respond([rows[p] for p in range(planes)], radiation, pick, fields)
    devices, _, width = send.shape
    slots = early.shape[1]
    for d in range(devices):
        send[d, pl.ds(0, slots), :] = early[d, :, :]
        send[d, pl.ds(slots, slots), :] = response[:, d * width : (d + 1) * width]
        if send.shape[1] > 2 * slots:
            send[d, pl.ds(2 * slots, SUB), :] = level[d, :, :]
    named[...] = merge_named(own[...].astype(F32)[:SUB], wide, across[...].astype(F32)[:SUB])
    for copy in copies:
        copy.wait()


def bin_named_kernel(received, named, own_bins, signal, hits, known):
    devices, rows, width = received.shape
    slots = rows // 2
    groups = slots // SUB
    patch = lax.broadcasted_iota(jnp.int32, (slots, known.shape[-1]), 1).astype(F32) + 1.0
    for d in range(devices):
        columns = [named[:, groups * d + g : groups * d + g + 1] for g in range(groups)]
        ids = jnp.concatenate([jnp.broadcast_to(c, (SUB, patch.shape[1])) for c in columns], axis=0)
        known[d, :, :] = (ids == patch).astype(F32).astype(BF16)
    flat = known[...].reshape(devices * slots, patch.shape[1])
    level = lax.dot_general(flat, own_bins[...], (((1,), (1,)), ((), ())), preferred_element_type=F32)
    lane = lax.broadcasted_iota(jnp.int32, level.shape, 1).astype(F32)
    for step in range(2):
        hit = (level == lane - float(step)).astype(F32).astype(BF16)
        hits[:, pl.ds(step * slots, slots), :] = hit.reshape(devices, slots, LEVELS)
    left = received[...].reshape(devices * rows, width)
    right = hits[...].reshape(devices * rows, LEVELS)
    signal[...] = lax.dot_general(left, right, (((0,), (0,)), ((), ())), preferred_element_type=F32)


def bin_kernel(received, signal, hits):
    devices, rows, width = received.shape
    slots = (rows - SUB) // 2
    groups = slots // SUB
    lane = lax.broadcasted_iota(jnp.int32, (slots, LEVELS), 1).astype(F32)
    for d in range(devices):
        tile = received[d, pl.ds(2 * slots, SUB), :].astype(F32)
        starts = [g * (width // groups) for g in range(groups)]
        level = jnp.concatenate([jnp.broadcast_to(tile[:, k : k + 1], (SUB, LEVELS)) for k in starts], axis=0)
        for step in range(2):
            hit = (level == lane - float(step)).astype(F32).astype(BF16)
            hits[d, pl.ds(step * slots, slots), :] = hit
    left = received[:, pl.ds(0, 2 * slots), :].reshape(devices * 2 * slots, width)
    right = hits[...].reshape(devices * 2 * slots, LEVELS)
    signal[...] = lax.dot_general(left, right, (((0,), (0,)), ((), ())), preferred_element_type=F32)


def per_device(populations, omega, walls, radiation, bins, counts, sample_site, sample_patch):
    _, planes, ny, nz = populations.shape
    slots = sample_site.shape[-1]
    size_x, size_y = lax.axis_size("gx"), lax.axis_size("gy")
    devices = size_x * size_y
    width = radiation.shape[0] // devices

    def swap(far, near, axis, size):
        far_pairs = [(i, (i - 1 + 2 * (i % 2)) % size) for i in range(size)]
        near_pairs = [(i, i + 1 - 2 * (i % 2)) for i in range(size)]
        return lax.ppermute(far, axis, far_pairs), lax.ppermute(near, axis, near_pairs)

    dma = pltpu.SemaphoreType.DMA
    block, cells = populations.shape, (planes, ny, nz)
    beside = (20 * SUB, nz)
    far, near, own = call(
        functools.partial(rows_kernel, size_y),
        [HBM] * 4,
        [(VMEM, beside, BF16)] * 2 + [(VMEM, (2 * SUB, nz), BF16)],
        [
            pltpu.VMEM(block, F32), pltpu.VMEM(cells, F32), pltpu.VMEM(cells, walls.dtype),
            pltpu.VMEM(sample_patch.shape, sample_patch.dtype),
            pltpu.VMEM((2, 29, SUB, nz), F32), pltpu.VMEM((2, *beside), F32), dma((10,)),
        ],
        cost=1 << 20,
        limit=64800000,
    )(populations, omega, walls, sample_patch)
    far, near = swap(far, near, "gy", size_y)
    across = lax.ppermute(own, "gy", [(i, (i + size_y // 2) % size_y) for i in range(size_y)])
    pick, level, own_bins, radiation = call(
        functools.partial(slots_kernel, size_y),
        [VMEM] * 2 + [SMEM] * 3,
        [
            (VMEM, (nz // LANES, slots, planes * ny), BF16),
            (VMEM, (devices, SUB, width), BF16),
            (VMEM, (LEVELS, bins.shape[0]), BF16),
            (VMEM, radiation.shape[::-1], BF16),
        ],
        cost=1 << 22,
    )(bins.T, radiation, counts, sample_site, sample_patch)
    (main,) = call(first_main_kernel, [VMEM] * 3, [(VMEM, block, F32)], cost=1 << 22)(populations, omega, walls)

    edge = (planes, SUB, nz)
    face, last_face = ((face_rows(ny, reach), nz) for reach in (2, 1))
    faces, last_faces = ([(VMEM, shape, BF16)] * 2 for shape in (face, last_face))
    halo, retain, solid, named, far, near = call(
        first_halo_kernel,
        [VMEM] * 5,
        [(VMEM, (27, *edge), F32), (VMEM, edge, F32), (VMEM, edge, F32), (VMEM, (SUB, nz), F32), *faces],
        [pltpu.VMEM((2, *beside), F32)],
        cost=1 << 20,
    )(far, near, main, own, across)
    far, near = swap(far, near, "gx", size_x)

    def relaxed(n):
        return [(VMEM, (27, n, ny, nz), F32), (VMEM, (27, n, SUB, nz), F32), (VMEM, (4, n, ny, nz), F32)]

    read = pltpu.VMEM((27, ny + SUB, nz), F32)
    wide, last_wide = (pltpu.VMEM((2, *shape), F32) for shape in (face, last_face))
    args = (main, halo, populations, omega, walls, retain, solid)
    main_in, halo_in, macro_in = call(
        middle_inner_kernel, [VMEM] * 7, relaxed(planes - 2), [read], cost=1 << 22
    )(*args)
    main_out, halo_out, macro_out, named, far, near = call(
        middle_outer_kernel, [VMEM] * 12, relaxed(2) + [(VMEM, (2 * SUB, nz), BF16), *last_faces], [read, wide], cost=1 << 22
    )(*args, far, near, named, macro_in, pick)
    far, near = swap(far, near, "gx", size_x)
    across = lax.ppermute(named, "gx", [(i, (i + size_x // 2) % size_x) for i in range(size_x)])

    fields = pltpu.VMEM((4, planes * ny, nz), BF16)
    inner = (4, planes - 2, ny, nz)
    started, spare, part, inner, early = call(
        last_early_kernel,
        [VMEM] * 10,
        [
            (HBM, block, F32),
            (VMEM, (2, 9, ny, nz), F32),
            (VMEM, (4, 2, ny, nz), F32),
            (VMEM, inner, F32),
            (VMEM, (devices, slots, width), BF16),
        ],
        [pltpu.VMEM(block, F32), fields, dma((planes,))],
        cost=1 << 22,
    )(main_in, halo_in, main_out, halo_out, populations, walls, macro_in, macro_out, radiation, pick)
    ride = (size_x, size_y) == (8, 4)
    sent = 2 * slots if ride else 2 * slots + SUB
    advanced, send, named = call(
        last_kernel,
        [VMEM] * 12 + [HBM],
        [(HBM, block, F32), (VMEM, (devices, sent, width), BF16), (VMEM, (SUB, nz), F32)],
        [pltpu.VMEM((9, 2, ny, nz), F32), fields, last_wide, dma((2,))],
        aliases={12: 0},
        cost=1 << 22,
    )(far, near, walls, spare, part, inner, radiation, pick, early, level, named, across, started)
    received = lax.all_to_all(send, ("gx", "gy"), 0, 0, tiled=True)
    hits = pltpu.VMEM((devices, 2 * slots, LEVELS), BF16)
    result = [(VMEM, (width, LEVELS), F32)]
    if ride:
        known = pltpu.VMEM((devices, slots, bins.shape[0]), BF16)
        (signal,) = call(bin_named_kernel, [VMEM] * 3, result, [hits, known], cost=1 << 20)(received, named, own_bins)
    else:
        (signal,) = call(bin_kernel, [VMEM], result, [hits], cost=1 << 20)(received)
    return advanced, signal


def solution(mesh):
    return jax.shard_map(
        per_device,
        mesh=mesh,
        in_specs=(
            P(None, "gx", "gy", None),
            P("gx", "gy", None),
            P("gx", "gy", None),
            P(),
            P(),
            P("gx", "gy"),
            P("gx", "gy", None),
            P("gx", "gy", None),
        ),
        out_specs=(P(None, "gx", "gy", None), P(("gx", "gy"), None)),
        check_vma=False,
    )
```

```python
import functools

import jax
import jax.numpy as jnp
from jax import lax
from jax.experimental import pallas as pl
from jax.experimental.pallas import tpu as pltpu
from jax.sharding import PartitionSpec as P

F32 = jnp.float32
BF16 = jnp.bfloat16
LEVELS = 128
OBS_BLK = 128
SOLID = 1e30
LIMIT = 1e29
LANES = 128
SUB = 8

WEIGHT = [
    (8.0 / 27.0, 2.0 / 27.0, 1.0 / 54.0, 1.0 / 216.0)[
        int(i // 9 != 1) + int(i // 3 % 3 != 1) + int(i % 3 != 1)
    ]
    for i in range(27)
]
STEP = [(i // 9 - 1, i // 3 % 3 - 1, i % 3 - 1) for i in range(27)]
VMEM = pl.BlockSpec(memory_space=pltpu.VMEM)
SMEM = pl.BlockSpec(memory_space=pltpu.SMEM)
HBM = pl.BlockSpec(memory_space=pltpu.HBM)


def call(kernel, in_specs, out, scratch=(), aliases=None, cost=0, limit=14 * 1024 * 1024):
    return pl.pallas_call(
        kernel,
        out_shape=[jax.ShapeDtypeStruct(shape, dtype) for _, shape, dtype in out],
        in_specs=in_specs,
        out_specs=[spec for spec, _, _ in out],
        scratch_shapes=list(scratch),
        input_output_aliases=aliases or {},
        compiler_params=pltpu.CompilerParams(vmem_limit_bytes=limit),
        cost_estimate=pl.CostEstimate(flops=cost, bytes_accessed=cost, transcendentals=0),
    )


def raw_moments(f):
    s, d, e = [], [], []
    for k in range(9):
        low, mid, high = f[3 * k : 3 * k + 3]
        ends = high + low
        s.append(ends + mid)
        d.append(high - low)
        e.append(ends)
    s_y, dy, ey, dz, dyz, ez = [], [], [], [], [], []
    for a in range(3):
        ends = s[3 * a + 2] + s[3 * a]
        s_y.append(ends + s[3 * a + 1])
        dy.append(s[3 * a + 2] - s[3 * a])
        ey.append(ends)
        dz.append(d[3 * a] + d[3 * a + 1] + d[3 * a + 2])
        dyz.append(d[3 * a + 2] - d[3 * a])
        ez.append(e[3 * a] + e[3 * a + 1] + e[3 * a + 2])
    m200 = s_y[2] + s_y[0]
    rho = m200 + s_y[1]
    jx = s_y[2] - s_y[0]
    jy = dy[0] + dy[1] + dy[2]
    jz = dz[0] + dz[1] + dz[2]
    m020 = ey[0] + ey[1] + ey[2]
    m002 = ez[0] + ez[1] + ez[2]
    m110 = dy[2] - dy[0]
    m101 = dz[2] - dz[0]
    m011 = dyz[0] + dyz[1] + dyz[2]
    return rho, jx, jy, jz, m200, m020, m002, m110, m101, m011


def unshift(k0, k1, k2, v, v2, vv, vp, vm):
    if k0 is None and k2 is None:
        return vm * k1, -(v2 * k1), vp * k1
    diff = v * k0
    ends = vv * k0
    if k1 is not None:
        diff = diff + k1
        ends = ends + v2 * k1
    if k2 is not None:
        ends = ends + k2
    high = 0.5 * (ends + diff)
    return high - diff, k0 - ends, high


def collide(f, retain):
    rho, jx, jy, jz, m200, m020, m002, m110, m101, m011 = raw_moments(f)
    inv = 1.0 / rho
    ux, uy, uz = jx * inv, jy * inv, jz * inv
    k200, k020, k002 = m200 - jx * ux, m020 - jy * uy, m002 - jz * uz
    third = 1.0 / 3.0
    d1 = retain * (k200 - k020)
    d2 = retain * (k200 - k002)
    xx = (rho + d1 + d2) * third
    yy = xx - d1
    zz = xx - d2
    xy = retain * (m110 - jx * uy)
    xz = retain * (m101 - jx * uz)
    yz = retain * (m011 - jy * uz)
    xy2, xz2, yz2 = 2.0 * xy, 2.0 * xz, 2.0 * yz
    xyi, xzi, yzi = xy2 * inv, xz2 * inv, yz2 * inv
    xxi = xx * inv
    yyi = yy * inv
    q_xy, q_xz, q_yz = xy * xyi, xz * xzi, yz * yzi
    xxyy = xxi * yy + q_xy
    xxzz = xxi * zz + q_xz
    yyzz = yyi * zz + q_yz
    xxyz = xxi * yz + xy * xzi
    xyyz = yyi * xz + xy * yzi
    xyzz = (zz * inv) * xy + xz * yzi
    full = xxi * (yyi * zz + q_yz) + (yyi * q_xz + (zz * inv) * q_xy) + (2.0 * xyi) * (xz * yzi)
    table = {
        (0, 0): (rho, None, xx),
        (1, 0): (None, xy, None),
        (2, 0): (yy, None, xxyy),
        (0, 1): (None, xz, None),
        (1, 1): (yz, None, xxyz),
        (2, 1): (None, xyyz, None),
        (0, 2): (zz, None, xxzz),
        (1, 2): (None, xyzz, None),
        (2, 2): (yyzz, None, full),
    }

    def speeds(v):
        return v, 2.0 * v, v * v, v + 0.5, v - 0.5

    sx, sy, sz = speeds(ux), speeds(uy), speeds(uz)
    after_x = {}
    for (b, c), ks in table.items():
        for a, value in enumerate(unshift(*ks, *sx)):
            after_x[a, b, c] = value
    out = [None] * 27
    for a in range(3):
        after_y = {}
        for c in range(3):
            triple = unshift(*(after_x[a, b, c] for b in range(3)), *sy)
            for b, value in enumerate(triple):
                after_y[b, c] = value
        for b in range(3):
            triple = unshift(*(after_y[b, c] for c in range(3)), *sz)
            for c, value in enumerate(triple):
                out[9 * a + 3 * b + c] = value
    return out, (rho, jx, jy, jz)


def odd_block(axis):
    return lax.rem(lax.axis_index(axis), 2)


def widen(far, near, wide, axis):
    odd = odd_block(axis)
    wide[odd, :, :] = far[...].astype(F32)
    wide[1 - odd, :, :] = near[...].astype(F32)


def merge_named(own, wide, *others):
    named = own
    for more in (wide[0, pl.ds(wide.shape[1] - SUB, SUB), :], wide[1, pl.ds(wide.shape[1] - SUB, SUB), :], *others):
        named = jnp.maximum(named, more)
    return named


def start_all(copies):
    for copy in copies:
        copy.start()
    return copies


def rows_order(side):
    outward = 1 - 2 * side
    both = [i for i in range(27) if STEP[i][1] == outward]
    return both, [i for i in range(27) if STEP[i][1] != outward]


def named_tile(patches, place, nz):
    slots = patches.shape[-1]
    groups = slots // SUB
    ids = jnp.broadcast_to(patches[0, :, :].astype(F32) + 1.0, (SUB, slots))
    row = lax.broadcasted_iota(jnp.int32, (SUB, slots), 0)
    slot = lax.broadcasted_iota(jnp.int32, (SUB, slots), 1)
    lane = lax.broadcasted_iota(jnp.int32, (SUB, nz), 1)
    tile = jnp.zeros((SUB, nz), F32)
    for g in range(groups):
        column = jnp.sum(jnp.where(slot == SUB * g + row, ids, 0.0), axis=1, keepdims=True)
        tile = jnp.where(lane == place * groups + g, column, tile)
    return tile


def rows_kernel(
    size_y, pops_in, omega_in, walls_in, patches_in, far, near, own,
    pops, omega, walls, patches, packed, faces, sems,
):
    planes, ny, nz = omega.shape
    row = lax.broadcasted_iota(jnp.int32, (SUB, nz), 0)
    chunk = 4
    spans = [pl.ds(i, min(chunk, 27 - i)) for i in range(0, 27, chunk)]
    cells = [
        pltpu.make_async_copy(omega_in, omega, sems.at[0, len(spans)]),
        pltpu.make_async_copy(walls_in, walls, sems.at[1, len(spans)]),
        pltpu.make_async_copy(patches_in, patches, sems.at[0, len(spans) + 1]),
    ]
    copies = [
        pltpu.make_async_copy(pops_in.at[span, :, rows, :], pops.at[span, :, rows, :], sems.at[side, k])
        for k, span in enumerate(spans)
        for side, rows in enumerate((pl.ds(0, 2), pl.ds(ny - 2, 2)))
    ]
    start_all(cells + copies)

    def read(group, plane, first):
        part = pl.ds(first, SUB)
        if group < 27:
            return pops[group, plane, part, :]
        if group == 27:
            return 1.0 - omega[plane, part, :]
        return walls[plane, part, :].astype(F32)

    def pack(group):
        for side, first, at in ((0, ny - SUB, SUB - 2), (1, 0, 0)):
            tile = None
            for plane in range(planes):
                turn = (2 * plane - at) % SUB
                piece = read(group, plane, first)
                piece = pltpu.roll(piece, turn, 0) if turn else piece
                tile = piece if tile is None else jnp.where(row // 2 == plane, piece, tile)
            packed[side, group, :, :] = tile

    for copy in cells:
        copy.wait()
    pack(27)
    pack(28)
    named = named_tile(patches, lax.axis_index("gx") * size_y + lax.axis_index("gy"), nz)
    own[...] = jnp.concatenate([named, jnp.zeros((SUB, nz), F32)], axis=0).astype(BF16)
    for i in range(27):
        if i % chunk == 0:
            for copy in copies[i // chunk * 2 : i // chunk * 2 + 2]:
                copy.wait()
        pack(i)
    for side in range(2):
        for part in range(nz // LANES):
            cols = pl.ds(LANES * part, LANES)
            closed = packed[side, 28, :, cols] > 0.5
            f = [packed[side, i, :, cols] * WEIGHT[i] for i in range(27)]
            relaxed, _ = collide(f, packed[side, 27, :, cols])
            for i in range(27):
                packed[side, i, :, cols] = jnp.where(closed, SOLID, relaxed[i]) * (1.0 / WEIGHT[i]) - 1.0
        both, edge = rows_order(side)
        edge = edge + [27, 28]
        tiles = [packed[side, i, :, :] for i in both]
        for k in range(0, len(edge), 2):
            one, two = (packed[side, i, :, :] for i in edge[k : k + 2])
            at_edge = row % 2 == 1 - side
            tiles.append(jnp.where(at_edge, one, pltpu.roll(two, SUB - 1 if side == 0 else 1, 0)))
        tiles.append(named)
        for k, tile in enumerate(tiles):
            faces[side, pl.ds(SUB * k, SUB), :] = tile
    odd = odd_block("gy")
    far[...] = faces[1 - odd, :, :].astype(BF16)
    near[...] = faces[odd, :, :].astype(BF16)


def first_main_kernel(pops, omega, walls, post):
    planes, ny, nz = omega.shape

    def body(plane, carry):
        for t in range(ny // SUB):
            for part in range(nz // LANES):
                at = (plane, pl.ds(SUB * t, SUB), pl.ds(LANES * part, LANES))
                f = [pops[(i, *at)] * WEIGHT[i] for i in range(27)]
                closed = walls[at] == 1
                out, _ = collide(f, 1.0 - omega[at])
                for i in range(27):
                    post[(i, *at)] = jnp.where(closed, SOLID, out[i])
        return carry

    lax.fori_loop(0, planes, body, 0)


def corner_rows(reach):
    places = {}
    for k in range(9):
        sy, j = STEP[k][1], k % 3
        if reach == 2:
            rows = {1: ((6, 6), (7, 7)), 0: ((7, 3), (0, 4)), -1: ((0, 0), (1, 1))}[sy]
            places[k] = [(ring, j, at) for ring, at in rows]
        else:
            places[k] = {1: [(7, 0, j)], 0: [], -1: [(0, 0, 3 + j)]}[sy]
    return places


def face_rows(ny, reach):
    return 9 * ny + (4 if reach == 2 else 2) * SUB


def pack_x(main, halo, plane, first, reach, named, out):
    ny, nz = main.shape[2:]
    row = lax.broadcasted_iota(jnp.int32, (SUB, nz), 0)
    scaled = lambda ref, k: ref[first + k, plane, :, :] * (1.0 / WEIGHT[k]) - 1.0
    for k in range(9):
        out[pl.ds(ny * k, ny), :] = scaled(main, k).astype(BF16)
    tiles = [jnp.zeros((SUB, nz), F32) for _ in range((out.shape[0] - 9 * ny) // SUB)]
    for k, places in corner_rows(reach).items():
        for ring, tile, at in places:
            turn = (at - ring) % SUB
            value = scaled(halo, k)
            value = pltpu.roll(value, turn, 0) if turn else value
            tiles[tile] = jnp.where(row == at, value, tiles[tile])
    tiles[-1] = named
    out[pl.ds(9 * ny, SUB * len(tiles)), :] = jnp.concatenate(tiles, axis=0).astype(BF16)


def pack_faces(main, halo, last, reach, named, far, near):
    odd = odd_block("gx")
    pack_x(main, halo, odd * last, odd * 18, reach, named, far)
    pack_x(main, halo, (1 - odd) * last, (1 - odd) * 18, reach, named, near)


def first_halo_kernel(far, near, main, own, across, halo, retain, solid, named, send_far, send_near, wide):
    _, planes, _, nz = halo.shape
    row = lax.broadcasted_iota(jnp.int32, (SUB, nz), 0)
    widen(far, near, wide, "gy")

    def received(side, group, plane):
        both, edge = rows_order(side)
        edge = edge + [27, 28]
        turn = (SUB - 2, 0)[side] - 2 * plane
        if group in both:
            tile = both.index(group)
        else:
            k = edge.index(group)
            tile = len(both) + k // 2
            turn += (k % 2) * (1 - 2 * side)
        value = wide[side, pl.ds(SUB * tile, SUB), :]
        return pltpu.roll(value, turn % SUB, 0) if turn % SUB else value

    def beside(group, plane):
        return jnp.where(row < 4, received(1, group, plane), received(0, group, plane))

    for plane in range(planes):
        retain[plane, :, :] = beside(27, plane)
        solid[plane, :, :] = beside(28, plane)
        for i in range(27):
            halo[i, plane, :, :] = (beside(i, plane) + 1.0) * WEIGHT[i]
    named[...] = merge_named(own[...].astype(F32)[:SUB], wide, across[...].astype(F32)[:SUB])
    pack_faces(main, halo, planes - 1, 2, named[...], send_far, send_near)


def turned(value, i):
    _, sy, sz = STEP[i]
    if sy:
        value = pltpu.roll(value, sy % value.shape[0], 0)
    if sz:
        value = pltpu.roll(value, sz % value.shape[1], 1)
    return value


def pull(load, i, plane):
    value = turned(load(i, plane - STEP[i][0]), i)
    return jnp.where(value > LIMIT, load(26 - i, plane), value)


def loader(planes, ny, places, wide=None):
    def load(i, plane):
        if 0 <= plane < planes:
            main, halo, at = places[plane]
            return jnp.concatenate([main[i, at, :, :], halo[i, at, :, :]], axis=0)
        side, k = (0, i - 18) if plane < 0 else (1, i)
        reach = 2 if wide.shape[1] == face_rows(ny, 2) else 1
        used = corner_rows(reach)[k]
        if used:
            ring, tile, at = used[0]
            halo = wide[side, pl.ds(9 * ny + SUB * tile, SUB), :]
            halo = pltpu.roll(halo, (ring - at) % SUB, 0) if ring != at else halo
        else:
            halo = jnp.zeros((SUB, wide.shape[2]), F32)
        both = jnp.concatenate([wide[side, pl.ds(ny * k, ny), :], halo], axis=0)
        return (both + 1.0) * WEIGHT[i]

    return load


def collide_rows(at, t, f, closed, keep, main2, macro):
    rows, cols = t
    out, sums = collide(f, keep)
    for i in range(27):
        main2[i, at, rows, cols] = jnp.where(closed, SOLID, out[i])
    macro[0, at, rows, cols] = sums[0] - 1.0
    for m in range(1, 4):
        macro[m, at, rows, cols] = sums[m]


def middle_inner_kernel(main, halo, pops, omega, walls, retain, solid, main2, halo2, macro, ready, read):
    planes, ny, nz = omega.shape
    last = planes - 1
    load = loader(planes, ny, [(main, halo, p) for p in range(planes)])
    for plane in (*range(1, last), 0, last):
        inside = 0 < plane < last
        own = walls[plane, :, :] == 1
        for i in range(27):
            value = pull(load, i, plane) if 0 <= plane - STEP[i][0] <= last else load(26 - i, plane)
            value = [jnp.where(own, pops[i, plane, :, :] * WEIGHT[i], value[:ny]), value[ny:]]
            for rows, part in zip((pl.ds(0, ny), pl.ds(ny, SUB)), value):
                if inside:
                    read[i, rows, :] = part
                else:
                    ready[i, int(plane > 0), rows, :] = part
        if not inside:
            continue
        at = plane - 1
        for part in range(nz // LANES):
            cols = pl.ds(LANES * part, LANES)
            for t in range(ny // SUB):
                rows = pl.ds(SUB * t, SUB)
                f = [read[i, rows, cols] for i in range(27)]
                closed = walls[plane, rows, cols] == 1
                collide_rows(at, (rows, cols), f, closed, 1.0 - omega[plane, rows, cols], main2, macro)
            out, _ = collide([read[i, pl.ds(ny, SUB), cols] for i in range(27)], retain[plane, :, cols])
            closed = solid[plane, :, cols] > 0.5
            for i in range(27):
                halo2[i, at, :, cols] = jnp.where(closed, SOLID, out[i])


def middle_outer_kernel(
    ready, omega, walls, retain, solid, far, near, own, _,
    main2, halo2, macro, named, send_far, send_near, read, wide,
):
    planes, ny, nz = omega.shape
    last = planes - 1
    widen(far, near, wide, "gx")
    load = loader(planes, ny, None, wide)
    sides = ((0, 18), (last, 0))
    for at, (plane, first) in enumerate(sides):
        solid_cell = walls[plane, :, :] == 1
        for k in range(9):
            value = turned(load(first + k, plane - STEP[first + k][0]), first + k)
            spare = ready[first + k, at, :, :]
            shut = value > LIMIT
            read[k, at, pl.ds(0, ny), :] = jnp.where(solid_cell | shut[:ny], spare[:ny], value[:ny])
            read[k, at, pl.ds(ny, SUB), :] = jnp.where(shut[ny:], spare[ny:], value[ny:])

    def streamed(at, rows, cols):
        first = sides[at][1]
        return [
            read[i - first, at, rows, cols] if 0 <= i - first < 9 else ready[i, at, rows, cols] for i in range(27)
        ]

    row = lax.broadcasted_iota(jnp.int32, (SUB, LANES), 0)
    edge = (row == 0) | (row == SUB - 1)
    merge = lambda pair: jnp.where(edge, pair[0], pltpu.roll(pair[1], SUB // 2, 0))
    for part in range(nz // LANES):
        cols = pl.ds(LANES * part, LANES)
        for at, (plane, _) in enumerate(sides):
            for t in range(ny // SUB):
                rows = pl.ds(SUB * t, SUB)
                closed = walls[plane, rows, cols] == 1
                keep = 1.0 - omega[plane, rows, cols]
                collide_rows(at, (rows, cols), streamed(at, rows, cols), closed, keep, main2, macro)
        both = [streamed(at, pl.ds(ny, SUB), cols) for at in range(2)]
        keep = merge([retain[plane, :, cols] for plane, _ in sides])
        closed = merge([solid[plane, :, cols] for plane, _ in sides]) > 0.5
        out, _ = collide([merge(pair) for pair in zip(*both)], keep)
        for i in range(27):
            value = jnp.where(closed, SOLID, out[i])
            halo2[i, 0, :, cols] = value
            halo2[i, 1, :, cols] = pltpu.roll(value, SUB // 2, 0)
    more = merge_named(own[...], wide)
    named[...] = jnp.concatenate([more, jnp.zeros(more.shape, F32)], axis=0).astype(BF16)
    pack_faces(main2, halo2, 1, 1, more, send_far, send_near)


def add_moments(sums, i, f):
    for m, sign in enumerate((1,) + STEP[i]):
        if sign:
            term = f if sign > 0 else -f
            sums[m] = term if sums[m] is None else sums[m] + term


def respond(planes, radiation, pick, fields):
    for p, rows in enumerate(planes):
        ny = rows[0].shape[0]
        for m in range(4):
            fields[m, pl.ds(p * ny, ny), :] = rows[m].astype(BF16)
    parts = []
    for m in range(4):
        total = None
        for h in range(pick.shape[0]):
            term = jnp.dot(pick[h, :, :], fields[m, :, pl.ds(LANES * h, LANES)], preferred_element_type=F32)
            total = term if total is None else total + term
        parts.append(total)
    surface = jnp.concatenate(parts, axis=1).astype(BF16)
    response = jnp.dot(surface, radiation[...], preferred_element_type=F32)
    return response.astype(BF16)


def slots_kernel(size_y, bins, radiation, counts, sites, patches, pick, level, own_bins, turned_radiation):
    halves, slots, lines = pick.shape
    slot = lax.broadcasted_iota(jnp.int32, (slots, lines), 0)
    line = lax.broadcasted_iota(jnp.int32, (slots, lines), 1)
    wanted = jnp.full((slots, lines), -1, jnp.int32)
    for k in range(slots):
        site = jnp.where(k < counts[0, 0], sites[0, 0, k], -halves)
        wanted = jnp.where(slot == k, site, wanted)
    for h in range(halves):
        pick[h, :, :] = (wanted == line * halves + h).astype(BF16)

    n_patch = bins.shape[1]
    slot = lax.broadcasted_iota(jnp.int32, (slots, n_patch), 0)
    named = lax.broadcasted_iota(jnp.int32, (slots, n_patch), 1)
    wanted = jnp.full((slots, n_patch), -1, jnp.int32)
    for k in range(slots):
        wanted = jnp.where(slot == k, patches[0, 0, k], wanted)
    chosen = (wanted == named).astype(BF16)
    per_block = lax.dot_general(
        chosen, bins[...].astype(F32).astype(BF16), (((1,), (1,)), ((), ())), preferred_element_type=F32
    )
    devices, _, width = level.shape
    groups = slots // SUB
    group = lax.broadcasted_iota(jnp.int32, (SUB, width), 1) // (width // groups)
    tiles = {}
    for d in range(devices):
        blk = d * width // OBS_BLK
        if blk not in tiles:
            tile = None
            for g in range(groups):
                column = per_block[SUB * g : SUB * (g + 1), blk : blk + 1]
                column = jnp.broadcast_to(column, (SUB, width))
                tile = column if tile is None else jnp.where(group == g, column, tile)
            tiles[blk] = tile.astype(BF16)
        level[d, :, :] = tiles[blk]

    place = lax.axis_index("gx") * size_y + lax.axis_index("gy")
    mine = bins[pl.ds(lax.div(place * width, OBS_BLK), 1), :].astype(F32)
    own_bins[...] = jnp.broadcast_to(mine, own_bins.shape).astype(BF16)

    observers, terms = radiation.shape

    def body(k, carry):
        rows = pl.ds(pl.multiple_of(k * terms, terms), terms)
        turned_radiation[:, rows] = radiation[rows, :].T
        return carry

    lax.fori_loop(0, observers // terms, body, 0)


def last_early_kernel(
    main_in, halo_in, main_out, halo_out, pops, walls, macro_in, macro_out, radiation, pick,
    out, spare, part, inner, send, g_out, fields, sems,
):
    planes, ny, _ = walls.shape
    last = planes - 1
    places = [(main_out, halo_out, 0)]
    places += [(main_in, halo_in, p) for p in range(planes - 2)]
    places += [(main_out, halo_out, 1)]
    load = loader(planes, ny, places)
    copies = []
    for plane in (0, last, *range(1, last)):
        own = walls[plane, :, :] == 1
        edge = {0: 0, last: 1}.get(plane)
        sums = [None] * 4
        for i in range(27):
            if 0 <= plane - STEP[i][0] <= last:
                value = pull(load, i, plane)[:ny]
                g = jnp.where(own, pops[i, plane, :, :], value * (1.0 / WEIGHT[i]))
                g_out[i, plane, :, :] = g
                add_moments(sums, i, g * WEIGHT[i])
            else:
                bounced = load(26 - i, plane)[:ny]
                spare[edge, i % 9, :, :] = jnp.where(own, pops[i, plane, :, :] * WEIGHT[i], bounced)
        for m in range(4):
            if edge is None:
                inner[m, plane - 1, :, :] = sums[m] - 1.0 if m == 0 else sums[m]
            else:
                part[m, edge, :, :] = sums[m]
        span = pl.ds((0, 9)[edge], 18) if edge is not None else pl.ds(0, 27)
        copies += start_all(
            [pltpu.make_async_copy(g_out.at[span, plane], out.at[span, plane], sems.at[len(copies)])]
        )
    rows = [[macro_out[m, 0, :, :] for m in range(4)]]
    rows += [[macro_in[m, p, :, :] for m in range(4)] for p in range(planes - 2)]
    rows += [[macro_out[m, 1, :, :] for m in range(4)]]
    response = respond(rows, radiation, pick, fields)
    devices, _, width = send.shape
    for d in range(devices):
        send[d, :, :] = response[:, d * width : (d + 1) * width]
    for copy in copies:
        copy.wait()


def last_kernel(
    far, near, walls, spare, part, inner, radiation, pick, early, level, own, across, started,
    out, send, named, g_out, fields, wide, sems,
):
    planes, ny, _ = walls.shape
    last = planes - 1
    widen(far, near, wide, "gx")
    load = loader(planes, ny, None, wide)
    rows, copies = {}, []
    for edge, (plane, first) in enumerate(((0, 18), (last, 0))):
        own = walls[plane, :, :] == 1
        sums = [part[m, edge, :, :] for m in range(4)]
        for k in range(9):
            i = first + k
            value = turned(load(i, plane - STEP[i][0]), i)[:ny]
            f = jnp.where(own | (value > LIMIT), spare[edge, k, :, :], value)
            g_out[k, edge, :, :] = f * (1.0 / WEIGHT[i])
            add_moments(sums, i, f)
        rows[plane] = [sums[0] - 1.0, *sums[1:]]
        copies += start_all(
            [pltpu.make_async_copy(g_out.at[:, edge], out.at[pl.ds(first, 9), plane], sems.at[edge])]
        )
    for p in range(planes - 2):
        rows[p + 1] = [inner[m, p, :, :] for m in range(4)]
    response = respond([rows[p] for p in range(planes)], radiation, pick, fields)
    devices, _, width = send.shape
    slots = early.shape[1]
    for d in range(devices):
        send[d, pl.ds(0, slots), :] = early[d, :, :]
        send[d, pl.ds(slots, slots), :] = response[:, d * width : (d + 1) * width]
        if send.shape[1] > 2 * slots:
            send[d, pl.ds(2 * slots, SUB), :] = level[d, :, :]
    named[...] = merge_named(own[...].astype(F32)[:SUB], wide, across[...].astype(F32)[:SUB])
    for copy in copies:
        copy.wait()


def bin_named_kernel(received, named, own_bins, signal, hits, known):
    devices, rows, width = received.shape
    slots = rows // 2
    groups = slots // SUB
    patch = lax.broadcasted_iota(jnp.int32, (slots, known.shape[-1]), 1).astype(F32) + 1.0
    for d in range(devices):
        columns = [named[:, groups * d + g : groups * d + g + 1] for g in range(groups)]
        ids = jnp.concatenate([jnp.broadcast_to(c, (SUB, patch.shape[1])) for c in columns], axis=0)
        known[d, :, :] = (ids == patch).astype(F32).astype(BF16)
    flat = known[...].reshape(devices * slots, patch.shape[1])
    level = lax.dot_general(flat, own_bins[...], (((1,), (1,)), ((), ())), preferred_element_type=F32)
    lane = lax.broadcasted_iota(jnp.int32, level.shape, 1).astype(F32)
    for step in range(2):
        hit = (level == lane - float(step)).astype(F32).astype(BF16)
        hits[:, pl.ds(step * slots, slots), :] = hit.reshape(devices, slots, LEVELS)
    left = received[...].reshape(devices * rows, width)
    right = hits[...].reshape(devices * rows, LEVELS)
    signal[...] = lax.dot_general(left, right, (((0,), (0,)), ((), ())), preferred_element_type=F32)


def bin_kernel(received, signal, hits):
    devices, rows, width = received.shape
    slots = (rows - SUB) // 2
    groups = slots // SUB
    lane = lax.broadcasted_iota(jnp.int32, (slots, LEVELS), 1).astype(F32)
    for d in range(devices):
        tile = received[d, pl.ds(2 * slots, SUB), :].astype(F32)
        starts = [g * (width // groups) for g in range(groups)]
        level = jnp.concatenate([jnp.broadcast_to(tile[:, k : k + 1], (SUB, LEVELS)) for k in starts], axis=0)
        for step in range(2):
            hit = (level == lane - float(step)).astype(F32).astype(BF16)
            hits[d, pl.ds(step * slots, slots), :] = hit
    left = received[:, pl.ds(0, 2 * slots), :].reshape(devices * 2 * slots, width)
    right = hits[...].reshape(devices * 2 * slots, LEVELS)
    signal[...] = lax.dot_general(left, right, (((0,), (0,)), ((), ())), preferred_element_type=F32)


def per_device(populations, omega, walls, radiation, bins, counts, sample_site, sample_patch):
    _, planes, ny, nz = populations.shape
    slots = sample_site.shape[-1]
    size_x, size_y = lax.axis_size("gx"), lax.axis_size("gy")
    devices = size_x * size_y
    width = radiation.shape[0] // devices

    def swap(far, near, axis, size):
        far_pairs = [(i, (i - 1 + 2 * (i % 2)) % size) for i in range(size)]
        near_pairs = [(i, i + 1 - 2 * (i % 2)) for i in range(size)]
        return lax.ppermute(far, axis, far_pairs), lax.ppermute(near, axis, near_pairs)

    dma = pltpu.SemaphoreType.DMA
    block, cells = populations.shape, (planes, ny, nz)
    beside = (20 * SUB, nz)
    far, near, own = call(
        functools.partial(rows_kernel, size_y),
        [HBM] * 4,
        [(VMEM, beside, BF16)] * 2 + [(VMEM, (2 * SUB, nz), BF16)],
        [
            pltpu.VMEM(block, F32), pltpu.VMEM(cells, F32), pltpu.VMEM(cells, walls.dtype),
            pltpu.VMEM(sample_patch.shape, sample_patch.dtype),
            pltpu.VMEM((2, 29, SUB, nz), F32), pltpu.VMEM((2, *beside), F32), dma((2, 9)),
        ],
        cost=1 << 20,
        limit=64800000,
    )(populations, omega, walls, sample_patch)
    far, near = swap(far, near, "gy", size_y)
    across = lax.ppermute(own, "gy", [(i, (i + size_y // 2) % size_y) for i in range(size_y)])
    pick, level, own_bins, radiation = call(
        functools.partial(slots_kernel, size_y),
        [VMEM] * 2 + [SMEM] * 3,
        [
            (VMEM, (nz // LANES, slots, planes * ny), BF16),
            (VMEM, (devices, SUB, width), BF16),
            (VMEM, (LEVELS, bins.shape[0]), BF16),
            (VMEM, radiation.shape[::-1], BF16),
        ],
        cost=1 << 22,
    )(bins.T, radiation, counts, sample_site, sample_patch)
    (main,) = call(first_main_kernel, [VMEM] * 3, [(VMEM, block, F32)], cost=1 << 22)(populations, omega, walls)

    edge = (planes, SUB, nz)
    face, last_face = ((face_rows(ny, reach), nz) for reach in (2, 1))
    faces, last_faces = ([(VMEM, shape, BF16)] * 2 for shape in (face, last_face))
    halo, retain, solid, named, far, near = call(
        first_halo_kernel,
        [VMEM] * 5,
        [(VMEM, (27, *edge), F32), (VMEM, edge, F32), (VMEM, edge, F32), (VMEM, (SUB, nz), F32), *faces],
        [pltpu.VMEM((2, *beside), F32)],
        cost=1 << 20,
    )(far, near, main, own, across)
    far, near = swap(far, near, "gx", size_x)

    def relaxed(n):
        return [(VMEM, (27, n, ny, nz), F32), (VMEM, (27, n, SUB, nz), F32), (VMEM, (4, n, ny, nz), F32)]

    read = pltpu.VMEM((27, ny + SUB, nz), F32)
    wide, last_wide = (pltpu.VMEM((2, *shape), F32) for shape in (face, last_face))
    main_in, halo_in, macro_in, ready = call(
        middle_inner_kernel,
        [VMEM] * 7,
        relaxed(planes - 2) + [(VMEM, (27, 2, ny + SUB, nz), F32)],
        [read],
        cost=1 << 22,
    )(main, halo, populations, omega, walls, retain, solid)
    main_out, halo_out, macro_out, named, far, near = call(
        middle_outer_kernel,
        [VMEM] * 9,
        relaxed(2) + [(VMEM, (2 * SUB, nz), BF16), *last_faces],
        [pltpu.VMEM((9, 2, ny + SUB, nz), F32), wide],
        cost=1 << 22,
    )(ready, omega, walls, retain, solid, far, near, named, pick)
    far, near = swap(far, near, "gx", size_x)
    across = lax.ppermute(named, "gx", [(i, (i + size_x // 2) % size_x) for i in range(size_x)])

    fields = pltpu.VMEM((4, planes * ny, nz), BF16)
    inner = (4, planes - 2, ny, nz)
    started, spare, part, inner, early = call(
        last_early_kernel,
        [VMEM] * 10,
        [
            (HBM, block, F32),
            (VMEM, (2, 9, ny, nz), F32),
            (VMEM, (4, 2, ny, nz), F32),
            (VMEM, inner, F32),
            (VMEM, (devices, slots, width), BF16),
        ],
        [pltpu.VMEM(block, F32), fields, dma((planes,))],
        cost=1 << 22,
    )(main_in, halo_in, main_out, halo_out, populations, walls, macro_in, macro_out, radiation, pick)
    ride = (size_x, size_y) == (8, 4)
    sent = 2 * slots if ride else 2 * slots + SUB
    advanced, send, named = call(
        last_kernel,
        [VMEM] * 12 + [HBM],
        [(HBM, block, F32), (VMEM, (devices, sent, width), BF16), (VMEM, (SUB, nz), F32)],
        [pltpu.VMEM((9, 2, ny, nz), F32), fields, last_wide, dma((2,))],
        aliases={12: 0},
        cost=1 << 22,
    )(far, near, walls, spare, part, inner, radiation, pick, early, level, named, across, started)
    received = lax.all_to_all(send, ("gx", "gy"), 0, 0, tiled=True)
    hits = pltpu.VMEM((devices, 2 * slots, LEVELS), BF16)
    result = [(VMEM, (width, LEVELS), F32)]
    if ride:
        known = pltpu.VMEM((devices, slots, bins.shape[0]), BF16)
        (signal,) = call(bin_named_kernel, [VMEM] * 3, result, [hits, known], cost=1 << 20)(received, named, own_bins)
    else:
        (signal,) = call(bin_kernel, [VMEM], result, [hits], cost=1 << 20)(received)
    return advanced, signal


def solution(mesh):
    return jax.shard_map(
        per_device,
        mesh=mesh,
        in_specs=(
            P(None, "gx", "gy", None),
            P("gx", "gy", None),
            P("gx", "gy", None),
            P(),
            P(),
            P("gx", "gy"),
            P("gx", "gy", None),
            P("gx", "gy", None),
        ),
        out_specs=(P(None, "gx", "gy", None), P(("gx", "gy"), None)),
        check_vma=False,
    )
```

```python
import functools

import jax
import jax.numpy as jnp
from jax import lax
from jax.experimental import pallas as pl
from jax.experimental.pallas import tpu as pltpu
from jax.sharding import PartitionSpec as P

F32 = jnp.float32
BF16 = jnp.bfloat16
LEVELS = 128
OBS_BLK = 128
SOLID = 1e30
LIMIT = 1e29
LANES = 128
SUB = 8

WEIGHT = [
    (8.0 / 27.0, 2.0 / 27.0, 1.0 / 54.0, 1.0 / 216.0)[
        int(i // 9 != 1) + int(i // 3 % 3 != 1) + int(i % 3 != 1)
    ]
    for i in range(27)
]
STEP = [(i // 9 - 1, i // 3 % 3 - 1, i % 3 - 1) for i in range(27)]
VMEM = pl.BlockSpec(memory_space=pltpu.VMEM)
SMEM = pl.BlockSpec(memory_space=pltpu.SMEM)
HBM = pl.BlockSpec(memory_space=pltpu.HBM)


def call(kernel, in_specs, out, scratch=(), aliases=None, cost=0, limit=14 * 1024 * 1024):
    return pl.pallas_call(
        kernel,
        out_shape=[jax.ShapeDtypeStruct(shape, dtype) for _, shape, dtype in out],
        in_specs=in_specs,
        out_specs=[spec for spec, _, _ in out],
        scratch_shapes=list(scratch),
        input_output_aliases=aliases or {},
        compiler_params=pltpu.CompilerParams(vmem_limit_bytes=limit),
        cost_estimate=pl.CostEstimate(flops=cost, bytes_accessed=cost, transcendentals=0),
    )


def raw_moments(f):
    s, d, e = [], [], []
    for k in range(9):
        low, mid, high = f[3 * k : 3 * k + 3]
        ends = high + low
        s.append(ends + mid)
        d.append(high - low)
        e.append(ends)
    s_y, dy, ey, dz, dyz, ez = [], [], [], [], [], []
    for a in range(3):
        ends = s[3 * a + 2] + s[3 * a]
        s_y.append(ends + s[3 * a + 1])
        dy.append(s[3 * a + 2] - s[3 * a])
        ey.append(ends)
        dz.append(d[3 * a] + d[3 * a + 1] + d[3 * a + 2])
        dyz.append(d[3 * a + 2] - d[3 * a])
        ez.append(e[3 * a] + e[3 * a + 1] + e[3 * a + 2])
    m200 = s_y[2] + s_y[0]
    rho = m200 + s_y[1]
    jx = s_y[2] - s_y[0]
    jy = dy[0] + dy[1] + dy[2]
    jz = dz[0] + dz[1] + dz[2]
    m020 = ey[0] + ey[1] + ey[2]
    m002 = ez[0] + ez[1] + ez[2]
    m110 = dy[2] - dy[0]
    m101 = dz[2] - dz[0]
    m011 = dyz[0] + dyz[1] + dyz[2]
    return rho, jx, jy, jz, m200, m020, m002, m110, m101, m011


def unshift(k0, k1, k2, v, v2, vv, vp, vm):
    if k0 is None and k2 is None:
        return vm * k1, -(v2 * k1), vp * k1
    diff = v * k0
    ends = vv * k0
    if k1 is not None:
        diff = diff + k1
        ends = ends + v2 * k1
    if k2 is not None:
        ends = ends + k2
    high = 0.5 * (ends + diff)
    return high - diff, k0 - ends, high


def collide(f, retain):
    rho, jx, jy, jz, m200, m020, m002, m110, m101, m011 = raw_moments(f)
    inv = 1.0 / rho
    ux, uy, uz = jx * inv, jy * inv, jz * inv
    k200, k020, k002 = m200 - jx * ux, m020 - jy * uy, m002 - jz * uz
    third = 1.0 / 3.0
    d1 = retain * (k200 - k020)
    d2 = retain * (k200 - k002)
    xx = (rho + d1 + d2) * third
    yy = xx - d1
    zz = xx - d2
    xy = retain * (m110 - jx * uy)
    xz = retain * (m101 - jx * uz)
    yz = retain * (m011 - jy * uz)
    xy2, xz2, yz2 = 2.0 * xy, 2.0 * xz, 2.0 * yz
    xyi, xzi, yzi = xy2 * inv, xz2 * inv, yz2 * inv
    xxi = xx * inv
    yyi = yy * inv
    q_xy, q_xz, q_yz = xy * xyi, xz * xzi, yz * yzi
    xxyy = xxi * yy + q_xy
    xxzz = xxi * zz + q_xz
    yyzz = yyi * zz + q_yz
    xxyz = xxi * yz + xy * xzi
    xyyz = yyi * xz + xy * yzi
    xyzz = (zz * inv) * xy + xz * yzi
    full = xxi * (yyi * zz + q_yz) + (yyi * q_xz + (zz * inv) * q_xy) + (2.0 * xyi) * (xz * yzi)
    table = {
        (0, 0): (rho, None, xx),
        (1, 0): (None, xy, None),
        (2, 0): (yy, None, xxyy),
        (0, 1): (None, xz, None),
        (1, 1): (yz, None, xxyz),
        (2, 1): (None, xyyz, None),
        (0, 2): (zz, None, xxzz),
        (1, 2): (None, xyzz, None),
        (2, 2): (yyzz, None, full),
    }

    def speeds(v):
        return v, 2.0 * v, v * v, v + 0.5, v - 0.5

    sx, sy, sz = speeds(ux), speeds(uy), speeds(uz)
    after_x = {}
    for (b, c), ks in table.items():
        for a, value in enumerate(unshift(*ks, *sx)):
            after_x[a, b, c] = value
    out = [None] * 27
    for a in range(3):
        after_y = {}
        for c in range(3):
            triple = unshift(*(after_x[a, b, c] for b in range(3)), *sy)
            for b, value in enumerate(triple):
                after_y[b, c] = value
        for b in range(3):
            triple = unshift(*(after_y[b, c] for c in range(3)), *sz)
            for c, value in enumerate(triple):
                out[9 * a + 3 * b + c] = value
    return out, (rho, jx, jy, jz)


def odd_block(axis):
    return lax.rem(lax.axis_index(axis), 2)


def widen(far, near, wide, axis):
    odd = odd_block(axis)
    wide[odd, :, :] = far[...].astype(F32)
    wide[1 - odd, :, :] = near[...].astype(F32)


def merge_named(own, wide, *others):
    named = own
    for more in (wide[0, pl.ds(wide.shape[1] - SUB, SUB), :], wide[1, pl.ds(wide.shape[1] - SUB, SUB), :], *others):
        named = jnp.maximum(named, more)
    return named


def start_all(copies):
    for copy in copies:
        copy.start()
    return copies


def rows_order(side):
    outward = 1 - 2 * side
    both = [i for i in range(27) if STEP[i][1] == outward]
    return both, [i for i in range(27) if STEP[i][1] != outward]


def named_tile(patches, place, nz):
    slots = patches.shape[-1]
    groups = slots // SUB
    ids = jnp.broadcast_to(patches[0, :, :].astype(F32) + 1.0, (SUB, slots))
    row = lax.broadcasted_iota(jnp.int32, (SUB, slots), 0)
    slot = lax.broadcasted_iota(jnp.int32, (SUB, slots), 1)
    lane = lax.broadcasted_iota(jnp.int32, (SUB, nz), 1)
    tile = jnp.zeros((SUB, nz), F32)
    for g in range(groups):
        column = jnp.sum(jnp.where(slot == SUB * g + row, ids, 0.0), axis=1, keepdims=True)
        tile = jnp.where(lane == place * groups + g, column, tile)
    return tile


def rows_kernel(
    size_y, pops_in, omega_in, walls_in, patches_in, far, near, own,
    pops, omega, walls, patches, packed, faces, sems,
):
    planes, ny, nz = omega.shape
    row = lax.broadcasted_iota(jnp.int32, (SUB, nz), 0)
    chunk = 4
    spans = [pl.ds(i, min(chunk, 27 - i)) for i in range(0, 27, chunk)]
    cells = [
        pltpu.make_async_copy(omega_in, omega, sems.at[0, len(spans)]),
        pltpu.make_async_copy(walls_in, walls, sems.at[1, len(spans)]),
        pltpu.make_async_copy(patches_in, patches, sems.at[0, len(spans) + 1]),
    ]
    copies = [
        pltpu.make_async_copy(pops_in.at[span, :, rows, :], pops.at[span, :, rows, :], sems.at[side, k])
        for k, span in enumerate(spans)
        for side, rows in enumerate((pl.ds(0, 2), pl.ds(ny - 2, 2)))
    ]
    start_all(cells + copies)

    def read(group, plane, first):
        part = pl.ds(first, SUB)
        if group < 27:
            return pops[group, plane, part, :]
        if group == 27:
            return 1.0 - omega[plane, part, :]
        return walls[plane, part, :].astype(F32)

    def pack(group):
        for side, first, at in ((0, ny - SUB, SUB - 2), (1, 0, 0)):
            tile = None
            for plane in range(planes):
                turn = (2 * plane - at) % SUB
                piece = read(group, plane, first)
                piece = pltpu.roll(piece, turn, 0) if turn else piece
                tile = piece if tile is None else jnp.where(row // 2 == plane, piece, tile)
            packed[side, group, :, :] = tile

    for copy in cells:
        copy.wait()
    pack(27)
    pack(28)
    named = named_tile(patches, lax.axis_index("gx") * size_y + lax.axis_index("gy"), nz)
    own[...] = jnp.concatenate([named, jnp.zeros((SUB, nz), F32)], axis=0).astype(BF16)
    for i in range(27):
        if i % chunk == 0:
            for copy in copies[i // chunk * 2 : i // chunk * 2 + 2]:
                copy.wait()
        pack(i)
    for side in range(2):
        for part in range(nz // LANES):
            cols = pl.ds(LANES * part, LANES)
            closed = packed[side, 28, :, cols] > 0.5
            f = [packed[side, i, :, cols] * WEIGHT[i] for i in range(27)]
            relaxed, _ = collide(f, packed[side, 27, :, cols])
            for i in range(27):
                packed[side, i, :, cols] = jnp.where(closed, SOLID, relaxed[i]) * (1.0 / WEIGHT[i]) - 1.0
        both, edge = rows_order(side)
        edge = edge + [27, 28]
        tiles = [packed[side, i, :, :] for i in both]
        for k in range(0, len(edge), 2):
            one, two = (packed[side, i, :, :] for i in edge[k : k + 2])
            at_edge = row % 2 == 1 - side
            tiles.append(jnp.where(at_edge, one, pltpu.roll(two, SUB - 1 if side == 0 else 1, 0)))
        tiles.append(named)
        for k, tile in enumerate(tiles):
            faces[side, pl.ds(SUB * k, SUB), :] = tile
    odd = odd_block("gy")
    far[...] = faces[1 - odd, :, :].astype(BF16)
    near[...] = faces[odd, :, :].astype(BF16)


def first_main_kernel(pops, omega, walls, post):
    planes, ny, nz = omega.shape

    def body(plane, carry):
        for t in range(ny // SUB):
            for part in range(nz // LANES):
                at = (plane, pl.ds(SUB * t, SUB), pl.ds(LANES * part, LANES))
                f = [pops[(i, *at)] * WEIGHT[i] for i in range(27)]
                closed = walls[at] == 1
                out, _ = collide(f, 1.0 - omega[at])
                for i in range(27):
                    post[(i, *at)] = jnp.where(closed, SOLID, out[i])
        return carry

    lax.fori_loop(0, planes, body, 0)


def corner_rows(reach):
    places = {}
    for k in range(9):
        sy, j = STEP[k][1], k % 3
        if reach == 2:
            rows = {1: ((6, 6), (7, 7)), 0: ((7, 3), (0, 4)), -1: ((0, 0), (1, 1))}[sy]
            places[k] = [(ring, j, at) for ring, at in rows]
        else:
            places[k] = {1: [(7, 0, j)], 0: [], -1: [(0, 0, 3 + j)]}[sy]
    return places


def face_rows(ny, reach):
    return 9 * ny + (4 if reach == 2 else 2) * SUB


def pack_x(main, halo, plane, first, reach, named, out):
    ny, nz = main.shape[2:]
    row = lax.broadcasted_iota(jnp.int32, (SUB, nz), 0)
    scaled = lambda ref, k: ref[first + k, plane, :, :] * (1.0 / WEIGHT[k]) - 1.0
    for k in range(9):
        out[pl.ds(ny * k, ny), :] = scaled(main, k).astype(BF16)
    tiles = [jnp.zeros((SUB, nz), F32) for _ in range((out.shape[0] - 9 * ny) // SUB)]
    for k, places in corner_rows(reach).items():
        for ring, tile, at in places:
            turn = (at - ring) % SUB
            value = scaled(halo, k)
            value = pltpu.roll(value, turn, 0) if turn else value
            tiles[tile] = jnp.where(row == at, value, tiles[tile])
    tiles[-1] = named
    out[pl.ds(9 * ny, SUB * len(tiles)), :] = jnp.concatenate(tiles, axis=0).astype(BF16)


def pack_faces(main, halo, last, reach, named, far, near):
    odd = odd_block("gx")
    pack_x(main, halo, odd * last, odd * 18, reach, named, far)
    pack_x(main, halo, (1 - odd) * last, (1 - odd) * 18, reach, named, near)


def first_halo_kernel(near, far, main, own, across, halo, retain, solid, named, send_far, send_near, wide):
    _, planes, _, nz = halo.shape
    row = lax.broadcasted_iota(jnp.int32, (SUB, nz), 0)
    widen(far, near, wide, "gy")

    def received(side, group, plane):
        both, edge = rows_order(side)
        edge = edge + [27, 28]
        turn = (SUB - 2, 0)[side] - 2 * plane
        if group in both:
            tile = both.index(group)
        else:
            k = edge.index(group)
            tile = len(both) + k // 2
            turn += (k % 2) * (1 - 2 * side)
        value = wide[side, pl.ds(SUB * tile, SUB), :]
        return pltpu.roll(value, turn % SUB, 0) if turn % SUB else value

    def beside(group, plane):
        return jnp.where(row < 4, received(1, group, plane), received(0, group, plane))

    for plane in range(planes):
        retain[plane, :, :] = beside(27, plane)
        solid[plane, :, :] = beside(28, plane)
        for i in range(27):
            halo[i, plane, :, :] = (beside(i, plane) + 1.0) * WEIGHT[i]
    named[...] = merge_named(own[...].astype(F32)[:SUB], wide, across[...].astype(F32)[:SUB])
    pack_faces(main, halo, planes - 1, 2, named[...], send_far, send_near)


def turned(value, i):
    _, sy, sz = STEP[i]
    if sy:
        value = pltpu.roll(value, sy % value.shape[0], 0)
    if sz:
        value = pltpu.roll(value, sz % value.shape[1], 1)
    return value


def pull(load, i, plane):
    value = turned(load(i, plane - STEP[i][0]), i)
    return jnp.where(value > LIMIT, load(26 - i, plane), value)


def loader(planes, ny, places, wide=None):
    def load(i, plane):
        if 0 <= plane < planes:
            main, halo, at = places[plane]
            return jnp.concatenate([main[i, at, :, :], halo[i, at, :, :]], axis=0)
        side, k = (0, i - 18) if plane < 0 else (1, i)
        reach = 2 if wide.shape[1] == face_rows(ny, 2) else 1
        used = corner_rows(reach)[k]
        if used:
            ring, tile, at = used[0]
            halo = wide[side, pl.ds(9 * ny + SUB * tile, SUB), :]
            halo = pltpu.roll(halo, (ring - at) % SUB, 0) if ring != at else halo
        else:
            halo = jnp.zeros((SUB, wide.shape[2]), F32)
        both = jnp.concatenate([wide[side, pl.ds(ny * k, ny), :], halo], axis=0)
        return (both + 1.0) * WEIGHT[i]

    return load


def collide_rows(at, t, f, closed, keep, main2, macro):
    rows, cols = t
    out, sums = collide(f, keep)
    for i in range(27):
        main2[i, at, rows, cols] = jnp.where(closed, SOLID, out[i])
    macro[0, at, rows, cols] = sums[0] - 1.0
    for m in range(1, 4):
        macro[m, at, rows, cols] = sums[m]


def middle_inner_kernel(main, halo, pops, omega, walls, retain, solid, main2, halo2, macro, ready, read):
    planes, ny, nz = omega.shape
    last = planes - 1
    load = loader(planes, ny, [(main, halo, p) for p in range(planes)])
    for plane in (*range(1, last), 0, last):
        inside = 0 < plane < last
        own = walls[plane, :, :] == 1
        for i in range(27):
            value = pull(load, i, plane) if 0 <= plane - STEP[i][0] <= last else load(26 - i, plane)
            value = [jnp.where(own, pops[i, plane, :, :] * WEIGHT[i], value[:ny]), value[ny:]]
            for rows, part in zip((pl.ds(0, ny), pl.ds(ny, SUB)), value):
                if inside:
                    read[i, rows, :] = part
                else:
                    ready[i, int(plane > 0), rows, :] = part
        if not inside:
            continue
        at = plane - 1
        for part in range(nz // LANES):
            cols = pl.ds(LANES * part, LANES)
            for t in range(ny // SUB):
                rows = pl.ds(SUB * t, SUB)
                f = [read[i, rows, cols] for i in range(27)]
                closed = walls[plane, rows, cols] == 1
                collide_rows(at, (rows, cols), f, closed, 1.0 - omega[plane, rows, cols], main2, macro)
            out, _ = collide([read[i, pl.ds(ny, SUB), cols] for i in range(27)], retain[plane, :, cols])
            closed = solid[plane, :, cols] > 0.5
            for i in range(27):
                halo2[i, at, :, cols] = jnp.where(closed, SOLID, out[i])


def middle_outer_kernel(
    ready, omega, walls, retain, solid, far, near, own, _,
    main2, halo2, macro, named, send_far, send_near, read, wide,
):
    planes, ny, nz = omega.shape
    last = planes - 1
    widen(far, near, wide, "gx")
    load = loader(planes, ny, None, wide)
    sides = ((0, 18), (last, 0))
    for at, (plane, first) in enumerate(sides):
        solid_cell = walls[plane, :, :] == 1
        for k in range(9):
            value = turned(load(first + k, plane - STEP[first + k][0]), first + k)
            spare = ready[first + k, at, :, :]
            shut = value > LIMIT
            read[k, at, pl.ds(0, ny), :] = jnp.where(solid_cell | shut[:ny], spare[:ny], value[:ny])
            read[k, at, pl.ds(ny, SUB), :] = jnp.where(shut[ny:], spare[ny:], value[ny:])

    def streamed(at, rows, cols):
        first = sides[at][1]
        return [
            read[i - first, at, rows, cols] if 0 <= i - first < 9 else ready[i, at, rows, cols] for i in range(27)
        ]

    row = lax.broadcasted_iota(jnp.int32, (SUB, LANES), 0)
    edge = (row == 0) | (row == SUB - 1)
    merge = lambda pair: jnp.where(edge, pair[0], pltpu.roll(pair[1], SUB // 2, 0))
    for part in range(nz // LANES):
        cols = pl.ds(LANES * part, LANES)
        for at, (plane, _) in enumerate(sides):
            for t in range(ny // SUB):
                rows = pl.ds(SUB * t, SUB)
                closed = walls[plane, rows, cols] == 1
                keep = 1.0 - omega[plane, rows, cols]
                collide_rows(at, (rows, cols), streamed(at, rows, cols), closed, keep, main2, macro)
        both = [streamed(at, pl.ds(ny, SUB), cols) for at in range(2)]
        keep = merge([retain[plane, :, cols] for plane, _ in sides])
        closed = merge([solid[plane, :, cols] for plane, _ in sides]) > 0.5
        out, _ = collide([merge(pair) for pair in zip(*both)], keep)
        for i in range(27):
            value = jnp.where(closed, SOLID, out[i])
            halo2[i, 0, :, cols] = value
            halo2[i, 1, :, cols] = pltpu.roll(value, SUB // 2, 0)
    more = merge_named(own[...], wide)
    named[...] = jnp.concatenate([more, jnp.zeros(more.shape, F32)], axis=0).astype(BF16)
    pack_faces(main2, halo2, 1, 1, more, send_far, send_near)


def add_moments(sums, i, f):
    for m, sign in enumerate((1,) + STEP[i]):
        if sign:
            term = f if sign > 0 else -f
            sums[m] = term if sums[m] is None else sums[m] + term


def respond(planes, radiation, pick, fields):
    for p, rows in enumerate(planes):
        ny = rows[0].shape[0]
        for m in range(4):
            fields[m, pl.ds(p * ny, ny), :] = rows[m].astype(BF16)
    parts = []
    for m in range(4):
        total = None
        for h in range(pick.shape[0]):
            term = jnp.dot(pick[h, :, :], fields[m, :, pl.ds(LANES * h, LANES)], preferred_element_type=F32)
            total = term if total is None else total + term
        parts.append(total)
    surface = jnp.concatenate(parts, axis=1).astype(BF16)
    response = jnp.dot(surface, radiation[...], preferred_element_type=F32)
    return response.astype(BF16)


def fill_levels(per_block, level):
    devices, _, width = level.shape
    slots = per_block.shape[0]
    groups = slots // SUB
    group = lax.broadcasted_iota(jnp.int32, (SUB, width), 1) // (width // groups)
    tiles = {}
    for d in range(devices):
        blk = d * width // OBS_BLK
        if blk not in tiles:
            tile = None
            for g in range(groups):
                column = per_block[SUB * g : SUB * (g + 1), blk : blk + 1]
                column = jnp.broadcast_to(column, (SUB, width))
                tile = column if tile is None else jnp.where(group == g, column, tile)
            tiles[blk] = tile.astype(BF16)
        level[d, :, :] = tiles[blk]


def slots_kernel(size_y, ride, bins, radiation, counts, sites, patches, pick, level, own_bins, turned_radiation):
    halves, slots, lines = pick.shape
    slot = lax.broadcasted_iota(jnp.int32, (slots, lines), 0)
    line = lax.broadcasted_iota(jnp.int32, (slots, lines), 1)
    wanted = jnp.full((slots, lines), -1, jnp.int32)
    for k in range(slots):
        wanted = jnp.where(slot == k, sites[0, 0, k], wanted)
    wanted = jnp.where(slot < jnp.broadcast_to(counts[...], slot.shape), wanted, -halves)
    for h in range(halves):
        pick[h, :, :] = (wanted == line * halves + h).astype(BF16)

    n_patch = bins.shape[1]
    slot = lax.broadcasted_iota(jnp.int32, (slots, n_patch), 0)
    named = lax.broadcasted_iota(jnp.int32, (slots, n_patch), 1)
    wanted = jnp.full((slots, n_patch), -1, jnp.int32)
    for k in range(slots):
        wanted = jnp.where(slot == k, patches[0, 0, k], wanted)
    chosen = (wanted == named).astype(BF16)
    per_block = lax.dot_general(
        chosen, bins[...].astype(F32).astype(BF16), (((1,), (1,)), ((), ())), preferred_element_type=F32
    )
    devices, _, width = level.shape
    if not ride:
        fill_levels(per_block, level)
    place = lax.axis_index("gx") * size_y + lax.axis_index("gy")
    mine = bins[pl.ds(lax.div(place * width, OBS_BLK), 1), :].astype(F32)
    own_bins[...] = jnp.broadcast_to(mine, own_bins.shape).astype(BF16)

    observers, terms = radiation.shape

    def body(k, carry):
        rows = pl.ds(pl.multiple_of(k * terms, terms), terms)
        turned_radiation[:, rows] = radiation[rows, :].T
        return carry

    lax.fori_loop(0, observers // terms, body, 0)


def last_early_kernel(
    main_in, halo_in, main_out, halo_out, pops, walls, macro_in, macro_out, radiation, pick,
    out, spare, part, inner, send, g_out, fields, sems,
):
    planes, ny, _ = walls.shape
    last = planes - 1
    places = [(main_out, halo_out, 0)]
    places += [(main_in, halo_in, p) for p in range(planes - 2)]
    places += [(main_out, halo_out, 1)]
    load = loader(planes, ny, places)
    copies = []
    for plane in (0, last, *range(1, last)):
        own = walls[plane, :, :] == 1
        edge = {0: 0, last: 1}.get(plane)
        sums = [None] * 4
        for i in range(27):
            if 0 <= plane - STEP[i][0] <= last:
                value = pull(load, i, plane)[:ny]
                g = jnp.where(own, pops[i, plane, :, :], value * (1.0 / WEIGHT[i]))
                g_out[i, plane, :, :] = g
                add_moments(sums, i, g * WEIGHT[i])
            else:
                bounced = load(26 - i, plane)[:ny]
                spare[edge, i % 9, :, :] = jnp.where(own, pops[i, plane, :, :] * WEIGHT[i], bounced)
        for m in range(4):
            if edge is None:
                inner[m, plane - 1, :, :] = sums[m] - 1.0 if m == 0 else sums[m]
            else:
                part[m, edge, :, :] = sums[m]
        span = pl.ds((0, 9)[edge], 18) if edge is not None else pl.ds(0, 27)
        copies += start_all(
            [pltpu.make_async_copy(g_out.at[span, plane], out.at[span, plane], sems.at[len(copies)])]
        )
    rows = [[macro_out[m, 0, :, :] for m in range(4)]]
    rows += [[macro_in[m, p, :, :] for m in range(4)] for p in range(planes - 2)]
    rows += [[macro_out[m, 1, :, :] for m in range(4)]]
    response = respond(rows, radiation, pick, fields)
    devices, _, width = send.shape
    for d in range(devices):
        send[d, :, :] = response[:, d * width : (d + 1) * width]
    for copy in copies:
        copy.wait()


def last_kernel(
    far, near, walls, spare, part, inner, radiation, pick, early, level, own, across, started,
    out, send, named, g_out, fields, wide, sems,
):
    planes, ny, _ = walls.shape
    last = planes - 1
    widen(far, near, wide, "gx")
    load = loader(planes, ny, None, wide)
    rows, copies = {}, []
    for edge, (plane, first) in enumerate(((0, 18), (last, 0))):
        own = walls[plane, :, :] == 1
        sums = [part[m, edge, :, :] for m in range(4)]
        for k in range(9):
            i = first + k
            value = turned(load(i, plane - STEP[i][0]), i)[:ny]
            f = jnp.where(own | (value > LIMIT), spare[edge, k, :, :], value)
            g_out[k, edge, :, :] = f * (1.0 / WEIGHT[i])
            add_moments(sums, i, f)
        rows[plane] = [sums[0] - 1.0, *sums[1:]]
        copies += start_all(
            [pltpu.make_async_copy(g_out.at[:, edge], out.at[pl.ds(first, 9), plane], sems.at[edge])]
        )
    for p in range(planes - 2):
        rows[p + 1] = [inner[m, p, :, :] for m in range(4)]
    response = respond([rows[p] for p in range(planes)], radiation, pick, fields)
    devices, _, width = send.shape
    slots = early.shape[1]
    for d in range(devices):
        send[d, pl.ds(0, slots), :] = early[d, :, :]
        send[d, pl.ds(slots, slots), :] = response[:, d * width : (d + 1) * width]
        if send.shape[1] > 2 * slots:
            send[d, pl.ds(2 * slots, SUB), :] = level[d, :, :]
    named[...] = merge_named(own[...].astype(F32)[:SUB], wide, across[...].astype(F32)[:SUB])
    for copy in copies:
        copy.wait()


def bin_named_kernel(received, named, own_bins, signal, hits, known):
    devices, rows, width = received.shape
    slots = rows // 2
    groups = slots // SUB
    patch = lax.broadcasted_iota(jnp.int32, (slots, known.shape[-1]), 1).astype(F32) + 1.0
    for d in range(devices):
        columns = [named[:, groups * d + g : groups * d + g + 1] for g in range(groups)]
        ids = jnp.concatenate([jnp.broadcast_to(c, (SUB, patch.shape[1])) for c in columns], axis=0)
        known[d, :, :] = (ids == patch).astype(F32).astype(BF16)
    flat = known[...].reshape(devices * slots, patch.shape[1])
    level = lax.dot_general(flat, own_bins[...], (((1,), (1,)), ((), ())), preferred_element_type=F32)
    lane = lax.broadcasted_iota(jnp.int32, level.shape, 1).astype(F32)
    for step in range(2):
        hit = (level == lane - float(step)).astype(F32).astype(BF16)
        hits[:, pl.ds(step * slots, slots), :] = hit.reshape(devices, slots, LEVELS)
    left = received[...].reshape(devices * rows, width)
    right = hits[...].reshape(devices * rows, LEVELS)
    signal[...] = lax.dot_general(left, right, (((0,), (0,)), ((), ())), preferred_element_type=F32)


def bin_kernel(received, signal, hits):
    devices, rows, width = received.shape
    slots = (rows - SUB) // 2
    groups = slots // SUB
    lane = lax.broadcasted_iota(jnp.int32, (slots, LEVELS), 1).astype(F32)
    for d in range(devices):
        tile = received[d, pl.ds(2 * slots, SUB), :].astype(F32)
        starts = [g * (width // groups) for g in range(groups)]
        level = jnp.concatenate([jnp.broadcast_to(tile[:, k : k + 1], (SUB, LEVELS)) for k in starts], axis=0)
        for step in range(2):
            hit = (level == lane - float(step)).astype(F32).astype(BF16)
            hits[d, pl.ds(step * slots, slots), :] = hit
    left = received[:, pl.ds(0, 2 * slots), :].reshape(devices * 2 * slots, width)
    right = hits[...].reshape(devices * 2 * slots, LEVELS)
    signal[...] = lax.dot_general(left, right, (((0,), (0,)), ((), ())), preferred_element_type=F32)


def per_device(populations, omega, walls, radiation, bins, counts, sample_site, sample_patch):
    _, planes, ny, nz = populations.shape
    slots = sample_site.shape[-1]
    size_x, size_y = lax.axis_size("gx"), lax.axis_size("gy")
    devices = size_x * size_y
    width = radiation.shape[0] // devices
    ride = (size_x, size_y) == (8, 4)

    def swap(far, near, axis, size):
        far_pairs = [(i, (i - 1 + 2 * (i % 2)) % size) for i in range(size)]
        near_pairs = [(i, i + 1 - 2 * (i % 2)) for i in range(size)]
        return lax.ppermute(far, axis, far_pairs), lax.ppermute(near, axis, near_pairs)

    dma = pltpu.SemaphoreType.DMA
    block, cells = populations.shape, (planes, ny, nz)
    beside = (20 * SUB, nz)
    far, near, own = call(
        functools.partial(rows_kernel, size_y),
        [HBM] * 4,
        [(VMEM, beside, BF16)] * 2 + [(VMEM, (2 * SUB, nz), BF16)],
        [
            pltpu.VMEM(block, F32), pltpu.VMEM(cells, F32), pltpu.VMEM(cells, walls.dtype),
            pltpu.VMEM(sample_patch.shape, sample_patch.dtype),
            pltpu.VMEM((2, 29, SUB, nz), F32), pltpu.VMEM((2, *beside), F32), dma((2, 9)),
        ],
        cost=1 << 20,
        limit=64800000,
    )(populations, omega, walls, sample_patch)
    far, near = swap(far, near, "gy", size_y)
    across = lax.ppermute(own, "gy", [(i, (i + size_y // 2) % size_y) for i in range(size_y)])
    pick, level, own_bins, radiation = call(
        functools.partial(slots_kernel, size_y, ride),
        [VMEM] * 3 + [SMEM] * 2,
        [
            (VMEM, (nz // LANES, slots, planes * ny), BF16),
            (VMEM, (devices, SUB, width), BF16),
            (VMEM, (LEVELS, bins.shape[0]), BF16),
            (VMEM, radiation.shape[::-1], BF16),
        ],
        cost=1 << 22,
    )(bins.T, radiation, counts, sample_site, sample_patch)
    (main,) = call(first_main_kernel, [VMEM] * 3, [(VMEM, block, F32)], cost=1 << 22)(populations, omega, walls)

    edge = (planes, SUB, nz)
    face, last_face = ((face_rows(ny, reach), nz) for reach in (2, 1))
    faces, last_faces = ([(VMEM, shape, BF16)] * 2 for shape in (face, last_face))
    halo, retain, solid, named, far, near = call(
        first_halo_kernel,
        [VMEM] * 5,
        [(VMEM, (27, *edge), F32), (VMEM, edge, F32), (VMEM, edge, F32), (VMEM, (SUB, nz), F32), *faces],
        [pltpu.VMEM((2, *beside), F32)],
        cost=1 << 20,
    )(near, far, main, own, across)
    far, near = swap(far, near, "gx", size_x)

    def relaxed(n):
        return [(VMEM, (27, n, ny, nz), F32), (VMEM, (27, n, SUB, nz), F32), (VMEM, (4, n, ny, nz), F32)]

    read = pltpu.VMEM((27, ny + SUB, nz), F32)
    wide, last_wide = (pltpu.VMEM((2, *shape), F32) for shape in (face, last_face))
    main_in, halo_in, macro_in, ready = call(
        middle_inner_kernel,
        [VMEM] * 7,
        relaxed(planes - 2) + [(VMEM, (27, 2, ny + SUB, nz), F32)],
        [read],
        cost=1 << 22,
    )(main, halo, populations, omega, walls, retain, solid)
    main_out, halo_out, macro_out, named, far, near = call(
        middle_outer_kernel,
        [VMEM] * 9,
        relaxed(2) + [(VMEM, (2 * SUB, nz), BF16), *last_faces],
        [pltpu.VMEM((9, 2, ny + SUB, nz), F32), wide],
        cost=1 << 22,
    )(ready, omega, walls, retain, solid, far, near, named, pick)
    far, near = swap(far, near, "gx", size_x)
    across = lax.ppermute(named, "gx", [(i, (i + size_x // 2) % size_x) for i in range(size_x)])

    fields = pltpu.VMEM((4, planes * ny, nz), BF16)
    inner = (4, planes - 2, ny, nz)
    started, spare, part, inner, early = call(
        last_early_kernel,
        [VMEM] * 10,
        [
            (HBM, block, F32),
            (VMEM, (2, 9, ny, nz), F32),
            (VMEM, (4, 2, ny, nz), F32),
            (VMEM, inner, F32),
            (VMEM, (devices, slots, width), BF16),
        ],
        [pltpu.VMEM(block, F32), fields, dma((planes,))],
        cost=1 << 22,
    )(main_in, halo_in, main_out, halo_out, populations, walls, macro_in, macro_out, radiation, pick)
    sent = 2 * slots if ride else 2 * slots + SUB
    advanced, send, named = call(
        last_kernel,
        [VMEM] * 12 + [HBM],
        [(HBM, block, F32), (VMEM, (devices, sent, width), BF16), (VMEM, (SUB, nz), F32)],
        [pltpu.VMEM((9, 2, ny, nz), F32), fields, last_wide, dma((2,))],
        aliases={12: 0},
        cost=1 << 22,
    )(far, near, walls, spare, part, inner, radiation, pick, early, level, named, across, started)
    received = lax.all_to_all(send, ("gx", "gy"), 0, 0, tiled=True)
    hits = pltpu.VMEM((devices, 2 * slots, LEVELS), BF16)
    result = [(VMEM, (width, LEVELS), F32)]
    if ride:
        known = pltpu.VMEM((devices, slots, bins.shape[0]), BF16)
        (signal,) = call(bin_named_kernel, [VMEM] * 3, result, [hits, known], cost=1 << 20)(received, named, own_bins)
    else:
        (signal,) = call(bin_kernel, [VMEM], result, [hits], cost=1 << 20)(received)
    return advanced, signal


def solution(mesh):
    return jax.shard_map(
        per_device,
        mesh=mesh,
        in_specs=(
            P(None, "gx", "gy", None),
            P("gx", "gy", None),
            P("gx", "gy", None),
            P(),
            P(),
            P("gx", "gy"),
            P("gx", "gy", None),
            P("gx", "gy", None),
        ),
        out_specs=(P(None, "gx", "gy", None), P(("gx", "gy"), None)),
        check_vma=False,
    )
```

```python
import functools

import jax
import jax.numpy as jnp
from jax import lax
from jax.experimental import pallas as pl
from jax.experimental.pallas import tpu as pltpu
from jax.sharding import PartitionSpec as P

F32 = jnp.float32
BF16 = jnp.bfloat16
LEVELS = 128
OBS_BLK = 128
SOLID = 1e30
LIMIT = 1e29
LANES = 128
SUB = 8

WEIGHT = [
    (8.0 / 27.0, 2.0 / 27.0, 1.0 / 54.0, 1.0 / 216.0)[
        int(i // 9 != 1) + int(i // 3 % 3 != 1) + int(i % 3 != 1)
    ]
    for i in range(27)
]
STEP = [(i // 9 - 1, i // 3 % 3 - 1, i % 3 - 1) for i in range(27)]
VMEM = pl.BlockSpec(memory_space=pltpu.VMEM)
SMEM = pl.BlockSpec(memory_space=pltpu.SMEM)
HBM = pl.BlockSpec(memory_space=pltpu.HBM)


def call(kernel, in_specs, out, scratch=(), aliases=None, cost=0, limit=14 * 1024 * 1024):
    return pl.pallas_call(
        kernel,
        out_shape=[jax.ShapeDtypeStruct(shape, dtype) for _, shape, dtype in out],
        in_specs=in_specs,
        out_specs=[spec for spec, _, _ in out],
        scratch_shapes=list(scratch),
        input_output_aliases=aliases or {},
        compiler_params=pltpu.CompilerParams(vmem_limit_bytes=limit),
        cost_estimate=pl.CostEstimate(flops=cost, bytes_accessed=cost, transcendentals=0),
    )


def raw_moments(f):
    s, d, e = [], [], []
    for k in range(9):
        low, mid, high = f[3 * k : 3 * k + 3]
        ends = high + low
        s.append(ends + mid)
        d.append(high - low)
        e.append(ends)
    s_y, dy, ey, dz, dyz, ez = [], [], [], [], [], []
    for a in range(3):
        ends = s[3 * a + 2] + s[3 * a]
        s_y.append(ends + s[3 * a + 1])
        dy.append(s[3 * a + 2] - s[3 * a])
        ey.append(ends)
        dz.append(d[3 * a] + d[3 * a + 1] + d[3 * a + 2])
        dyz.append(d[3 * a + 2] - d[3 * a])
        ez.append(e[3 * a] + e[3 * a + 1] + e[3 * a + 2])
    m200 = s_y[2] + s_y[0]
    rho = m200 + s_y[1]
    jx = s_y[2] - s_y[0]
    jy = dy[0] + dy[1] + dy[2]
    jz = dz[0] + dz[1] + dz[2]
    m020 = ey[0] + ey[1] + ey[2]
    m002 = ez[0] + ez[1] + ez[2]
    m110 = dy[2] - dy[0]
    m101 = dz[2] - dz[0]
    m011 = dyz[0] + dyz[1] + dyz[2]
    return rho, jx, jy, jz, m200, m020, m002, m110, m101, m011


def unshift(k0, k1, k2, v, v2, vv, vp, vm):
    if k0 is None and k2 is None:
        return vm * k1, -(v2 * k1), vp * k1
    diff = v * k0
    ends = vv * k0
    if k1 is not None:
        diff = diff + k1
        ends = ends + v2 * k1
    if k2 is not None:
        ends = ends + k2
    high = 0.5 * (ends + diff)
    return high - diff, k0 - ends, high


def collide(f, retain):
    rho, jx, jy, jz, m200, m020, m002, m110, m101, m011 = raw_moments(f)
    inv = 1.0 / rho
    ux, uy, uz = jx * inv, jy * inv, jz * inv
    k200, k020, k002 = m200 - jx * ux, m020 - jy * uy, m002 - jz * uz
    third = 1.0 / 3.0
    d1 = retain * (k200 - k020)
    d2 = retain * (k200 - k002)
    xx = (rho + d1 + d2) * third
    yy = xx - d1
    zz = xx - d2
    xy = retain * (m110 - jx * uy)
    xz = retain * (m101 - jx * uz)
    yz = retain * (m011 - jy * uz)
    xy2, xz2, yz2 = 2.0 * xy, 2.0 * xz, 2.0 * yz
    xyi, xzi, yzi = xy2 * inv, xz2 * inv, yz2 * inv
    xxi = xx * inv
    yyi = yy * inv
    q_xy, q_xz, q_yz = xy * xyi, xz * xzi, yz * yzi
    xxyy = xxi * yy + q_xy
    xxzz = xxi * zz + q_xz
    yyzz = yyi * zz + q_yz
    xxyz = xxi * yz + xy * xzi
    xyyz = yyi * xz + xy * yzi
    xyzz = (zz * inv) * xy + xz * yzi
    full = xxi * (yyi * zz + q_yz) + (yyi * q_xz + (zz * inv) * q_xy) + (2.0 * xyi) * (xz * yzi)
    table = {
        (0, 0): (rho, None, xx),
        (1, 0): (None, xy, None),
        (2, 0): (yy, None, xxyy),
        (0, 1): (None, xz, None),
        (1, 1): (yz, None, xxyz),
        (2, 1): (None, xyyz, None),
        (0, 2): (zz, None, xxzz),
        (1, 2): (None, xyzz, None),
        (2, 2): (yyzz, None, full),
    }

    def speeds(v):
        return v, 2.0 * v, v * v, v + 0.5, v - 0.5

    sx, sy, sz = speeds(ux), speeds(uy), speeds(uz)
    after_x = {}
    for (b, c), ks in table.items():
        for a, value in enumerate(unshift(*ks, *sx)):
            after_x[a, b, c] = value
    out = [None] * 27
    for a in range(3):
        after_y = {}
        for c in range(3):
            triple = unshift(*(after_x[a, b, c] for b in range(3)), *sy)
            for b, value in enumerate(triple):
                after_y[b, c] = value
        for b in range(3):
            triple = unshift(*(after_y[b, c] for c in range(3)), *sz)
            for c, value in enumerate(triple):
                out[9 * a + 3 * b + c] = value
    return out, (rho, jx, jy, jz)


def odd_block(axis):
    return lax.rem(lax.axis_index(axis), 2)


def widen(far, near, wide, axis):
    odd = odd_block(axis)
    wide[odd, :, :] = far[...].astype(F32)
    wide[1 - odd, :, :] = near[...].astype(F32)


def merge_named(own, wide, *others):
    named = own
    for more in (wide[0, pl.ds(wide.shape[1] - SUB, SUB), :], wide[1, pl.ds(wide.shape[1] - SUB, SUB), :], *others):
        named = jnp.maximum(named, more)
    return named


def start_all(copies):
    for copy in copies:
        copy.start()
    return copies


def rows_order(side):
    outward = 1 - 2 * side
    both = [i for i in range(27) if STEP[i][1] == outward]
    return both, [i for i in range(27) if STEP[i][1] != outward]


def named_tile(patches, place, nz):
    slots = patches.shape[-1]
    groups = slots // SUB
    ids = jnp.broadcast_to(patches[0, :, :].astype(F32) + 1.0, (SUB, slots))
    row = lax.broadcasted_iota(jnp.int32, (SUB, slots), 0)
    slot = lax.broadcasted_iota(jnp.int32, (SUB, slots), 1)
    lane = lax.broadcasted_iota(jnp.int32, (SUB, nz), 1)
    tile = jnp.zeros((SUB, nz), F32)
    for g in range(groups):
        column = jnp.sum(jnp.where(slot == SUB * g + row, ids, 0.0), axis=1, keepdims=True)
        tile = jnp.where(lane == place * groups + g, column, tile)
    return tile


def rows_kernel(
    size_y, pops_in, omega_in, walls_in, patches_in, far, near, own,
    pops, omega, walls, patches, packed, faces, sems,
):
    planes, ny, nz = omega.shape
    row = lax.broadcasted_iota(jnp.int32, (SUB, nz), 0)
    chunk = 4
    spans = [pl.ds(i, min(chunk, 27 - i)) for i in range(0, 27, chunk)]
    cells = [
        pltpu.make_async_copy(omega_in, omega, sems.at[0, len(spans)]),
        pltpu.make_async_copy(walls_in, walls, sems.at[1, len(spans)]),
        pltpu.make_async_copy(patches_in, patches, sems.at[0, len(spans) + 1]),
    ]
    copies = [
        pltpu.make_async_copy(pops_in.at[span, :, rows, :], pops.at[span, :, rows, :], sems.at[side, k])
        for k, span in enumerate(spans)
        for side, rows in enumerate((pl.ds(0, 2), pl.ds(ny - 2, 2)))
    ]
    start_all(cells + copies)

    def read(group, plane, first):
        part = pl.ds(first, SUB)
        if group < 27:
            return pops[group, plane, part, :]
        if group == 27:
            return 1.0 - omega[plane, part, :]
        return walls[plane, part, :].astype(F32)

    def pack(group):
        for side, first, at in ((0, ny - SUB, SUB - 2), (1, 0, 0)):
            tile = None
            for plane in range(planes):
                turn = (2 * plane - at) % SUB
                piece = read(group, plane, first)
                piece = pltpu.roll(piece, turn, 0) if turn else piece
                tile = piece if tile is None else jnp.where(row // 2 == plane, piece, tile)
            packed[side, group, :, :] = tile

    for copy in cells:
        copy.wait()
    pack(27)
    pack(28)
    named = named_tile(patches, lax.axis_index("gx") * size_y + lax.axis_index("gy"), nz)
    own[...] = jnp.concatenate([named, jnp.zeros((SUB, nz), F32)], axis=0).astype(BF16)
    for i in range(27):
        if i % chunk == 0:
            for copy in copies[i // chunk * 2 : i // chunk * 2 + 2]:
                copy.wait()
        pack(i)
    for side in range(2):
        for part in range(nz // LANES):
            cols = pl.ds(LANES * part, LANES)
            closed = packed[side, 28, :, cols] > 0.5
            f = [packed[side, i, :, cols] * WEIGHT[i] for i in range(27)]
            relaxed, _ = collide(f, packed[side, 27, :, cols])
            for i in range(27):
                packed[side, i, :, cols] = jnp.where(closed, SOLID, relaxed[i]) * (1.0 / WEIGHT[i]) - 1.0
        both, edge = rows_order(side)
        edge = edge + [27, 28]
        tiles = [packed[side, i, :, :] for i in both]
        for k in range(0, len(edge), 2):
            one, two = (packed[side, i, :, :] for i in edge[k : k + 2])
            at_edge = row % 2 == 1 - side
            tiles.append(jnp.where(at_edge, one, pltpu.roll(two, SUB - 1 if side == 0 else 1, 0)))
        tiles.append(named)
        for k, tile in enumerate(tiles):
            faces[side, pl.ds(SUB * k, SUB), :] = tile
    odd = odd_block("gy")
    far[...] = faces[1 - odd, :, :].astype(BF16)
    near[...] = faces[odd, :, :].astype(BF16)


def first_main_kernel(pops, omega, walls, post):
    planes, ny, nz = omega.shape

    def body(plane, carry):
        for t in range(ny // SUB):
            for part in range(nz // LANES):
                at = (plane, pl.ds(SUB * t, SUB), pl.ds(LANES * part, LANES))
                f = [pops[(i, *at)] * WEIGHT[i] for i in range(27)]
                closed = walls[at] == 1
                out, _ = collide(f, 1.0 - omega[at])
                for i in range(27):
                    post[(i, *at)] = jnp.where(closed, SOLID, out[i])
        return carry

    lax.fori_loop(0, planes, body, 0)


def corner_rows(reach):
    places = {}
    for k in range(9):
        sy, j = STEP[k][1], k % 3
        if reach == 2:
            rows = {1: ((6, 6), (7, 7)), 0: ((7, 3), (0, 4)), -1: ((0, 0), (1, 1))}[sy]
            places[k] = [(ring, j, at) for ring, at in rows]
        else:
            places[k] = {1: [(7, 0, j)], 0: [], -1: [(0, 0, 3 + j)]}[sy]
    return places


def face_rows(ny, reach):
    return 9 * ny + (4 if reach == 2 else 2) * SUB


def pack_x(main, halo, plane, first, reach, named, out):
    ny, nz = main.shape[2:]
    row = lax.broadcasted_iota(jnp.int32, (SUB, nz), 0)
    scaled = lambda ref, k: ref[first + k, plane, :, :] * (1.0 / WEIGHT[k]) - 1.0
    for k in range(9):
        out[pl.ds(ny * k, ny), :] = scaled(main, k).astype(BF16)
    tiles = [jnp.zeros((SUB, nz), F32) for _ in range((out.shape[0] - 9 * ny) // SUB)]
    for k, places in corner_rows(reach).items():
        for ring, tile, at in places:
            turn = (at - ring) % SUB
            value = scaled(halo, k)
            value = pltpu.roll(value, turn, 0) if turn else value
            tiles[tile] = jnp.where(row == at, value, tiles[tile])
    tiles[-1] = named
    out[pl.ds(9 * ny, SUB * len(tiles)), :] = jnp.concatenate(tiles, axis=0).astype(BF16)


def pack_faces(main, halo, last, reach, named, far, near):
    odd = odd_block("gx")
    pack_x(main, halo, odd * last, odd * 18, reach, named, far)
    pack_x(main, halo, (1 - odd) * last, (1 - odd) * 18, reach, named, near)


def first_halo_kernel(near, far, main, own, across, halo, retain, solid, named, send_far, send_near, wide):
    _, planes, _, nz = halo.shape
    row = lax.broadcasted_iota(jnp.int32, (SUB, nz), 0)
    widen(far, near, wide, "gy")

    def received(side, group, plane):
        both, edge = rows_order(side)
        edge = edge + [27, 28]
        turn = (SUB - 2, 0)[side] - 2 * plane
        if group in both:
            tile = both.index(group)
        else:
            k = edge.index(group)
            tile = len(both) + k // 2
            turn += (k % 2) * (1 - 2 * side)
        value = wide[side, pl.ds(SUB * tile, SUB), :]
        return pltpu.roll(value, turn % SUB, 0) if turn % SUB else value

    def beside(group, plane):
        return jnp.where(row < 4, received(1, group, plane), received(0, group, plane))

    for plane in range(planes):
        retain[plane, :, :] = beside(27, plane)
        solid[plane, :, :] = beside(28, plane)
        for i in range(27):
            halo[i, plane, :, :] = (beside(i, plane) + 1.0) * WEIGHT[i]
    named[...] = merge_named(own[...].astype(F32)[:SUB], wide, across[...].astype(F32)[:SUB])
    pack_faces(main, halo, planes - 1, 2, named[...], send_far, send_near)


def turned(value, i):
    _, sy, sz = STEP[i]
    if sy:
        value = pltpu.roll(value, sy % value.shape[0], 0)
    if sz:
        value = pltpu.roll(value, sz % value.shape[1], 1)
    return value


def pull(load, i, plane):
    value = turned(load(i, plane - STEP[i][0]), i)
    return jnp.where(value > LIMIT, load(26 - i, plane), value)


def loader(planes, ny, places, wide=None):
    def load(i, plane):
        if 0 <= plane < planes:
            main, halo, at = places[plane]
            return jnp.concatenate([main[i, at, :, :], halo[i, at, :, :]], axis=0)
        side, k = (0, i - 18) if plane < 0 else (1, i)
        reach = 2 if wide.shape[1] == face_rows(ny, 2) else 1
        used = corner_rows(reach)[k]
        if used:
            ring, tile, at = used[0]
            halo = wide[side, pl.ds(9 * ny + SUB * tile, SUB), :]
            halo = pltpu.roll(halo, (ring - at) % SUB, 0) if ring != at else halo
        else:
            halo = jnp.zeros((SUB, wide.shape[2]), F32)
        both = jnp.concatenate([wide[side, pl.ds(ny * k, ny), :], halo], axis=0)
        return (both + 1.0) * WEIGHT[i]

    return load


def collide_rows(at, t, f, closed, keep, main2, macro):
    rows, cols = t
    out, sums = collide(f, keep)
    for i in range(27):
        main2[i, at, rows, cols] = jnp.where(closed, SOLID, out[i])
    macro[0, at, rows, cols] = sums[0] - 1.0
    for m in range(1, 4):
        macro[m, at, rows, cols] = sums[m]


def middle_inner_kernel(main, halo, pops, omega, walls, retain, solid, main2, halo2, macro, ready, read):
    planes, ny, nz = omega.shape
    last = planes - 1
    load = loader(planes, ny, [(main, halo, p) for p in range(planes)])
    for plane in (*range(1, last), 0, last):
        inside = 0 < plane < last
        own = walls[plane, :, :] == 1
        for i in range(27):
            value = pull(load, i, plane) if 0 <= plane - STEP[i][0] <= last else load(26 - i, plane)
            value = [jnp.where(own, pops[i, plane, :, :] * WEIGHT[i], value[:ny]), value[ny:]]
            for rows, part in zip((pl.ds(0, ny), pl.ds(ny, SUB)), value):
                if inside:
                    read[i, rows, :] = part
                else:
                    ready[i, int(plane > 0), rows, :] = part
        if not inside:
            continue
        at = plane - 1
        for part in range(nz // LANES):
            cols = pl.ds(LANES * part, LANES)
            for t in range(ny // SUB):
                rows = pl.ds(SUB * t, SUB)
                f = [read[i, rows, cols] for i in range(27)]
                closed = walls[plane, rows, cols] == 1
                collide_rows(at, (rows, cols), f, closed, 1.0 - omega[plane, rows, cols], main2, macro)
            out, _ = collide([read[i, pl.ds(ny, SUB), cols] for i in range(27)], retain[plane, :, cols])
            closed = solid[plane, :, cols] > 0.5
            for i in range(27):
                halo2[i, at, :, cols] = jnp.where(closed, SOLID, out[i])


def middle_outer_kernel(
    ready, omega, walls, retain, solid, near, far, own, _,
    main2, halo2, macro, named, send_far, send_near, read, wide,
):
    planes, ny, nz = omega.shape
    last = planes - 1
    widen(far, near, wide, "gx")
    load = loader(planes, ny, None, wide)
    sides = ((0, 18), (last, 0))
    for at, (plane, first) in enumerate(sides):
        solid_cell = walls[plane, :, :] == 1
        for k in range(9):
            value = turned(load(first + k, plane - STEP[first + k][0]), first + k)
            spare = ready[first + k, at, :, :]
            shut = value > LIMIT
            read[k, at, pl.ds(0, ny), :] = jnp.where(solid_cell | shut[:ny], spare[:ny], value[:ny])
            read[k, at, pl.ds(ny, SUB), :] = jnp.where(shut[ny:], spare[ny:], value[ny:])

    def streamed(at, rows, cols):
        first = sides[at][1]
        return [
            read[i - first, at, rows, cols] if 0 <= i - first < 9 else ready[i, at, rows, cols] for i in range(27)
        ]

    row = lax.broadcasted_iota(jnp.int32, (SUB, LANES), 0)
    edge = (row == 0) | (row == SUB - 1)
    merge = lambda pair: jnp.where(edge, pair[0], pltpu.roll(pair[1], SUB // 2, 0))
    for part in range(nz // LANES):
        cols = pl.ds(LANES * part, LANES)
        for at, (plane, _) in enumerate(sides):
            for t in range(ny // SUB):
                rows = pl.ds(SUB * t, SUB)
                closed = walls[plane, rows, cols] == 1
                keep = 1.0 - omega[plane, rows, cols]
                collide_rows(at, (rows, cols), streamed(at, rows, cols), closed, keep, main2, macro)
        both = [streamed(at, pl.ds(ny, SUB), cols) for at in range(2)]
        keep = merge([retain[plane, :, cols] for plane, _ in sides])
        closed = merge([solid[plane, :, cols] for plane, _ in sides]) > 0.5
        out, _ = collide([merge(pair) for pair in zip(*both)], keep)
        for i in range(27):
            value = jnp.where(closed, SOLID, out[i])
            halo2[i, 0, :, cols] = value
            halo2[i, 1, :, cols] = pltpu.roll(value, SUB // 2, 0)
    more = merge_named(own[...], wide)
    named[...] = jnp.concatenate([more, jnp.zeros(more.shape, F32)], axis=0).astype(BF16)
    pack_faces(main2, halo2, 1, 1, more, send_far, send_near)


def add_moments(sums, i, f):
    for m, sign in enumerate((1,) + STEP[i]):
        if sign:
            term = f if sign > 0 else -f
            sums[m] = term if sums[m] is None else sums[m] + term


def respond(planes, radiation, pick, fields):
    for p, rows in enumerate(planes):
        ny = rows[0].shape[0]
        for m in range(4):
            fields[m, pl.ds(p * ny, ny), :] = rows[m].astype(BF16)
    parts = []
    for m in range(4):
        total = None
        for h in range(pick.shape[0]):
            term = jnp.dot(pick[h, :, :], fields[m, :, pl.ds(LANES * h, LANES)], preferred_element_type=F32)
            total = term if total is None else total + term
        parts.append(total)
    surface = jnp.concatenate(parts, axis=1).astype(BF16)
    response = jnp.dot(surface, radiation[...], preferred_element_type=F32)
    return response.astype(BF16)


def fill_levels(per_block, level):
    devices, _, width = level.shape
    slots = per_block.shape[0]
    groups = slots // SUB
    group = lax.broadcasted_iota(jnp.int32, (SUB, width), 1) // (width // groups)
    tiles = {}
    for d in range(devices):
        blk = d * width // OBS_BLK
        if blk not in tiles:
            tile = None
            for g in range(groups):
                column = per_block[SUB * g : SUB * (g + 1), blk : blk + 1]
                column = jnp.broadcast_to(column, (SUB, width))
                tile = column if tile is None else jnp.where(group == g, column, tile)
            tiles[blk] = tile.astype(BF16)
        level[d, :, :] = tiles[blk]


def slots_kernel(size_y, ride, bins, radiation, counts, sites, patches, pick, level, own_bins, turned_radiation):
    halves, slots, lines = pick.shape
    slot = lax.broadcasted_iota(jnp.int32, (slots, lines), 0)
    line = lax.broadcasted_iota(jnp.int32, (slots, lines), 1)
    wanted = jnp.full((slots, lines), -1, jnp.int32)
    for k in range(slots):
        wanted = jnp.where(slot == k, sites[0, 0, k], wanted)
    wanted = jnp.where(slot < jnp.broadcast_to(counts[...], slot.shape), wanted, -halves)
    for h in range(halves):
        pick[h, :, :] = (wanted == line * halves + h).astype(BF16)

    n_patch = bins.shape[1]
    slot = lax.broadcasted_iota(jnp.int32, (slots, n_patch), 0)
    named = lax.broadcasted_iota(jnp.int32, (slots, n_patch), 1)
    wanted = jnp.full((slots, n_patch), -1, jnp.int32)
    for k in range(slots):
        wanted = jnp.where(slot == k, patches[0, 0, k], wanted)
    chosen = (wanted == named).astype(BF16)
    per_block = lax.dot_general(
        chosen, bins[...].astype(F32).astype(BF16), (((1,), (1,)), ((), ())), preferred_element_type=F32
    )
    devices, _, width = level.shape
    if not ride:
        fill_levels(per_block, level)
    place = lax.axis_index("gx") * size_y + lax.axis_index("gy")
    mine = bins[pl.ds(lax.div(place * width, OBS_BLK), 1), :].astype(F32)
    own_bins[...] = jnp.broadcast_to(mine, own_bins.shape).astype(BF16)

    observers, terms = radiation.shape

    def body(k, carry):
        rows = pl.ds(pl.multiple_of(k * terms, terms), terms)
        turned_radiation[:, rows] = radiation[rows, :].T
        return carry

    lax.fori_loop(0, observers // terms, body, 0)


def last_early_kernel(
    main_in, halo_in, main_out, halo_out, pops, walls, macro_in, macro_out, radiation, pick,
    out, spare, part, inner, send, g_out, fields, sems,
):
    planes, ny, _ = walls.shape
    last = planes - 1
    places = [(main_out, halo_out, 0)]
    places += [(main_in, halo_in, p) for p in range(planes - 2)]
    places += [(main_out, halo_out, 1)]
    load = loader(planes, ny, places)
    copies = []
    for plane in (0, last, *range(1, last)):
        own = walls[plane, :, :] == 1
        edge = {0: 0, last: 1}.get(plane)
        sums = [None] * 4
        for i in range(27):
            if 0 <= plane - STEP[i][0] <= last:
                value = pull(load, i, plane)[:ny]
                g = jnp.where(own, pops[i, plane, :, :], value * (1.0 / WEIGHT[i]))
                g_out[i, plane, :, :] = g
                add_moments(sums, i, g * WEIGHT[i])
            else:
                bounced = load(26 - i, plane)[:ny]
                spare[edge, i % 9, :, :] = jnp.where(own, pops[i, plane, :, :] * WEIGHT[i], bounced)
        for m in range(4):
            if edge is None:
                inner[m, plane - 1, :, :] = sums[m] - 1.0 if m == 0 else sums[m]
            else:
                part[m, edge, :, :] = sums[m]
        span = pl.ds((0, 9)[edge], 18) if edge is not None else pl.ds(0, 27)
        copies += start_all(
            [pltpu.make_async_copy(g_out.at[span, plane], out.at[span, plane], sems.at[len(copies)])]
        )
    rows = [[macro_out[m, 0, :, :] for m in range(4)]]
    rows += [[macro_in[m, p, :, :] for m in range(4)] for p in range(planes - 2)]
    rows += [[macro_out[m, 1, :, :] for m in range(4)]]
    response = respond(rows, radiation, pick, fields)
    devices, _, width = send.shape
    for d in range(devices):
        send[d, :, :] = response[:, d * width : (d + 1) * width]
    for copy in copies:
        copy.wait()


def last_kernel(
    far, near, walls, spare, part, inner, radiation, pick, early, level, own, across, started,
    out, send, named, g_out, fields, wide, sems,
):
    planes, ny, _ = walls.shape
    last = planes - 1
    widen(far, near, wide, "gx")
    load = loader(planes, ny, None, wide)
    rows, copies = {}, []
    for edge, (plane, first) in enumerate(((0, 18), (last, 0))):
        own = walls[plane, :, :] == 1
        sums = [part[m, edge, :, :] for m in range(4)]
        for k in range(9):
            i = first + k
            value = turned(load(i, plane - STEP[i][0]), i)[:ny]
            f = jnp.where(own | (value > LIMIT), spare[edge, k, :, :], value)
            g_out[k, edge, :, :] = f * (1.0 / WEIGHT[i])
            add_moments(sums, i, f)
        rows[plane] = [sums[0] - 1.0, *sums[1:]]
        copies += start_all(
            [pltpu.make_async_copy(g_out.at[:, edge], out.at[pl.ds(first, 9), plane], sems.at[edge])]
        )
    for p in range(planes - 2):
        rows[p + 1] = [inner[m, p, :, :] for m in range(4)]
    response = respond([rows[p] for p in range(planes)], radiation, pick, fields)
    devices, _, width = send.shape
    slots = early.shape[1]
    for d in range(devices):
        send[d, pl.ds(0, slots), :] = early[d, :, :]
        send[d, pl.ds(slots, slots), :] = response[:, d * width : (d + 1) * width]
        if send.shape[1] > 2 * slots:
            send[d, pl.ds(2 * slots, SUB), :] = level[d, :, :]
    named[...] = merge_named(own[...].astype(F32)[:SUB], wide, across[...].astype(F32)[:SUB])
    for copy in copies:
        copy.wait()


def bin_named_kernel(received, named, own_bins, signal, hits, known):
    devices, rows, width = received.shape
    slots = rows // 2
    groups = slots // SUB
    patch = lax.broadcasted_iota(jnp.int32, (slots, known.shape[-1]), 1).astype(F32) + 1.0
    for d in range(devices):
        columns = [named[:, groups * d + g : groups * d + g + 1] for g in range(groups)]
        ids = jnp.concatenate([jnp.broadcast_to(c, (SUB, patch.shape[1])) for c in columns], axis=0)
        known[d, :, :] = (ids == patch).astype(F32).astype(BF16)
    flat = known[...].reshape(devices * slots, patch.shape[1])
    level = lax.dot_general(flat, own_bins[...], (((1,), (1,)), ((), ())), preferred_element_type=F32)
    lane = lax.broadcasted_iota(jnp.int32, level.shape, 1).astype(F32)
    for step in range(2):
        hit = (level == lane - float(step)).astype(F32).astype(BF16)
        hits[:, pl.ds(step * slots, slots), :] = hit.reshape(devices, slots, LEVELS)
    left = received[...].reshape(devices * rows, width)
    right = hits[...].reshape(devices * rows, LEVELS)
    signal[...] = lax.dot_general(left, right, (((0,), (0,)), ((), ())), preferred_element_type=F32)


def bin_kernel(received, signal, hits):
    devices, rows, width = received.shape
    slots = (rows - SUB) // 2
    groups = slots // SUB
    lane = lax.broadcasted_iota(jnp.int32, (slots, LEVELS), 1).astype(F32)
    for d in range(devices):
        tile = received[d, pl.ds(2 * slots, SUB), :].astype(F32)
        starts = [g * (width // groups) for g in range(groups)]
        level = jnp.concatenate([jnp.broadcast_to(tile[:, k : k + 1], (SUB, LEVELS)) for k in starts], axis=0)
        for step in range(2):
            hit = (level == lane - float(step)).astype(F32).astype(BF16)
            hits[d, pl.ds(step * slots, slots), :] = hit
    left = received[:, pl.ds(0, 2 * slots), :].reshape(devices * 2 * slots, width)
    right = hits[...].reshape(devices * 2 * slots, LEVELS)
    signal[...] = lax.dot_general(left, right, (((0,), (0,)), ((), ())), preferred_element_type=F32)


def per_device(populations, omega, walls, radiation, bins, counts, sample_site, sample_patch):
    _, planes, ny, nz = populations.shape
    slots = sample_site.shape[-1]
    size_x, size_y = lax.axis_size("gx"), lax.axis_size("gy")
    devices = size_x * size_y
    width = radiation.shape[0] // devices
    ride = (size_x, size_y) == (8, 4)

    def swap(far, near, axis, size):
        far_pairs = [(i, (i - 1 + 2 * (i % 2)) % size) for i in range(size)]
        near_pairs = [(i, i + 1 - 2 * (i % 2)) for i in range(size)]
        return lax.ppermute(far, axis, far_pairs), lax.ppermute(near, axis, near_pairs)

    dma = pltpu.SemaphoreType.DMA
    block, cells = populations.shape, (planes, ny, nz)
    beside = (20 * SUB, nz)
    far, near, own = call(
        functools.partial(rows_kernel, size_y),
        [HBM] * 4,
        [(VMEM, beside, BF16)] * 2 + [(VMEM, (2 * SUB, nz), BF16)],
        [
            pltpu.VMEM(block, F32), pltpu.VMEM(cells, F32), pltpu.VMEM(cells, walls.dtype),
            pltpu.VMEM(sample_patch.shape, sample_patch.dtype),
            pltpu.VMEM((2, 29, SUB, nz), F32), pltpu.VMEM((2, *beside), F32), dma((2, 9)),
        ],
        cost=1 << 20,
        limit=64800000,
    )(populations, omega, walls, sample_patch)
    far, near = swap(far, near, "gy", size_y)
    across = lax.ppermute(own, "gy", [(i, (i + size_y // 2) % size_y) for i in range(size_y)])
    pick, level, own_bins, radiation = call(
        functools.partial(slots_kernel, size_y, ride),
        [VMEM] * 3 + [SMEM] * 2,
        [
            (VMEM, (nz // LANES, slots, planes * ny), BF16),
            (VMEM, (devices, SUB, width), BF16),
            (VMEM, (LEVELS, bins.shape[0]), BF16),
            (VMEM, radiation.shape[::-1], BF16),
        ],
        cost=1 << 22,
    )(bins.T, radiation, counts, sample_site, sample_patch)
    (main,) = call(first_main_kernel, [VMEM] * 3, [(VMEM, block, F32)], cost=1 << 22)(populations, omega, walls)

    edge = (planes, SUB, nz)
    face, last_face = ((face_rows(ny, reach), nz) for reach in (2, 1))
    faces, last_faces = ([(VMEM, shape, BF16)] * 2 for shape in (face, last_face))
    halo, retain, solid, named, far, near = call(
        first_halo_kernel,
        [VMEM] * 5,
        [(VMEM, (27, *edge), F32), (VMEM, edge, F32), (VMEM, edge, F32), (VMEM, (SUB, nz), F32), *faces],
        [pltpu.VMEM((2, *beside), F32)],
        cost=1 << 20,
    )(near, far, main, own, across)
    far, near = swap(far, near, "gx", size_x)

    def relaxed(n):
        return [(VMEM, (27, n, ny, nz), F32), (VMEM, (27, n, SUB, nz), F32), (VMEM, (4, n, ny, nz), F32)]

    read = pltpu.VMEM((27, ny + SUB, nz), F32)
    wide, last_wide = (pltpu.VMEM((2, *shape), F32) for shape in (face, last_face))
    main_in, halo_in, macro_in, ready = call(
        middle_inner_kernel,
        [VMEM] * 7,
        relaxed(planes - 2) + [(VMEM, (27, 2, ny + SUB, nz), F32)],
        [read],
        cost=1 << 22,
    )(main, halo, populations, omega, walls, retain, solid)
    main_out, halo_out, macro_out, named, far, near = call(
        middle_outer_kernel,
        [VMEM] * 9,
        relaxed(2) + [(VMEM, (2 * SUB, nz), BF16), *last_faces],
        [pltpu.VMEM((9, 2, ny + SUB, nz), F32), wide],
        cost=1 << 22,
    )(ready, omega, walls, retain, solid, near, far, named, pick)
    far, near = swap(far, near, "gx", size_x)
    across = lax.ppermute(named, "gx", [(i, (i + size_x // 2) % size_x) for i in range(size_x)])

    fields = pltpu.VMEM((4, planes * ny, nz), BF16)
    inner = (4, planes - 2, ny, nz)
    started, spare, part, inner, early = call(
        last_early_kernel,
        [VMEM] * 10,
        [
            (HBM, block, F32),
            (VMEM, (2, 9, ny, nz), F32),
            (VMEM, (4, 2, ny, nz), F32),
            (VMEM, inner, F32),
            (VMEM, (devices, slots, width), BF16),
        ],
        [pltpu.VMEM(block, F32), fields, dma((planes,))],
        cost=1 << 22,
    )(main_in, halo_in, main_out, halo_out, populations, walls, macro_in, macro_out, radiation, pick)
    sent = 2 * slots if ride else 2 * slots + SUB
    advanced, send, named = call(
        last_kernel,
        [VMEM] * 12 + [HBM],
        [(HBM, block, F32), (VMEM, (devices, sent, width), BF16), (VMEM, (SUB, nz), F32)],
        [pltpu.VMEM((9, 2, ny, nz), F32), fields, last_wide, dma((2,))],
        aliases={12: 0},
        cost=1 << 22,
    )(far, near, walls, spare, part, inner, radiation, pick, early, level, named, across, started)
    received = lax.all_to_all(send, ("gx", "gy"), 0, 0, tiled=True)
    hits = pltpu.VMEM((devices, 2 * slots, LEVELS), BF16)
    result = [(VMEM, (width, LEVELS), F32)]
    if ride:
        known = pltpu.VMEM((devices, slots, bins.shape[0]), BF16)
        (signal,) = call(bin_named_kernel, [VMEM] * 3, result, [hits, known], cost=1 << 20)(received, named, own_bins)
    else:
        (signal,) = call(bin_kernel, [VMEM], result, [hits], cost=1 << 20)(received)
    return advanced, signal


def solution(mesh):
    return jax.shard_map(
        per_device,
        mesh=mesh,
        in_specs=(
            P(None, "gx", "gy", None),
            P("gx", "gy", None),
            P("gx", "gy", None),
            P(),
            P(),
            P("gx", "gy"),
            P("gx", "gy", None),
            P("gx", "gy", None),
        ),
        out_specs=(P(None, "gx", "gy", None), P(("gx", "gy"), None)),
        check_vma=False,
    )
```
